32 devices in a mesh: fsdp: 16 (over z, x, core), rep: 2 (over y).
Axes of the slice: x: 2, y: 2, z: 4, core: 2. Of those that a mesh axis runs over, the one named last changes fastest.
Arguments:
- tokens: bfloat16 [14336, 1152], P(('fsdp', 'rep')), may hold values from -6 to 6
- condition: bfloat16 [32, 1152], P(('fsdp', 'rep')), may hold values from -6 to 6
- lengths: int32 [32], P(('fsdp', 'rep')), may hold values from 336 to 448, as said below
- targets: bfloat16 [14336, 768], P(('fsdp', 'rep')), may hold values from -6 to 6
- cotangent: bfloat16 [14336, 1152], P(('fsdp', 'rep')), may hold values from -6 to 6
- wide_weight: float32 [2, 1152, 16128], P(None, 'fsdp'), may hold values from -0.5 to 0.5
- deep_weight: float32 [2, 4608, 1152], P(None, 'fsdp'), may hold values from -0.09375 to 0.09375
- head_first: float32 [1152, 2048], P('fsdp'), may hold values from -0.1875 to 0.1875
- head_second: float32 [2048, 2816], P('fsdp'), may hold values from -0.125 to 0.125
- block_bias: float32 [2, 16128], replicated, may hold values from -4 to 4
- head_bias: float32 [4864], replicated, may hold values from -4 to 4
- wide_mean: float32 [2, 1152, 16128], P(None, 'fsdp'), may hold values from -64 to 64
- deep_mean: float32 [2, 4608, 1152], P(None, 'fsdp'), may hold values from -64 to 64
- head_first_mean: float32 [1152, 2048], P('fsdp'), may hold values from -0.078125 to 0.078125
- head_second_mean: float32 [2048, 2816], P('fsdp'), may hold values from -0.078125 to 0.078125
- block_bias_mean: float32 [2, 16128], replicated, may hold values from -64 to 64
- head_bias_mean: float32 [4864], replicated, may hold values from -0.15625 to 0.15625
- wide_square: float32 [2, 1152, 16128], P(None, 'fsdp'), may hold values from 9.17504 to 36.70016
- deep_square: float32 [2, 4608, 1152], P(None, 'fsdp'), may hold values from 9.17504 to 36.70016
- head_first_square: float32 [1152, 2048], P('fsdp'), may hold values from 2.1875e-06 to 8.75e-06
- head_second_square: float32 [2048, 2816], P('fsdp'), may hold values from 2.1875e-06 to 8.75e-06
- block_bias_square: float32 [2, 16128], replicated, may hold values from 9.17504 to 36.70016
- head_bias_square: float32 [4864], replicated, may hold values from 8.75e-06 to 3.5e-05
Outputs:
- output: bfloat16 [14336, 1152], P(('fsdp', 'rep'))
- input_grad: float32 [14336, 1152], P(('fsdp', 'rep'))
- wide_grad: float32 [2, 1152, 16128], P(None, 'fsdp')
- deep_grad: float32 [2, 4608, 1152], P(None, 'fsdp')
- head_first_grad: float32 [1152, 2048], P('fsdp')
- head_second_grad: float32 [2048, 2816], P('fsdp')
- block_bias_grad: float32 [2, 16128], replicated
- head_bias_grad: float32 [4864], replicated
- wide_mean_new: float32 [2, 1152, 16128], P(None, 'fsdp')
- deep_mean_new: float32 [2, 4608, 1152], P(None, 'fsdp')
- head_first_mean_new: float32 [1152, 2048], P('fsdp')
- head_second_mean_new: float32 [2048, 2816], P('fsdp')
- block_bias_mean_new: float32 [2, 16128], replicated
- head_bias_mean_new: float32 [4864], replicated
- wide_square_new: float32 [2, 1152, 16128], P(None, 'fsdp')
- deep_square_new: float32 [2, 4608, 1152], P(None, 'fsdp')
- head_first_square_new: float32 [1152, 2048], P('fsdp')
- head_second_square_new: float32 [2048, 2816], P('fsdp')
- block_bias_square_new: float32 [2, 16128], replicated
- head_bias_square_new: float32 [4864], replicated
- wide_weight_new: float32 [2, 1152, 16128], P(None, 'fsdp')
- deep_weight_new: float32 [2, 4608, 1152], P(None, 'fsdp')
- head_first_new: float32 [1152, 2048], P('fsdp')
- head_second_new: float32 [2048, 2816], P('fsdp')
- block_bias_new: float32 [2, 16128], replicated
- head_bias_new: float32 [4864], replicated
The draws below stay inside these ranges and needn't reach their ends.
Inputs may be any that keep to these rules, and one draw needn't show every extreme that they name: `lengths`: each sequence's valid tokens; some sequence is full in every draw.
All inputs are finite; a program needn't handle non-finite values.
Results may differ from the reference program's by a relative error of at most 0.024.
The reference program's roundings to bfloat16 on the way count: a program that leaves them out, or rounds other values in their place, can miss the bound.
Values may be sent and summed in bfloat16 or wider, within the bound.
A program may use at most 640 MiB of HBM per device.

```python
import math
from functools import partial
import jax
import jax.numpy as jnp
from jax import lax

MODEL_WIDTH = 1152
HEADS = 16
HEAD_DIM = 72
FF = 4608
PH = 2048
PZ = 768
SEQ_LEN = 448
STEP = 10
BATCH = 32
TOKENS = 14336
WIDE = 16128
NHB = 4864


def draw_wide_weight(key, part):
    key = jax.random.fold_in(key, 11)
    base = jax.random.truncated_normal(key, -6.0, 6.0, (2, MODEL_WIDTH, 10 * MODEL_WIDTH + FF), jnp.float32)
    column = jnp.arange(10 * MODEL_WIDTH + FF)
    factor = jnp.where((column >= 9 * MODEL_WIDTH) & (column < 10 * MODEL_WIDTH), (8.0 / MODEL_WIDTH) ** 0.5, MODEL_WIDTH ** (-0.5))
    return base * factor


def draw_lengths(key, part):
    key = jax.random.fold_in(key, 23)
    first_key, second_key = jax.random.split(key)
    least = SEQ_LEN - SEQ_LEN // 4
    values = jax.random.randint(first_key, (BATCH,), least, SEQ_LEN + 1, jnp.int32)
    place = jax.random.randint(second_key, (), 0, BATCH, jnp.int32)
    return values.at[place].set(SEQ_LEN)


def steps_of(stream_key, dims, cuts, smallest, high):
    level, own = 1.0, jax.random.fold_in(stream_key, 6)
    for axis_at, parts in cuts:
        steps = jnp.exp(jax.random.uniform(jax.random.fold_in(own, axis_at), (parts,), jnp.float32, smallest / len(cuts), high / len(cuts)))
        level = level * jnp.repeat(steps, dims[axis_at] // parts).reshape([-1 if axis == axis_at else 1 for axis in range(len(dims))])
    return level


def normal_values(own_key, shape, scale, most, cuts=(), held_as=jnp.bfloat16):
    values = scale * jax.random.normal(own_key, shape, jnp.float32)
    if cuts:
        values = values * steps_of(own_key, shape, cuts, -0.22, 0.18)
    return jnp.clip(values, -most, most).astype(held_as)


def setup_inputs(seed: int = 0) -> dict:
    keys = jax.random.split(jax.random.key(seed), 24)
    return {
        "tokens": normal_values(keys[0], (TOKENS, MODEL_WIDTH), 1.0, 6.0, ((0, 32),)),
        "condition": normal_values(keys[1], (BATCH, MODEL_WIDTH), 1.0, 6.0, ((0, 32),)),
        "lengths": draw_lengths(jax.random.fold_in(keys[23], 71), 0),
        "targets": normal_values(keys[3], (TOKENS, PZ), 1.0, 6.0, ((0, 32),)),
        "cotangent": normal_values(keys[4], (TOKENS, MODEL_WIDTH), 1.0, 6.0, ((0, 32),)),
        "wide_weight": draw_wide_weight(jax.random.fold_in(keys[23], 71), 0),
        "deep_weight": normal_values(keys[6], (2, FF, MODEL_WIDTH), FF ** -0.5, 0.09375, ((1, 16),), jnp.float32),
        "head_first": normal_values(keys[7], (MODEL_WIDTH, PH), MODEL_WIDTH ** -0.5, 0.1875, ((0, 16),), jnp.float32),
        "head_second": normal_values(keys[8], (PH, PH + PZ), PH ** -0.5, 0.125, ((0, 16),), jnp.float32),
        "block_bias": normal_values(keys[9], (2, WIDE), 0.3, 4.0, (), jnp.float32),
        "head_bias": normal_values(keys[10], (NHB,), 0.3, 4.0, (), jnp.float32),
        "wide_mean": normal_values(keys[11], (2, MODEL_WIDTH, WIDE), (0.111 * 0.8 * TOKENS ** 0.5), 64.0, ((1, 16),), jnp.float32),
        "deep_mean": normal_values(keys[12], (2, FF, MODEL_WIDTH), (0.111 * 0.8 * TOKENS ** 0.5), 64.0, ((1, 16),), jnp.float32),
        "head_first_mean": normal_values(keys[13], (MODEL_WIDTH, PH), (0.111 * 0.3 * TOKENS ** 0.5 / PZ), 0.078125, ((0, 16),), jnp.float32),
        "head_second_mean": normal_values(keys[14], (PH, PH + PZ), (0.111 * 0.3 * TOKENS ** 0.5 / PZ), 0.078125, ((0, 16),), jnp.float32),
        "block_bias_mean": normal_values(keys[15], (2, WIDE), (0.111 * 0.8 * TOKENS ** 0.5), 64.0, (), jnp.float32),
        "head_bias_mean": normal_values(keys[16], (NHB,), (0.111 * 0.6 * TOKENS ** 0.5 / PZ), 0.15625, (), jnp.float32),
        "wide_square": jnp.clip(jnp.exp(math.log(36.70016) - 1.3862944 * jax.random.uniform(keys[17], (2, MODEL_WIDTH, WIDE), jnp.float32) ** steps_of(keys[17], (2, MODEL_WIDTH, WIDE), ((1, 16),), -0.2, 0.2)), 9.17504, 36.70016),
        "deep_square": jnp.clip(jnp.exp(math.log(36.70016) - 1.3862944 * jax.random.uniform(keys[18], (2, FF, MODEL_WIDTH), jnp.float32) ** steps_of(keys[18], (2, FF, MODEL_WIDTH), ((1, 16),), -0.2, 0.2)), 9.17504, 36.70016),
        "head_first_square": jnp.clip(jnp.exp(math.log(8.750000233703759e-06) - 1.3862944 * jax.random.uniform(keys[19], (MODEL_WIDTH, PH), jnp.float32) ** steps_of(keys[19], (MODEL_WIDTH, PH), ((0, 16),), -0.2, 0.2)), 2.1875000584259396e-06, 8.750000233703759e-06),
        "head_second_square": jnp.clip(jnp.exp(math.log(8.750000233703759e-06) - 1.3862944 * jax.random.uniform(keys[20], (PH, PH + PZ), jnp.float32) ** steps_of(keys[20], (PH, PH + PZ), ((0, 16),), -0.2, 0.2)), 2.1875000584259396e-06, 8.750000233703759e-06),
        "block_bias_square": jnp.clip(jnp.exp(jax.random.uniform(keys[21], (2, WIDE), jnp.float32, math.log(9.17504), math.log(36.70016))), 9.17504, 36.70016),
        "head_bias_square": jnp.clip(jnp.exp(jax.random.uniform(keys[22], (NHB,), jnp.float32, math.log(8.750000233703759e-06), math.log(3.5000000934815034e-05))), 8.750000233703759e-06, 3.5000000934815034e-05),
    }


@jax.custom_vjp
def low(v):
    return lax.optimization_barrier(v.astype(jnp.bfloat16)).astype(jnp.float32)

@jax.custom_vjp
def low_back(v):
    return v

def low_keep(v):
    return (low(v), None)

def low_pass(kept, grad):
    return (grad,)

def back_keep(v):
    return (v, None)

def back_low(kept, grad):
    return (low(grad),)
low.defvjp(low_keep, low_pass)
low_back.defvjp(back_keep, back_low)
norm_epsilon = 1e-06
adam_epsilon = 1e-08
masked_score = -1e+30
repa_weight = 0.5
matrix_rate = 0.05
bias_rate = 0.3
matrix_decay = 0.01

def product(left, right):
    return jnp.dot(left, right, precision=lax.Precision.HIGHEST, preferred_element_type=jnp.float32)

def normalize(values):
    centred = values - lax.optimization_barrier(jnp.mean(values, axis=-1, keepdims=True))
    spread = lax.optimization_barrier(jnp.mean(centred * centred, axis=-1, keepdims=True))
    return centred * lax.rsqrt(spread + norm_epsilon)

def modulate(values, offset, factor):
    return normalize(values) * (1.0 + factor) + offset

def attend(inputs):
    queries, keys_in, values_in, visible = inputs
    scores = jnp.einsum('qhd,khd->hqk', queries, keys_in, precision=lax.Precision.HIGHEST) * HEAD_DIM ** (-0.5)
    scores = low_back(scores)
    scores = jnp.where(visible[None, None, :], scores, masked_score)
    weights = low(jax.nn.softmax(scores, axis=-1))
    return jnp.einsum('hqk,khd->qhd', weights, values_in, precision=lax.Precision.HIGHEST)

def residual_block(hidden, silu_low, wide_master, deep_master, bias, visible):
    sequences = hidden.shape[0]
    wide_matrix = low(wide_master)
    deep_matrix = low(deep_master)
    modulation = low_back(product(silu_low, wide_matrix[:, :6 * MODEL_WIDTH]) + bias[:6 * MODEL_WIDTH])
    modulation_parts = [modulation[:, None, number * MODEL_WIDTH:(number + 1) * MODEL_WIDTH] for number in range(6)]
    normed = low(modulate(hidden, modulation_parts[0], modulation_parts[1]))
    triple_bias = jnp.concatenate([bias[6 * MODEL_WIDTH:7 * MODEL_WIDTH], jnp.zeros((MODEL_WIDTH,), jnp.float32), bias[7 * MODEL_WIDTH:8 * MODEL_WIDTH]])
    triple = low(low_back(product(normed, wide_matrix[:, 6 * MODEL_WIDTH:9 * MODEL_WIDTH]) + triple_bias))
    pieces = triple.reshape(sequences, SEQ_LEN, 3, HEADS, HEAD_DIM)
    attended = lax.map(jax.checkpoint(attend), (pieces[:, :, 0], pieces[:, :, 1], pieces[:, :, 2], visible))
    attended = low(low_back(attended.reshape(sequences, SEQ_LEN, MODEL_WIDTH)))
    branch = low_back(product(attended, wide_matrix[:, 9 * MODEL_WIDTH:10 * MODEL_WIDTH]) + bias[8 * MODEL_WIDTH:9 * MODEL_WIDTH])
    middle = hidden + modulation_parts[2] * branch
    mixed = low(modulate(middle, modulation_parts[3], modulation_parts[4]))
    pre_active = low_back(product(mixed, wide_matrix[:, 10 * MODEL_WIDTH:]) + bias[9 * MODEL_WIDTH:9 * MODEL_WIDTH + FF])
    active = low(jax.nn.gelu(pre_active, approximate=True))
    feed_out = low_back(product(active, deep_matrix) + bias[9 * MODEL_WIDTH + FF:])
    return middle + modulation_parts[5] * feed_out

def projector(tapped, first_weight, rest_weight, bias, target_unit):
    first_pre = low_back(product(low(tapped), low(first_weight)) + bias[:PH])
    first_act = low(jax.nn.silu(first_pre))
    rest = low(rest_weight)
    second_pre = low_back(product(first_act, rest[:, :PH]) + bias[PH:2 * PH])
    second_act = low(jax.nn.silu(second_pre))
    projected = low_back(product(second_act, rest[:, PH:]) + bias[2 * PH:])
    unit = projected * lax.rsqrt(lax.optimization_barrier(jnp.sum(projected * projected, axis=-1, keepdims=True)) + norm_epsilon)
    return lax.optimization_barrier(jnp.sum(unit * target_unit, axis=-1))

def forward(hidden_in, params, silu_in, visible, unit_in):
    wide_all, deep_all, first_weight, rest_weight, bias_all, head_b = params
    tapped = residual_block(hidden_in, silu_in, wide_all[0], deep_all[0], bias_all[0], visible)
    aligned = projector(tapped, first_weight, rest_weight, head_b, unit_in)
    result = residual_block(tapped, silu_in, wide_all[1], deep_all[1], bias_all[1], visible)
    return (result, aligned)

def adam_update(weight, grad, first, second, rate, decay):
    first_new = 0.9 * first + 0.1 * grad
    second_new = 0.999 * second + 0.001 * grad * grad
    first_hat = first_new / (1.0 - 0.9 ** STEP)
    second_hat = second_new / (1.0 - 0.999 ** STEP)
    updated = weight - rate * (first_hat / (jnp.sqrt(second_hat) + adam_epsilon) + decay * weight)
    return (first_new, second_new, updated)

def reference(tokens, condition, lengths, targets, cotangent, wide_weight, deep_weight, head_first, head_second, block_bias, head_bias, wide_mean, deep_mean, head_first_mean, head_second_mean, block_bias_mean, head_bias_mean, wide_square, deep_square, head_first_square, head_second_square, block_bias_square, head_bias_square):
    group_size = 1
    while group_size * 2 * SEQ_LEN <= 4096 and BATCH % (group_size * 2) == 0:
        group_size = group_size * 2
    rounds = BATCH // group_size
    hidden = tokens.astype(jnp.float32).reshape(rounds, group_size, SEQ_LEN, MODEL_WIDTH)
    silu_low = low(jax.nn.silu(condition.astype(jnp.float32))).reshape(rounds, group_size, MODEL_WIDTH)
    raw_targets = targets.astype(jnp.float32)
    target_unit = raw_targets * lax.rsqrt(lax.optimization_barrier(jnp.sum(raw_targets * raw_targets, axis=-1, keepdims=True)) + norm_epsilon)
    target_unit = target_unit.reshape(rounds, group_size, SEQ_LEN, PZ)
    upstream = cotangent.astype(jnp.float32).reshape(rounds, group_size, SEQ_LEN, MODEL_WIDTH)
    length_rows = lengths.astype(jnp.int32).reshape(rounds, group_size)
    params = (wide_weight, deep_weight, head_first, head_second, block_bias, head_bias)

    def accumulate(totals, inputs):
        hidden_in, silu_in, length_in, unit_in, upstream_in = inputs
        visible = jnp.arange(SEQ_LEN, dtype=jnp.int32)[None, :] < length_in[:, None]
        (result, aligned), pullback = jax.vjp(partial(forward, silu_in=silu_in, visible=visible, unit_in=unit_in), hidden_in, params)
        input_part, weight_parts = pullback((upstream_in, -repa_weight * visible.astype(jnp.float32)))
        totals = jax.tree.map(jnp.add, totals, weight_parts)
        return (totals, (result.astype(jnp.bfloat16), input_part))
    starting = jax.tree.map(jnp.zeros_like, params)
    totals, (outputs, input_parts) = lax.scan(accumulate, starting, (hidden, silu_low, length_rows, target_unit, upstream))
    output = outputs.reshape(TOKENS, MODEL_WIDTH)
    input_grad = input_parts.reshape(TOKENS, MODEL_WIDTH)
    wide_grad, deep_grad, head_first_grad, head_second_grad, block_bias_grad, head_bias_grad = totals
    wide_m, wide_v, wide_new = adam_update(wide_weight, wide_grad, wide_mean, wide_square, matrix_rate, matrix_decay)
    deep_m, deep_v, deep_new = adam_update(deep_weight, deep_grad, deep_mean, deep_square, matrix_rate, matrix_decay)
    first_m, first_v, first_new = adam_update(head_first, head_first_grad, head_first_mean, head_first_square, matrix_rate, matrix_decay)
    second_m, second_v, second_new = adam_update(head_second, head_second_grad, head_second_mean, head_second_square, matrix_rate, matrix_decay)
    bias_m, bias_v, bias_new = adam_update(block_bias, block_bias_grad, block_bias_mean, block_bias_square, bias_rate, 0.0)
    hbias_m, hbias_v, hbias_new = adam_update(head_bias, head_bias_grad, head_bias_mean, head_bias_square, bias_rate, 0.0)
    return (output, input_grad, wide_grad, deep_grad, head_first_grad, head_second_grad, block_bias_grad, head_bias_grad, wide_m, deep_m, first_m, second_m, bias_m, hbias_m, wide_v, deep_v, first_v, second_v, bias_v, hbias_v, wide_new, deep_new, first_new, second_new, bias_new, hbias_new)
```

```python
import jax
import jax.numpy as jnp
from jax import lax
from jax.sharding import PartitionSpec as P

MODEL_WIDTH = 1152
HEADS = 16
HEAD_DIM = 72
FF = 4608
PH = 2048
PZ = 768
SEQ_LEN = 448
STEP = 10


norm_epsilon = 1e-06
adam_epsilon = 1e-08
masked_score = -1e30
repa_weight = 0.5
matrix_rate = 0.05
bias_rate = 0.3
matrix_decay = 0.01


def normalize(values):
    centred = values - jnp.mean(values, axis=-1, keepdims=True)
    spread = jnp.mean(centred * centred, axis=-1, keepdims=True)
    return centred * lax.rsqrt(spread + norm_epsilon)


def modulate(values, offset, factor):
    return normalize(values) * (1.0 + factor) + offset


def gelu_tanh(values):
    return jax.nn.gelu(values, approximate=True)


def split_modulation(modulation):
    columns = modulation.shape[-1] // 6
    return [modulation[:, None, number * columns : (number + 1) * columns] for number in range(6)]


def ring_order(chips):
    return list(range(0, chips, 2)) + list(range(1, chips, 2))[::-1]


def swap_cores(values):
    count = lax.axis_size("fsdp")
    return lax.ppermute(values, "fsdp", [(place, place ^ 1) for place in range(count)])


def paired_product(left, right):
    core = lax.axis_index("fsdp") % 2
    half = right.shape[-1] // 2
    kept = lax.dynamic_slice_in_dim(right, core * half, half, axis=1)
    sent = lax.dynamic_slice_in_dim(right, (1 - core) * half, half, axis=1)
    left_both = jnp.concatenate([left, swap_cores(left)], axis=0)
    right_both = jnp.concatenate([kept, swap_cores(sent)], axis=0)
    return lax.dot_general(
        left_both, right_both, (((0,), (0,)), ((), ())), preferred_element_type=jnp.float32
    ).astype(jnp.bfloat16)


def ring_reduce(term):
    count = lax.axis_size("fsdp")
    chips = count // 2
    device = lax.axis_index("fsdp")
    chip, core = device // 2, device % 2
    order = ring_order(chips)
    order_table = jnp.array(order, jnp.int32)
    place = jnp.array([order.index(number) for number in range(chips)], jnp.int32)[chip]
    parts = term.reshape(chips, 2, term.shape[0] // count, term.shape[1])
    totals = []
    for way, step in ((0, 1), (1, -1)):
        route = [
            (2 * order[spot] + side, 2 * order[(spot + step) % chips] + side)
            for spot in range(chips)
            for side in range(2)
        ]

        def own(hops):
            return parts[order_table[(place - step * hops) % chips], way]

        total = own(1)
        for hop in range(1, chips):
            total = lax.ppermute(total, "fsdp", route)
            total = (total.astype(jnp.float32) + own(hop + 1).astype(jnp.float32)).astype(
                jnp.bfloat16
            )
        totals.append(total)
    stacked = jnp.stack(totals)
    mine = stacked[core]
    other = swap_cores(stacked[1 - core])
    both = jnp.concatenate([mine, other, mine], axis=1)
    return lax.dynamic_slice_in_dim(
        both, core * term.shape[1], 2 * term.shape[1], axis=1
    )


def sum_copies(values):
    copies = lax.axis_size("rep")
    total = values.astype(jnp.float32)
    if copies == 2:
        return total + lax.ppermute(values, "rep", [(0, 1), (1, 0)]).astype(jnp.float32)
    return lax.psum(total, "rep")


def gathered_terms(row):
    return lax.all_gather(row, ("fsdp", "rep"), axis=0, tiled=True)


def fetch_block(wide_shard, deep_shard):
    rows = wide_shard.shape[0]
    count = lax.axis_size("fsdp")
    rest = wide_shard[:, 6 * MODEL_WIDTH :].astype(jnp.bfloat16)
    groups = rest.shape[1] // MODEL_WIDTH
    rest = rest.reshape(rows, groups, MODEL_WIDTH).transpose(1, 0, 2)
    deep = deep_shard.astype(jnp.bfloat16).reshape(-1, rows, MODEL_WIDTH)
    whole = lax.all_gather(
        jnp.concatenate([rest, deep], axis=0), "fsdp", axis=1, tiled=True
    )
    deep_whole = whole[groups:].reshape(-1, count, rows, MODEL_WIDTH)
    deep_whole = deep_whole.transpose(1, 0, 2, 3).reshape(-1, MODEL_WIDTH)
    return (whole[:groups], deep_whole)


def plane_modulation(silu_low, wide_weight, block_bias):
    count = lax.axis_size("fsdp")
    sequences = silu_low.shape[0]
    rows = wide_weight.shape[1]
    device = lax.axis_index("fsdp")
    spread = jnp.broadcast_to(
        silu_low.reshape(1, sequences, count, rows).transpose(2, 0, 1, 3)[:, 0],
        (count, sequences, rows),
    )
    met = lax.all_to_all(spread, "fsdp", 0, 0, tiled=True)
    met = met.reshape(count * sequences, rows)
    partial = [
        jnp.dot(
            met,
            wide_weight[block, :, : 6 * MODEL_WIDTH].astype(jnp.bfloat16),
            preferred_element_type=jnp.float32,
        )
        for block in range(2)
    ]
    partial = jnp.stack(partial, axis=1).reshape(count, sequences, 2, 6 * MODEL_WIDTH)
    back = lax.all_to_all(partial, "fsdp", 0, 0, tiled=True)
    total = jnp.sum(back, axis=0)
    return [total[:, block] + block_bias[block, : 6 * MODEL_WIDTH] for block in range(2)]


def attention_forward(inputs):
    queries, keys_in, values_in, visible = inputs
    factor = queries.shape[-1] ** (-0.5)
    scores = (
        jnp.einsum("qhd,khd->hqk", queries, keys_in, preferred_element_type=jnp.float32) * factor
    )
    scores = jnp.where(visible[None, None, :], scores, masked_score)
    largest = jnp.max(scores, axis=-1, keepdims=True)
    expanded = jnp.exp(scores - largest)
    totals = jnp.sum(expanded, axis=-1, keepdims=True)
    weights = (expanded / totals).astype(jnp.bfloat16)
    attended = jnp.einsum("hqk,khd->qhd", weights, values_in, preferred_element_type=jnp.float32)
    return (attended, largest + jnp.log(totals))


def attention_backward(inputs):
    queries, keys_in, values_in, visible, log_total, upstream = inputs
    factor = queries.shape[-1] ** (-0.5)
    scores = (
        jnp.einsum("qhd,khd->hqk", queries, keys_in, preferred_element_type=jnp.float32) * factor
    )
    scores = jnp.where(visible[None, None, :], scores, masked_score)
    chances = jnp.exp(scores - log_total)
    chance_grad = jnp.einsum(
        "qhd,khd->hqk", upstream, values_in, preferred_element_type=jnp.float32
    )
    value_grad = jnp.einsum(
        "hqk,qhd->khd", chances.astype(jnp.bfloat16), upstream, preferred_element_type=jnp.float32
    )
    centre = jnp.sum(chance_grad * chances, axis=-1, keepdims=True)
    score_grad = (chances * (chance_grad - centre)).astype(jnp.bfloat16)
    query_grad = (
        jnp.einsum("hqk,khd->qhd", score_grad, keys_in, preferred_element_type=jnp.float32) * factor
    )
    key_grad = (
        jnp.einsum("hqk,qhd->khd", score_grad, queries, preferred_element_type=jnp.float32) * factor
    )
    return (query_grad, key_grad, value_grad)


def joined(groups):
    return groups.transpose(1, 0, 2).reshape(groups.shape[1], -1)


def block_forward(hidden, modulation, wide_matrix, deep_matrix, bias, visible):
    sequences = hidden.shape[0]
    offset_first, factor_first, gate_first, offset_second, factor_second, gate_second = (
        split_modulation(modulation)
    )
    normed_low = modulate(hidden, offset_first, factor_first).astype(jnp.bfloat16)
    triple_bias = jnp.concatenate(
        [
            bias[6 * MODEL_WIDTH : 7 * MODEL_WIDTH],
            jnp.zeros((MODEL_WIDTH,), jnp.float32),
            bias[7 * MODEL_WIDTH : 8 * MODEL_WIDTH],
        ]
    )
    triple = (
        jnp.dot(
            normed_low,
            wide_matrix[0],
            preferred_element_type=jnp.float32,
        )
        + triple_bias
    ).astype(jnp.bfloat16)
    pieces = triple.reshape(sequences, SEQ_LEN, 3, HEADS, HEAD_DIM)
    attended, log_total = lax.map(
        attention_forward, (pieces[:, :, 0], pieces[:, :, 1], pieces[:, :, 2], visible)
    )
    attended_low = attended.reshape(sequences, SEQ_LEN, MODEL_WIDTH).astype(jnp.bfloat16)
    branch = (
        jnp.dot(
            attended_low,
            wide_matrix[1],
            preferred_element_type=jnp.float32,
        )
        + bias[8 * MODEL_WIDTH : 9 * MODEL_WIDTH]
    )
    middle = hidden + gate_first * branch
    mixed_low = modulate(middle, offset_second, factor_second).astype(jnp.bfloat16)
    pre_active = (
        jnp.dot(mixed_low, wide_matrix[2], preferred_element_type=jnp.float32)
        + bias[9 * MODEL_WIDTH : 9 * MODEL_WIDTH + FF]
    )
    active_low = gelu_tanh(pre_active).astype(jnp.bfloat16)
    feed_out = (
        jnp.dot(active_low, deep_matrix, preferred_element_type=jnp.float32)
        + bias[9 * MODEL_WIDTH + FF :]
    )
    result = middle + gate_second * feed_out
    saved = (
        hidden,
        modulation,
        normed_low,
        triple,
        log_total,
        attended_low,
        branch,
        middle,
        mixed_low,
        pre_active,
        active_low,
        feed_out,
    )
    return (result, saved)


def block_backward(upstream, saved, wide_matrix, deep_matrix, visible):
    (
        hidden,
        modulation,
        normed_low,
        triple,
        log_total,
        attended_low,
        branch,
        middle,
        mixed_low,
        pre_active,
        active_low,
        feed_out,
    ) = saved
    sequences = hidden.shape[0]
    offset_first, factor_first, gate_first, offset_second, factor_second, gate_second = (
        split_modulation(modulation)
    )
    feedforward_gradient = (upstream * gate_second).astype(jnp.bfloat16)
    gate_second_grad = jnp.sum(upstream * feed_out, axis=1)
    activation_gradient = jnp.einsum(
        "xjn,mn->xjm", feedforward_gradient, deep_matrix, preferred_element_type=jnp.float32
    )
    preactivation_gradient = jax.vjp(gelu_tanh, pre_active)[1](activation_gradient)[0].astype(
        jnp.bfloat16
    )
    mixed_grad = jnp.einsum(
        "qvm,am->qva",
        preactivation_gradient,
        wide_matrix[2],
        preferred_element_type=jnp.float32,
    )
    second_back = jax.vjp(modulate, middle, offset_second, factor_second)[1]
    middle_part, offset_second_grad, factor_second_grad = second_back(mixed_grad)
    middle_grad = upstream + middle_part
    gate_first_grad = jnp.sum(middle_grad * branch, axis=1)
    branch_gradient = (middle_grad * gate_first).astype(jnp.bfloat16)
    attended_grad = jnp.einsum(
        "tbr,ar->tba",
        branch_gradient,
        wide_matrix[1],
        preferred_element_type=jnp.float32,
    ).astype(jnp.bfloat16)
    pieces = triple.reshape(sequences, SEQ_LEN, 3, HEADS, HEAD_DIM)
    heads_grad = attended_grad.reshape(sequences, SEQ_LEN, HEADS, HEAD_DIM)
    query_grad, key_grad, value_grad = lax.map(
        attention_backward,
        (pieces[:, :, 0], pieces[:, :, 1], pieces[:, :, 2], visible, log_total, heads_grad),
    )
    triple_gradient = jnp.concatenate(
        [
            query_grad.reshape(sequences, SEQ_LEN, MODEL_WIDTH),
            key_grad.reshape(sequences, SEQ_LEN, MODEL_WIDTH),
            value_grad.reshape(sequences, SEQ_LEN, MODEL_WIDTH),
        ],
        axis=-1,
    ).astype(jnp.bfloat16)
    normed_grad = jnp.einsum(
        "tbr,ar->tba",
        triple_gradient,
        wide_matrix[0],
        preferred_element_type=jnp.float32,
    )
    first_back = jax.vjp(modulate, hidden, offset_first, factor_first)[1]
    hidden_part, offset_first_grad, factor_first_grad = first_back(normed_grad)
    hidden_grad = middle_grad + hidden_part
    modulation_grad = jnp.concatenate(
        [
            offset_first_grad[:, 0],
            factor_first_grad[:, 0],
            gate_first_grad,
            offset_second_grad[:, 0],
            factor_second_grad[:, 0],
            gate_second_grad,
        ],
        axis=-1,
    ).astype(jnp.bfloat16)
    bias_row = jnp.concatenate(
        [
            modulation_grad.astype(jnp.float32).sum(axis=0),
            jnp.sum(triple_gradient[..., :MODEL_WIDTH], axis=(0, 1), dtype=jnp.float32),
            jnp.sum(triple_gradient[..., 2 * MODEL_WIDTH :], axis=(0, 1), dtype=jnp.float32),
            jnp.sum(branch_gradient, axis=(0, 1), dtype=jnp.float32),
            jnp.sum(preactivation_gradient, axis=(0, 1), dtype=jnp.float32),
            jnp.sum(feedforward_gradient, axis=(0, 1), dtype=jnp.float32),
        ]
    )

    def flat(values):
        return values.reshape(-1, values.shape[-1])

    deep_grad = ring_reduce(paired_product(flat(active_low), flat(feedforward_gradient)))
    pre_grad = ring_reduce(paired_product(flat(mixed_low), flat(preactivation_gradient)))
    branch_grad = ring_reduce(paired_product(flat(attended_low), flat(branch_gradient)))
    triple_grad = ring_reduce(paired_product(flat(normed_low), flat(triple_gradient)))
    rest_grad = sum_copies(jnp.concatenate([triple_grad, branch_grad, pre_grad], axis=1))
    deep_grad = sum_copies(deep_grad)
    return (hidden_grad, modulation_grad, bias_row, rest_grad, deep_grad)


def adam_update(weight, grad, first, second, rate, decay):
    first_new = 0.9 * first + 0.1 * grad
    second_new = 0.999 * second + 0.001 * grad * grad
    first_hat = first_new / (1.0 - 0.9**STEP)
    second_hat = second_new / (1.0 - 0.999**STEP)
    updated = weight - rate * (first_hat / (jnp.sqrt(second_hat) + adam_epsilon) + decay * weight)
    return (first_new, second_new, updated)


def per_device(
    tokens,
    condition,
    lengths,
    targets,
    cotangent,
    wide_weight,
    deep_weight,
    head_first,
    head_second,
    block_bias,
    head_bias,
    wide_mean,
    deep_mean,
    head_first_mean,
    head_second_mean,
    block_bias_mean,
    head_bias_mean,
    wide_square,
    deep_square,
    head_first_square,
    head_second_square,
    block_bias_square,
    head_bias_square,
):
    sequences = condition.shape[0]
    hidden = tokens.astype(jnp.float32).reshape(sequences, SEQ_LEN, MODEL_WIDTH)
    silu_low = jax.nn.silu(condition.astype(jnp.float32)).astype(jnp.bfloat16)
    visible = jnp.arange(SEQ_LEN, dtype=jnp.int32)[None, :] < lengths[:, None]
    wide_early, deep_early = fetch_block(wide_weight[0], deep_weight[0])
    modulation_early, modulation_late = plane_modulation(silu_low, wide_weight, block_bias)
    wide_early = [joined(wide_early[:3]), wide_early[3], joined(wide_early[4:])]
    tapped, saved_early = block_forward(
        hidden, modulation_early, wide_early, deep_early, block_bias[0], visible
    )
    first_matrix, second_w = (
        lax.all_gather(head_first.astype(jnp.bfloat16), "fsdp", axis=0, tiled=True),
        lax.all_gather(head_second.astype(jnp.bfloat16), "fsdp", axis=0, tiled=True),
    )
    tapped_low = tapped.astype(jnp.bfloat16)
    first_pre = (
        jnp.dot(tapped_low, first_matrix, preferred_element_type=jnp.float32) + head_bias[:PH]
    )
    first_low = jax.nn.silu(first_pre).astype(jnp.bfloat16)
    second_pre = (
        jnp.dot(first_low, second_w[:, :PH], preferred_element_type=jnp.float32)
        + head_bias[PH : 2 * PH]
    )
    second_low = jax.nn.silu(second_pre).astype(jnp.bfloat16)
    projected = (
        jnp.dot(second_low, second_w[:, PH:], preferred_element_type=jnp.float32)
        + head_bias[2 * PH :]
    )
    wide_late, deep_late = fetch_block(wide_weight[1], deep_weight[1])
    wide_late = [joined(wide_late[:3]), wide_late[3], joined(wide_late[4:])]
    final, saved_late = block_forward(
        tapped, modulation_late, wide_late, deep_late, block_bias[1], visible
    )
    raw_targets = targets.astype(jnp.float32).reshape(sequences, SEQ_LEN, PZ)
    target_unit = raw_targets * lax.rsqrt(
        jnp.sum(raw_targets * raw_targets, axis=-1, keepdims=True) + norm_epsilon
    )

    def alignment(values):
        unit = values * lax.rsqrt(jnp.sum(values * values, axis=-1, keepdims=True) + norm_epsilon)
        return jnp.sum(unit * target_unit, axis=-1)

    upstream = cotangent.astype(jnp.float32).reshape(sequences, SEQ_LEN, MODEL_WIDTH)
    late_input_grad, late_modulation_grad, late_row, late_rest_grad, late_deep_grad = (
        block_backward(upstream, saved_late, wide_late, deep_late, visible)
    )
    projected_grad = jax.vjp(alignment, projected)[1](-repa_weight * visible.astype(jnp.float32))[
        0
    ].astype(jnp.bfloat16)
    second_act_grad = jnp.einsum(
        "slz,hz->slh", projected_grad, second_w[:, PH:], preferred_element_type=jnp.float32
    )
    second_grad = jax.vjp(jax.nn.silu, second_pre)[1](second_act_grad)[0].astype(jnp.bfloat16)
    first_act_grad = jnp.einsum(
        "slh,gh->slg", second_grad, second_w[:, :PH], preferred_element_type=jnp.float32
    )
    first_gradient = jax.vjp(jax.nn.silu, first_pre)[1](first_act_grad)[0].astype(jnp.bfloat16)
    tapped_gradient = jnp.einsum(
        "ejk,rk->ejr", first_gradient, first_matrix, preferred_element_type=jnp.float32
    )
    head_row = jnp.concatenate(
        [
            jnp.sum(first_gradient, axis=(0, 1), dtype=jnp.float32),
            jnp.sum(second_grad, axis=(0, 1), dtype=jnp.float32),
            jnp.sum(projected_grad, axis=(0, 1), dtype=jnp.float32),
        ]
    )

    def flat(values):
        return values.reshape(-1, values.shape[-1])

    first_weight_grad = sum_copies(
        ring_reduce(paired_product(flat(tapped_low), flat(first_gradient)))
    )
    second_weight_grad = sum_copies(
        jnp.concatenate(
            [
                ring_reduce(paired_product(flat(first_low), flat(second_grad))),
                ring_reduce(paired_product(flat(second_low), flat(projected_grad))),
            ],
            axis=1,
        )
    )
    input_grad, early_modulation_grad, early_row, early_rest_grad, early_deep_grad = (
        block_backward(
            late_input_grad + tapped_gradient, saved_early, wide_early, deep_early, visible
        )
    )
    all_silu = gathered_terms(silu_low)
    own_silu = lax.dynamic_slice_in_dim(
        all_silu,
        lax.axis_index("fsdp") * wide_weight.shape[1],
        wide_weight.shape[1],
        axis=1,
    )
    late_rows = gathered_terms(jnp.concatenate([late_row, head_row])[None])
    early_rows = gathered_terms(early_row[None])

    def modulation_weight_grad(rows):
        return lax.dot_general(
            own_silu,
            rows[:, : 6 * MODEL_WIDTH].astype(jnp.bfloat16),
            (((0,), (0,)), ((), ())),
            preferred_element_type=jnp.float32,
        )

    bias_width = block_bias.shape[1]
    wide_grad = jnp.stack(
        [
            jnp.concatenate([modulation_weight_grad(early_rows), early_rest_grad], axis=1),
            jnp.concatenate([modulation_weight_grad(late_rows), late_rest_grad], axis=1),
        ]
    )
    deep_grad = jnp.stack([early_deep_grad, late_deep_grad])
    late_sum = jnp.sum(late_rows, axis=0)
    block_bias_grad = jnp.stack([jnp.sum(early_rows, axis=0), late_sum[:bias_width]])
    head_bias_total = late_sum[bias_width:]
    wide_m, wide_v, wide_new = adam_update(
        wide_weight, wide_grad, wide_mean, wide_square, matrix_rate, matrix_decay
    )
    deep_m, deep_v, deep_new = adam_update(
        deep_weight, deep_grad, deep_mean, deep_square, matrix_rate, matrix_decay
    )
    first_m, first_v, first_new = adam_update(
        head_first, first_weight_grad, head_first_mean, head_first_square, matrix_rate, matrix_decay
    )
    second_m, second_v, second_new = adam_update(
        head_second,
        second_weight_grad,
        head_second_mean,
        head_second_square,
        matrix_rate,
        matrix_decay,
    )
    bias_m, bias_v, bias_new = adam_update(
        block_bias, block_bias_grad, block_bias_mean, block_bias_square, bias_rate, 0.0
    )
    hbias_m, hbias_v, hbias_new = adam_update(
        head_bias, head_bias_total, head_bias_mean, head_bias_square, bias_rate, 0.0
    )
    output = final.reshape(sequences * SEQ_LEN, MODEL_WIDTH).astype(jnp.bfloat16)
    input_flat = input_grad.reshape(sequences * SEQ_LEN, MODEL_WIDTH)
    return (
        output,
        input_flat,
        wide_grad,
        deep_grad,
        first_weight_grad,
        second_weight_grad,
        block_bias_grad,
        head_bias_total,
        wide_m,
        deep_m,
        first_m,
        second_m,
        bias_m,
        hbias_m,
        wide_v,
        deep_v,
        first_v,
        second_v,
        bias_v,
        hbias_v,
        wide_new,
        deep_new,
        first_new,
        second_new,
        bias_new,
        hbias_new,
    )


def solution(mesh):
    in_specs = (
        P(("fsdp", "rep"), None),
        P(("fsdp", "rep"), None),
        P(("fsdp", "rep")),
        P(("fsdp", "rep"), None),
        P(("fsdp", "rep"), None),
        P(None, "fsdp", None),
        P(None, "fsdp", None),
        P("fsdp", None),
        P("fsdp", None),
        P(),
        P(),
        P(None, "fsdp", None),
        P(None, "fsdp", None),
        P("fsdp", None),
        P("fsdp", None),
        P(),
        P(),
        P(None, "fsdp", None),
        P(None, "fsdp", None),
        P("fsdp", None),
        P("fsdp", None),
        P(),
        P(),
    )
    out_specs = (
        P(("fsdp", "rep"), None),
        P(("fsdp", "rep"), None),
        P(None, "fsdp", None),
        P(None, "fsdp", None),
        P("fsdp", None),
        P("fsdp", None),
        P(),
        P(),
        P(None, "fsdp", None),
        P(None, "fsdp", None),
        P("fsdp", None),
        P("fsdp", None),
        P(),
        P(),
        P(None, "fsdp", None),
        P(None, "fsdp", None),
        P("fsdp", None),
        P("fsdp", None),
        P(),
        P(),
        P(None, "fsdp", None),
        P(None, "fsdp", None),
        P("fsdp", None),
        P("fsdp", None),
        P(),
        P(),
    )
    return jax.shard_map(
        per_device, mesh=mesh, in_specs=in_specs, out_specs=out_specs, check_vma=False
    )
```

```python
from functools import partial
from typing import NamedTuple

import jax
import jax.numpy as jnp
from jax import lax
from jax.experimental import pallas as pl
from jax.experimental.pallas import tpu as pltpu
from jax.sharding import PartitionSpec as P

MESH = pl.DeviceIdType.MESH

MODEL_WIDTH = 1152
HEADS = 16
HEAD_DIM = 72
FF = 4608
PH = 2048
PZ = 768
SEQ_LEN = 448
STEP = 10


norm_epsilon = 1e-06
adam_epsilon = 1e-08
masked_score = -1e30
repa_weight = 0.5
matrix_rate = 0.05
bias_rate = 0.3
matrix_decay = 0.01


def normalize(values):
    centred = values - jnp.mean(values, axis=-1, keepdims=True)
    spread = jnp.mean(centred * centred, axis=-1, keepdims=True)
    return centred * lax.rsqrt(spread + norm_epsilon)


def modulate(values, offset, factor):
    return normalize(values) * (1.0 + factor) + offset


def gelu_tanh(values):
    return jax.nn.gelu(values, approximate=True)


def split_modulation(modulation):
    columns = modulation.shape[-1] // 6
    return [modulation[:, None, number * columns : (number + 1) * columns] for number in range(6)]


def outer_rows(left, right):
    flat_left = left.reshape(-1, left.shape[-1])
    flat_right = right.reshape(-1, right.shape[-1])
    return lax.dot_general(
        flat_left, flat_right, (((0,), (0,)), ((), ())), preferred_element_type=jnp.float32
    )


def swap_cores(values):
    count = lax.axis_size("fsdp")
    return lax.ppermute(values, "fsdp", [(place, place ^ 1) for place in range(count)])


class Term(NamedTuple):
    left: int
    right: int
    rows: int
    row_from: int
    columns: int
    column_from: int
    split: bool
    way: int
    start: int


def ring_place(chip, chips):
    return lax.div(chip, 2) + lax.rem(chip, 2) * (chips - 1 - 2 * lax.div(chip, 2))


def ring_chip(place, chips):
    upper = lax.div(place, (chips + 1) // 2)
    return 2 * place + upper * (2 * (chips - 1 - place) + 1 - 2 * place)


def reduce_body(terms, chips, lefts, rights, *refs):
    refs = list(refs)

    def take(count):
        taken = refs[:count]
        del refs[:count]
        return taken

    left_refs, right_refs = take(lefts), take(rights)
    outs = take(len(terms))
    own_left, own_right = take(lefts), take(rights)
    sib_left, sib_right = take(lefts), take(rights)
    landing, final = take(len(terms)), take(len(terms))
    split_at = [number for number, term in enumerate(terms) if term.split]
    give, got = take(len(split_at)), take(len(split_at))
    load_sem, swap_send, swap_recv, ring_send, ring_recv = take(5)
    give_send, got_recv, final_send, final_recv = take(4)

    device = lax.axis_index("fsdp")
    plane = lax.axis_index("rep")
    core, chip = lax.rem(device, 2), lax.div(device, 2)
    place = ring_place(chip, chips)
    sibling = {"fsdp": device + 1 - 2 * core}
    twin = {"rep": 1 - plane}
    ways = [
        {"fsdp": 2 * ring_chip(lax.rem(place + step, chips), chips) + core}
        for step in (1, chips - 1)
    ]

    barrier = pltpu.get_barrier_semaphore()
    partners = (ways[0], ways[1], sibling, twin)
    for partner in partners:
        pl.semaphore_signal(barrier, inc=1, device_id=partner, device_id_type=MESH)
    pl.semaphore_wait(barrier, len(partners))

    def remote(source, target, send_sem, recv_sem, partner):
        return pltpu.make_async_remote_copy(
            src_ref=source,
            dst_ref=target,
            send_sem=send_sem,
            recv_sem=recv_sem,
            device_id=partner,
            device_id_type=MESH,
        )

    loads, swaps = {}, {}
    for number in range(lefts):
        ref = left_refs[number]
        by_rows = len(ref.shape) == 4
        mine = ref.at[:, core] if by_rows else ref
        other = ref.at[:, 1 - core] if by_rows else ref
        loads["l", number] = pltpu.make_async_copy(mine, own_left[number], load_sem.at[number])
        swaps["l", number] = remote(
            other, sib_left[number], swap_send.at[number], swap_recv.at[number], sibling
        )
    for number in range(rights):
        ref, at = right_refs[number], lefts + number
        width = own_right[number].shape[1]
        if width == ref.shape[1]:
            mine = other = ref
        else:
            mine = ref.at[:, pl.ds(pl.multiple_of(core * width, 128), width)]
            other = ref.at[:, pl.ds(pl.multiple_of((1 - core) * width, 128), width)]
        loads["r", number] = pltpu.make_async_copy(mine, own_right[number], load_sem.at[at])
        swaps["r", number] = remote(
            other, sib_right[number], swap_send.at[at], swap_recv.at[at], sibling
        )
    first_use = {}
    for term in sorted(terms, key=lambda term: term.start - term.split):
        for key in (("l", term.left), ("r", term.right)):
            first_use.setdefault(key, term.start - term.split)
    for key in first_use:
        loads[key].start()
        swaps[key].start()
    for number, term in enumerate(terms):
        landing[number][0] = jnp.zeros(landing[number].shape[1:], jnp.bfloat16)

    def chunk(term, owner, part):
        rows = pl.ds(term.row_from, term.rows)
        from_column = term.column_from
        if term.split:
            from_column = pl.multiple_of(from_column + part * term.columns, 128)
        columns = pl.ds(from_column, term.columns)
        own = jnp.dot(
            own_left[term.left][owner, rows, :],
            own_right[term.right][:, columns],
            preferred_element_type=jnp.float32,
        )
        return own + jnp.dot(
            sib_left[term.left][owner, rows, :],
            sib_right[term.right][:, columns],
            preferred_element_type=jnp.float32,
        )

    def owner_at(term, hop):
        back = hop + 1 if term.way == 0 else 2 * chips - 1 - hop
        return ring_chip(lax.rem(place + 2 * chips - back, chips), chips)

    def give_copy(at, hop):
        return remote(
            give[at].at[hop],
            got[at].at[hop],
            give_send.at[at, hop],
            got_recv.at[at, hop],
            twin,
        )

    def ring_copy(number, hop):
        return remote(
            landing[number].at[hop],
            landing[number].at[hop + 1],
            ring_send.at[number, hop],
            ring_recv.at[number, hop + 1],
            ways[terms[number].way],
        )

    def arrival(number, hop):
        return remote(
            landing[number].at[hop],
            landing[number].at[hop],
            ring_send.at[number, hop],
            ring_recv.at[number, hop],
            ways[terms[number].way],
        )

    def final_copy(number):
        return remote(
            landing[number].at[chips - 1],
            final[number],
            final_send.at[number],
            final_recv.at[number],
            twin,
        )

    def step(clock, carry):
        for moment in sorted(set(first_use.values())):

            @pl.when(clock == moment)
            def _():
                for key, use in first_use.items():
                    if use == moment:
                        loads[key].wait()
                        swaps[key].wait_recv()

        for at, number in enumerate(split_at):
            term = terms[number]
            later = clock - term.start + 1

            @pl.when((later >= 0) & (later < chips))
            def _():
                give[at][later] = chunk(term, owner_at(term, later), 1 - plane).astype(
                    jnp.bfloat16
                )
                give_copy(at, later).start()

        for number, term in enumerate(terms):
            hop = clock - term.start

            @pl.when((hop >= 0) & (hop < chips))
            def _():
                total = chunk(term, owner_at(term, hop), plane)
                if term.split:
                    at = split_at.index(number)
                    give_copy(at, hop).wait_recv()
                    total = total + got[at][hop].astype(jnp.float32)

                @pl.when(hop > 0)
                def _():
                    arrival(number, hop).wait_recv()

                landing[number][hop] = (
                    total + landing[number][hop].astype(jnp.float32)
                ).astype(jnp.bfloat16)

                @pl.when(hop < chips - 1)
                def _():
                    ring_copy(number, hop).start()

                @pl.when(hop == chips - 1)
                def _():
                    final_copy(number).start()

        return carry

    lax.fori_loop(0, max(term.start for term in terms) + chips, step, 0)
    for number, term in enumerate(terms):
        final_copy(number).wait()
        mine = landing[number][chips - 1].astype(jnp.float32)
        other = final[number][...].astype(jnp.float32)
        if term.split:
            width = term.columns
            outs[number][:, pl.ds(pl.multiple_of(plane * width, 128), width)] = mine
            outs[number][:, pl.ds(pl.multiple_of((1 - plane) * width, 128), width)] = other
        else:
            outs[number][...] = mine + other

    def settle(hop, carry):
        for number in range(len(terms)):

            @pl.when(hop < chips - 1)
            def _():
                ring_copy(number, hop).wait_send()

        for at in range(len(split_at)):
            give_copy(at, hop).wait_send()
        return carry

    lax.fori_loop(0, chips, settle, 0)
    for key in first_use:
        swaps[key].wait_send()


def reduce_terms(terms, lefts, rights, identity):
    chips = lefts[0].shape[0]
    whole = {term.right for term in terms if lefts[term.left].ndim == 4}
    left_parts = [
        (left.shape[0],) + left.shape[-2:] for left in lefts
    ]
    right_parts = [
        (right.shape[0], right.shape[1] if number in whole else right.shape[1] // 2)
        for number, right in enumerate(rights)
    ]

    def vmem(shape):
        return pltpu.VMEM(shape, jnp.bfloat16)

    splits = [term for term in terms if term.split]
    operands = len(lefts) + len(rights)
    scratch = (
        [vmem(shape) for shape in left_parts + right_parts] * 2
        + [vmem((chips, term.rows, term.columns)) for term in terms]
        + [vmem((term.rows, term.columns)) for term in terms]
        + [vmem((chips, term.rows, term.columns)) for term in splits] * 2
        + [pltpu.SemaphoreType.DMA((operands,))] * 3
        + [pltpu.SemaphoreType.DMA((len(terms), chips))] * 2
        + [pltpu.SemaphoreType.DMA((len(splits), chips))] * 2
        + [pltpu.SemaphoreType.DMA((len(terms),))] * 2
    )
    return pl.pallas_call(
        partial(reduce_body, terms, chips, len(lefts), len(rights)),
        out_shape=[
            jax.ShapeDtypeStruct((term.rows, term.columns * (1 + term.split)), jnp.float32)
            for term in terms
        ],
        in_specs=[pl.BlockSpec(memory_space=pl.ANY)] * operands,
        out_specs=[pl.BlockSpec(memory_space=pltpu.VMEM)] * len(terms),
        scratch_shapes=scratch,
        compiler_params=pltpu.CompilerParams(
            collective_id=identity, has_side_effects=True, vmem_limit_bytes=60 * 1024 * 1024
        ),
    )(*lefts, *rights)


def by_chip(values):
    chips = lax.axis_size("fsdp") // 2
    return values.T.reshape(chips, -1, values.shape[0])


def by_device(values):
    chips = lax.axis_size("fsdp") // 2
    return values.T.reshape(chips, 2, -1, values.shape[0])


def padded_halves(values, half):
    tokens, columns = values.shape
    halves = values.reshape(tokens, 2, columns // 2)
    return jnp.pad(halves, ((0, 0), (0, 0), (0, half - columns // 2))).reshape(tokens, 2 * half)


def join_cores(pieces):
    core = lax.axis_index("fsdp") % 2
    both = jnp.concatenate(pieces, axis=1)
    rows = both.shape[0] // 2
    mine = lax.dynamic_slice_in_dim(both, core * rows, rows, axis=0)
    sent = lax.dynamic_slice_in_dim(both, (1 - core) * rows, rows, axis=0)
    other = swap_cores(sent)
    low = jnp.where(core == 0, mine, other)
    high = jnp.where(core == 0, other, mine)
    joined, at = [], 0
    for piece in pieces:
        end = at + piece.shape[1]
        joined += [low[:, at:end], high[:, at:end]]
        at = end
    return jnp.concatenate(joined, axis=1)


def round_up(value, step):
    return -(-value // step) * step


def plain_sum(left, right):
    total = lax.psum_scatter(
        outer_rows(left, right).astype(jnp.bfloat16), "fsdp", scatter_dimension=0, tiled=True
    )
    return lax.psum(total.astype(jnp.float32), "rep")


def kernels_fit(rows):
    return 2 * rows % 16 == 0 and lax.axis_size("rep") == 2


def sum_block_grads(
    normed, triple_grad, attended, branch_grad, mixed, pre_grad, active, feed_grad, identity
):
    rows = MODEL_WIDTH // lax.axis_size("fsdp")
    if not kernels_fit(rows):
        wide = jnp.concatenate(
            [
                plain_sum(normed, triple_grad),
                plain_sum(attended, branch_grad),
                plain_sum(mixed, pre_grad),
            ],
            axis=1,
        )
        return (wide, plain_sum(active, feed_grad))
    triple_half = round_up(triple_grad.shape[1] // 2, 256)
    branch_half = round_up(branch_grad.shape[1] // 2, 128)
    pre_half = pre_grad.shape[1] // 2
    plain_part = 8 * 128
    pre_part = (pre_half - plain_part) // 2
    deep_rows = active.shape[1] // lax.axis_size("fsdp") // 2
    terms = (
        Term(0, 0, 2 * rows, 0, triple_half // 2, 0, True, 0, 1),
        Term(2, 2, 2 * rows, 0, pre_part, plain_part, True, 1, 1),
        Term(3, 3, deep_rows, 0, MODEL_WIDTH, 0, False, 0, 1),
        Term(3, 3, deep_rows, deep_rows, MODEL_WIDTH, 0, False, 1, 1),
        Term(1, 1, 2 * rows, 0, branch_half, 0, False, 0, 2),
        Term(2, 2, 2 * rows, 0, plain_part, 0, False, 1, 2),
    )
    triple, pre_late, deep_low, deep_high, branch, pre_early = reduce_terms(
        terms,
        [by_chip(normed), by_chip(attended), by_chip(mixed), by_device(active)],
        [
            padded_halves(triple_grad, triple_half),
            padded_halves(branch_grad, branch_half),
            pre_grad,
            feed_grad,
        ],
        identity,
    )
    wide = join_cores(
        [
            triple[:, : triple_grad.shape[1] // 2],
            branch[:, : branch_grad.shape[1] // 2],
            jnp.concatenate([pre_early, pre_late], axis=1),
        ]
    )
    return (wide, jnp.concatenate([deep_low, deep_high], axis=0))


def sum_head_grads(tapped, first_grad, first, second_grad, second, projected_grad, identity):
    count = lax.axis_size("fsdp")
    rows, head_rows = tapped.shape[1] // count, first.shape[1] // count
    if not kernels_fit(rows):
        return (
            plain_sum(tapped, first_grad),
            jnp.concatenate(
                [plain_sum(first, second_grad), plain_sum(second, projected_grad)], axis=1
            ),
        )
    half, last = first_grad.shape[1] // 2, projected_grad.shape[1] // 2
    terms = (
        Term(1, 1, 2 * head_rows, 0, half // 2, 0, True, 1, 1),
        Term(0, 0, 2 * rows, 0, half, 0, False, 0, 1),
        Term(2, 2, 2 * head_rows, 0, last - 128, 128, False, 1, 1),
        Term(2, 2, 2 * head_rows, 0, 128, 0, False, 0, 1),
    )
    second_out, first_out, third_late, third_early = reduce_terms(
        terms,
        [by_chip(tapped), by_chip(first), by_chip(second)],
        [first_grad, second_grad, projected_grad],
        identity,
    )
    return (
        join_cores([first_out]),
        join_cores([second_out, jnp.concatenate([third_early, third_late], axis=1)]),
    )


def gathered_terms(row):
    return lax.all_gather(row, ("fsdp", "rep"), axis=0, tiled=True)


def fetch_block(wide_shard, deep_shard):
    rest = wide_shard[:, 6 * MODEL_WIDTH :].astype(jnp.bfloat16)
    whole = lax.all_gather(rest, "fsdp", axis=0, tiled=True)
    deep = lax.all_gather(deep_shard.astype(jnp.bfloat16), "fsdp", axis=0, tiled=True)
    split = (
        whole[:, : 3 * MODEL_WIDTH],
        whole[:, 3 * MODEL_WIDTH : 4 * MODEL_WIDTH],
        whole[:, 4 * MODEL_WIDTH :],
    )
    return (split, deep)


def plane_modulation(silu_low, wide_weight, block_bias):
    count = lax.axis_size("fsdp")
    sequences = silu_low.shape[0]
    rows = wide_weight.shape[1]
    device = lax.axis_index("fsdp")
    spread = jnp.broadcast_to(
        silu_low.reshape(1, sequences, count, rows).transpose(2, 0, 1, 3)[:, 0],
        (count, sequences, rows),
    )
    met = lax.all_to_all(spread, "fsdp", 0, 0, tiled=True)
    met = met.reshape(count * sequences, rows)
    partial = [
        jnp.dot(
            met,
            wide_weight[block, :, : 6 * MODEL_WIDTH].astype(jnp.bfloat16),
            preferred_element_type=jnp.float32,
        )
        for block in range(2)
    ]
    partial = jnp.stack(partial, axis=1).reshape(count, sequences, 2, 6 * MODEL_WIDTH)
    back = lax.all_to_all(partial, "fsdp", 0, 0, tiled=True)
    total = jnp.sum(back, axis=0)
    return [total[:, block] + block_bias[block, : 6 * MODEL_WIDTH] for block in range(2)]


def attention_forward(inputs):
    queries, keys_in, values_in, visible = inputs
    factor = queries.shape[-1] ** (-0.5)
    scores = (
        jnp.einsum("qhd,khd->hqk", queries, keys_in, preferred_element_type=jnp.float32) * factor
    )
    scores = jnp.where(visible[None, None, :], scores, masked_score)
    largest = jnp.max(scores, axis=-1, keepdims=True)
    expanded = jnp.exp(scores - largest)
    totals = jnp.sum(expanded, axis=-1, keepdims=True)
    weights = (expanded / totals).astype(jnp.bfloat16)
    attended = jnp.einsum("hqk,khd->qhd", weights, values_in, preferred_element_type=jnp.float32)
    return (attended, largest + jnp.log(totals))


def attention_scores_backward(queries, keys_in, values_in, visible, log_total, upstream):
    factor = queries.shape[-1] ** (-0.5)
    scores = (
        jnp.einsum("sqhd,skhd->shqk", queries, keys_in, preferred_element_type=jnp.float32)
        * factor
    )
    scores = jnp.where(visible[:, None, None, :], scores, masked_score)
    chances = jnp.exp(scores - log_total)
    chance_grad = jnp.einsum(
        "sqhd,skhd->shqk", upstream, values_in, preferred_element_type=jnp.float32
    )
    centre = jnp.sum(chance_grad * chances, axis=-1, keepdims=True)
    score_grad = (chances * (chance_grad - centre)).astype(jnp.bfloat16)
    return (chances.astype(jnp.bfloat16), score_grad)


def attention_products_backward(queries, keys_in, chances_low, score_grad, upstream):
    factor = queries.shape[-1] ** (-0.5)
    value_grad = jnp.einsum(
        "shqk,sqhd->skhd", chances_low, upstream, preferred_element_type=jnp.float32
    )
    query_grad = (
        jnp.einsum("shqk,skhd->sqhd", score_grad, keys_in, preferred_element_type=jnp.float32)
        * factor
    )
    key_grad = (
        jnp.einsum("shqk,sqhd->skhd", score_grad, queries, preferred_element_type=jnp.float32)
        * factor
    )
    return (query_grad, key_grad, value_grad)


def block_forward(hidden, modulation, wide_matrix, deep_matrix, bias, visible):
    sequences = hidden.shape[0]
    offset_first, factor_first, gate_first, offset_second, factor_second, gate_second = (
        split_modulation(modulation)
    )
    normed_low = modulate(hidden, offset_first, factor_first).astype(jnp.bfloat16)
    triple_bias = jnp.concatenate(
        [
            bias[6 * MODEL_WIDTH : 7 * MODEL_WIDTH],
            jnp.zeros((MODEL_WIDTH,), jnp.float32),
            bias[7 * MODEL_WIDTH : 8 * MODEL_WIDTH],
        ]
    )
    triple = (
        jnp.dot(
            normed_low,
            wide_matrix[0],
            preferred_element_type=jnp.float32,
        )
        + triple_bias
    ).astype(jnp.bfloat16)
    pieces = triple.reshape(sequences, SEQ_LEN, 3, HEADS, HEAD_DIM)
    attended, log_total = lax.map(
        attention_forward, (pieces[:, :, 0], pieces[:, :, 1], pieces[:, :, 2], visible)
    )
    attended_low = attended.reshape(sequences, SEQ_LEN, MODEL_WIDTH).astype(jnp.bfloat16)
    branch = (
        jnp.dot(
            attended_low,
            wide_matrix[1],
            preferred_element_type=jnp.float32,
        )
        + bias[8 * MODEL_WIDTH : 9 * MODEL_WIDTH]
    )
    middle = hidden + gate_first * branch
    mixed_low = modulate(middle, offset_second, factor_second).astype(jnp.bfloat16)
    pre_active = (
        jnp.dot(mixed_low, wide_matrix[2], preferred_element_type=jnp.float32)
        + bias[9 * MODEL_WIDTH : 9 * MODEL_WIDTH + FF]
    )
    active_low = gelu_tanh(pre_active).astype(jnp.bfloat16)
    feed_out = (
        jnp.dot(active_low, deep_matrix, preferred_element_type=jnp.float32)
        + bias[9 * MODEL_WIDTH + FF :]
    )
    result = middle + gate_second * feed_out
    saved = (
        hidden,
        modulation,
        normed_low,
        triple,
        log_total,
        attended_low,
        branch,
        middle,
        mixed_low,
        pre_active,
        active_low,
        feed_out,
    )
    return (result, saved)


def block_backward(upstream, saved, wide_matrix, deep_matrix, visible, identity):
    (
        hidden,
        modulation,
        normed_low,
        triple,
        log_total,
        attended_low,
        branch,
        middle,
        mixed_low,
        pre_active,
        active_low,
        feed_out,
    ) = saved
    sequences = hidden.shape[0]
    offset_first, factor_first, gate_first, offset_second, factor_second, gate_second = (
        split_modulation(modulation)
    )
    feedforward_gradient = (upstream * gate_second).astype(jnp.bfloat16)
    gate_second_grad = jnp.sum(upstream * feed_out, axis=1)
    activation_gradient = jnp.einsum(
        "xjn,mn->xjm", feedforward_gradient, deep_matrix, preferred_element_type=jnp.float32
    )
    preactivation_gradient = jax.vjp(gelu_tanh, pre_active)[1](activation_gradient)[0].astype(
        jnp.bfloat16
    )
    mixed_grad = jnp.einsum(
        "qvm,am->qva",
        preactivation_gradient,
        wide_matrix[2],
        preferred_element_type=jnp.float32,
    )
    second_back = jax.vjp(modulate, middle, offset_second, factor_second)[1]
    middle_part, offset_second_grad, factor_second_grad = second_back(mixed_grad)
    middle_grad = upstream + middle_part
    gate_first_grad = jnp.sum(middle_grad * branch, axis=1)
    branch_gradient = (middle_grad * gate_first).astype(jnp.bfloat16)
    attended_grad = jnp.einsum(
        "tbr,ar->tba",
        branch_gradient,
        wide_matrix[1],
        preferred_element_type=jnp.float32,
    ).astype(jnp.bfloat16)
    pieces = triple.reshape(sequences, SEQ_LEN, 3, HEADS, HEAD_DIM)
    heads_grad = attended_grad.reshape(sequences, SEQ_LEN, HEADS, HEAD_DIM)
    queries, keys_in, values_in = pieces[:, :, 0], pieces[:, :, 1], pieces[:, :, 2]
    chances_low, score_grad = attention_scores_backward(
        queries, keys_in, values_in, visible, log_total, heads_grad
    )
    query_grad, key_grad, value_grad = attention_products_backward(
        queries, keys_in, chances_low, score_grad, heads_grad
    )
    triple_gradient = jnp.concatenate(
        [
            query_grad.reshape(sequences, SEQ_LEN, MODEL_WIDTH),
            key_grad.reshape(sequences, SEQ_LEN, MODEL_WIDTH),
            value_grad.reshape(sequences, SEQ_LEN, MODEL_WIDTH),
        ],
        axis=-1,
    ).astype(jnp.bfloat16)
    normed_grad = jnp.einsum(
        "tbr,ar->tba",
        triple_gradient,
        wide_matrix[0],
        preferred_element_type=jnp.float32,
    )
    first_back = jax.vjp(modulate, hidden, offset_first, factor_first)[1]
    hidden_part, offset_first_grad, factor_first_grad = first_back(normed_grad)
    hidden_grad = middle_grad + hidden_part
    modulation_grad = jnp.concatenate(
        [
            offset_first_grad[:, 0],
            factor_first_grad[:, 0],
            gate_first_grad,
            offset_second_grad[:, 0],
            factor_second_grad[:, 0],
            gate_second_grad,
        ],
        axis=-1,
    ).astype(jnp.bfloat16)
    bias_row = jnp.concatenate(
        [
            modulation_grad.astype(jnp.float32).sum(axis=0),
            jnp.sum(triple_gradient[..., :MODEL_WIDTH], axis=(0, 1), dtype=jnp.float32),
            jnp.sum(triple_gradient[..., 2 * MODEL_WIDTH :], axis=(0, 1), dtype=jnp.float32),
            jnp.sum(branch_gradient, axis=(0, 1), dtype=jnp.float32),
            jnp.sum(preactivation_gradient, axis=(0, 1), dtype=jnp.float32),
            jnp.sum(feedforward_gradient, axis=(0, 1), dtype=jnp.float32),
        ]
    )

    def flat(values):
        return values.reshape(-1, values.shape[-1])

    weight_grads = sum_block_grads(
        flat(normed_low),
        flat(triple_gradient),
        flat(attended_low),
        flat(branch_gradient),
        flat(mixed_low),
        flat(preactivation_gradient),
        flat(active_low),
        flat(feedforward_gradient),
        identity,
    )
    return (hidden_grad, modulation_grad, bias_row, weight_grads)


def adam_update(weight, grad, first, second, rate, decay):
    first_new = 0.9 * first + 0.1 * grad
    second_new = 0.999 * second + 0.001 * grad * grad
    first_hat = first_new / (1.0 - 0.9**STEP)
    second_hat = second_new / (1.0 - 0.999**STEP)
    updated = weight - rate * (first_hat / (jnp.sqrt(second_hat) + adam_epsilon) + decay * weight)
    return (first_new, second_new, updated)


def per_device(
    tokens,
    condition,
    lengths,
    targets,
    cotangent,
    wide_weight,
    deep_weight,
    head_first,
    head_second,
    block_bias,
    head_bias,
    wide_mean,
    deep_mean,
    head_first_mean,
    head_second_mean,
    block_bias_mean,
    head_bias_mean,
    wide_square,
    deep_square,
    head_first_square,
    head_second_square,
    block_bias_square,
    head_bias_square,
):
    sequences = condition.shape[0]
    hidden = tokens.astype(jnp.float32).reshape(sequences, SEQ_LEN, MODEL_WIDTH)
    silu_low = jax.nn.silu(condition.astype(jnp.float32)).astype(jnp.bfloat16)
    visible = jnp.arange(SEQ_LEN, dtype=jnp.int32)[None, :] < lengths[:, None]
    wide_early, deep_early = fetch_block(wide_weight[0], deep_weight[0])
    modulation_early, modulation_late = plane_modulation(silu_low, wide_weight, block_bias)
    tapped, saved_early = block_forward(
        hidden, modulation_early, wide_early, deep_early, block_bias[0], visible
    )
    wide_late, deep_late = fetch_block(wide_weight[1], deep_weight[1])
    first_matrix, second_w = (
        lax.all_gather(head_first.astype(jnp.bfloat16), "fsdp", axis=0, tiled=True),
        lax.all_gather(head_second.astype(jnp.bfloat16), "fsdp", axis=0, tiled=True),
    )
    final, saved_late = block_forward(
        tapped, modulation_late, wide_late, deep_late, block_bias[1], visible
    )
    raw_targets = targets.astype(jnp.float32).reshape(sequences, SEQ_LEN, PZ)
    target_unit = raw_targets * lax.rsqrt(
        jnp.sum(raw_targets * raw_targets, axis=-1, keepdims=True) + norm_epsilon
    )

    def alignment(values):
        unit = values * lax.rsqrt(jnp.sum(values * values, axis=-1, keepdims=True) + norm_epsilon)
        return jnp.sum(unit * target_unit, axis=-1)

    upstream = cotangent.astype(jnp.float32).reshape(sequences, SEQ_LEN, MODEL_WIDTH)
    late_input_grad, late_modulation_grad, late_row, late_grads = block_backward(
        upstream, saved_late, wide_late, deep_late, visible, 0
    )
    tapped_low, late_input_grad = lax.optimization_barrier(
        (tapped.astype(jnp.bfloat16), late_input_grad)
    )
    first_pre = (
        jnp.dot(tapped_low, first_matrix, preferred_element_type=jnp.float32) + head_bias[:PH]
    )
    first_low = jax.nn.silu(first_pre).astype(jnp.bfloat16)
    second_pre = (
        jnp.dot(first_low, second_w[:, :PH], preferred_element_type=jnp.float32)
        + head_bias[PH : 2 * PH]
    )
    second_low = jax.nn.silu(second_pre).astype(jnp.bfloat16)
    projected = (
        jnp.dot(second_low, second_w[:, PH:], preferred_element_type=jnp.float32)
        + head_bias[2 * PH :]
    )
    projected_grad = jax.vjp(alignment, projected)[1](-repa_weight * visible.astype(jnp.float32))[
        0
    ].astype(jnp.bfloat16)
    second_act_grad = jnp.einsum(
        "slz,hz->slh", projected_grad, second_w[:, PH:], preferred_element_type=jnp.float32
    )
    second_grad = jax.vjp(jax.nn.silu, second_pre)[1](second_act_grad)[0].astype(jnp.bfloat16)
    first_act_grad = jnp.einsum(
        "slh,gh->slg", second_grad, second_w[:, :PH], preferred_element_type=jnp.float32
    )
    first_gradient = jax.vjp(jax.nn.silu, first_pre)[1](first_act_grad)[0].astype(jnp.bfloat16)
    tapped_gradient = jnp.einsum(
        "ejk,rk->ejr", first_gradient, first_matrix, preferred_element_type=jnp.float32
    )
    head_row = jnp.concatenate(
        [
            jnp.sum(first_gradient, axis=(0, 1), dtype=jnp.float32),
            jnp.sum(second_grad, axis=(0, 1), dtype=jnp.float32),
            jnp.sum(projected_grad, axis=(0, 1), dtype=jnp.float32),
        ]
    )


    def flat(values):
        return values.reshape(-1, values.shape[-1])

    first_weight_grad, second_weight_grad = sum_head_grads(
        flat(tapped_low),
        flat(first_gradient),
        flat(first_low),
        flat(second_grad),
        flat(second_low),
        flat(projected_grad),
        1,
    )
    input_grad, early_modulation_grad, early_row, early_grads = block_backward(
        late_input_grad + tapped_gradient,
        saved_early,
        wide_early,
        deep_early,
        visible,
        2,
    )
    late_rows = gathered_terms(
        jnp.concatenate([silu_low.astype(jnp.float32)[0], late_row, head_row])[None]
    )
    own_silu = lax.dynamic_slice_in_dim(
        late_rows,
        lax.axis_index("fsdp") * wide_weight.shape[1],
        wide_weight.shape[1],
        axis=1,
    ).astype(jnp.bfloat16)
    late_rows = late_rows[:, MODEL_WIDTH:]
    early_rows = gathered_terms(early_row[None])

    def modulation_weight_grad(rows):
        return lax.dot_general(
            own_silu,
            rows[:, : 6 * MODEL_WIDTH].astype(jnp.bfloat16),
            (((0,), (0,)), ((), ())),
            preferred_element_type=jnp.float32,
        )

    bias_width = block_bias.shape[1]
    wide_grad = jnp.stack(
        [
            jnp.concatenate(
                [modulation_weight_grad(early_rows), early_grads[0]],
                axis=1,
            ),
            jnp.concatenate(
                [modulation_weight_grad(late_rows), late_grads[0]],
                axis=1,
            ),
        ]
    )
    deep_grad = jnp.stack([early_grads[1], late_grads[1]])
    late_sum = jnp.sum(late_rows, axis=0)
    block_bias_grad = jnp.stack([jnp.sum(early_rows, axis=0), late_sum[:bias_width]])
    head_bias_total = late_sum[bias_width:]
    wide_m, wide_v, wide_new = adam_update(
        wide_weight, wide_grad, wide_mean, wide_square, matrix_rate, matrix_decay
    )
    deep_m, deep_v, deep_new = adam_update(
        deep_weight, deep_grad, deep_mean, deep_square, matrix_rate, matrix_decay
    )
    first_m, first_v, first_new = adam_update(
        head_first, first_weight_grad, head_first_mean, head_first_square, matrix_rate, matrix_decay
    )
    second_m, second_v, second_new = adam_update(
        head_second,
        second_weight_grad,
        head_second_mean,
        head_second_square,
        matrix_rate,
        matrix_decay,
    )
    bias_m, bias_v, bias_new = adam_update(
        block_bias, block_bias_grad, block_bias_mean, block_bias_square, bias_rate, 0.0
    )
    hbias_m, hbias_v, hbias_new = adam_update(
        head_bias, head_bias_total, head_bias_mean, head_bias_square, bias_rate, 0.0
    )
    output = final.reshape(sequences * SEQ_LEN, MODEL_WIDTH).astype(jnp.bfloat16)
    input_flat = input_grad.reshape(sequences * SEQ_LEN, MODEL_WIDTH)
    return (
        output,
        input_flat,
        wide_grad,
        deep_grad,
        first_weight_grad,
        second_weight_grad,
        block_bias_grad,
        head_bias_total,
        wide_m,
        deep_m,
        first_m,
        second_m,
        bias_m,
        hbias_m,
        wide_v,
        deep_v,
        first_v,
        second_v,
        bias_v,
        hbias_v,
        wide_new,
        deep_new,
        first_new,
        second_new,
        bias_new,
        hbias_new,
    )


def solution(mesh):
    in_specs = (
        P(("fsdp", "rep"), None),
        P(("fsdp", "rep"), None),
        P(("fsdp", "rep")),
        P(("fsdp", "rep"), None),
        P(("fsdp", "rep"), None),
        P(None, "fsdp", None),
        P(None, "fsdp", None),
        P("fsdp", None),
        P("fsdp", None),
        P(),
        P(),
        P(None, "fsdp", None),
        P(None, "fsdp", None),
        P("fsdp", None),
        P("fsdp", None),
        P(),
        P(),
        P(None, "fsdp", None),
        P(None, "fsdp", None),
        P("fsdp", None),
        P("fsdp", None),
        P(),
        P(),
    )
    out_specs = (
        P(("fsdp", "rep"), None),
        P(("fsdp", "rep"), None),
        P(None, "fsdp", None),
        P(None, "fsdp", None),
        P("fsdp", None),
        P("fsdp", None),
        P(),
        P(),
        P(None, "fsdp", None),
        P(None, "fsdp", None),
        P("fsdp", None),
        P("fsdp", None),
        P(),
        P(),
        P(None, "fsdp", None),
        P(None, "fsdp", None),
        P("fsdp", None),
        P("fsdp", None),
        P(),
        P(),
        P(None, "fsdp", None),
        P(None, "fsdp", None),
        P("fsdp", None),
        P("fsdp", None),
        P(),
        P(),
    )
    return jax.shard_map(
        per_device, mesh=mesh, in_specs=in_specs, out_specs=out_specs, check_vma=False
    )
```

```python
from functools import partial
from typing import NamedTuple

import jax
import jax.numpy as jnp
from jax import lax
from jax.experimental import pallas as pl
from jax.experimental.pallas import tpu as pltpu
from jax.sharding import PartitionSpec as P

MESH = pl.DeviceIdType.MESH

MODEL_WIDTH = 1152
HEADS = 16
HEAD_DIM = 72
FF = 4608
PH = 2048
PZ = 768
SEQ_LEN = 448
STEP = 10


norm_epsilon = 1e-06
adam_epsilon = 1e-08
masked_score = -1e30
repa_weight = 0.5
matrix_rate = 0.05
bias_rate = 0.3
matrix_decay = 0.01


def normalize(values):
    centred = values - jnp.mean(values, axis=-1, keepdims=True)
    spread = jnp.mean(centred * centred, axis=-1, keepdims=True)
    return centred * lax.rsqrt(spread + norm_epsilon)


def modulate(values, offset, factor):
    return normalize(values) * (1.0 + factor) + offset


def gelu_tanh(values):
    return jax.nn.gelu(values, approximate=True)


def split_modulation(modulation):
    columns = modulation.shape[-1] // 6
    return [modulation[:, None, number * columns : (number + 1) * columns] for number in range(6)]


def outer_rows(left, right):
    flat_left = left.reshape(-1, left.shape[-1])
    flat_right = right.reshape(-1, right.shape[-1])
    return lax.dot_general(
        flat_left, flat_right, (((0,), (0,)), ((), ())), preferred_element_type=jnp.float32
    )


def swap_cores(values):
    count = lax.axis_size("fsdp")
    return lax.ppermute(values, "fsdp", [(place, place ^ 1) for place in range(count)])


class Term(NamedTuple):
    left: int
    right: int
    rows: int
    row_from: int
    columns: int
    column_from: int
    split: bool
    way: int
    start: int


def ring_place(chip, chips):
    return lax.div(chip, 2) + lax.rem(chip, 2) * (chips - 1 - 2 * lax.div(chip, 2))


def ring_chip(place, chips):
    upper = lax.div(place, (chips + 1) // 2)
    return 2 * place + upper * (2 * (chips - 1 - place) + 1 - 2 * place)


def reduce_body(terms, chips, lefts, rights, *refs):
    refs = list(refs)

    def take(count):
        taken = refs[:count]
        del refs[:count]
        return taken

    left_refs, right_refs = take(lefts), take(rights)
    outs = take(len(terms))
    own_left, own_right = take(lefts), take(rights)
    sib_left, sib_right = take(lefts), take(rights)
    landing, final = take(len(terms)), take(len(terms))
    split_at = [number for number, term in enumerate(terms) if term.split]
    give, got = take(len(split_at)), take(len(split_at))
    load_sem, swap_send, swap_recv, ring_send, ring_recv = take(5)
    give_send, got_recv, final_send, final_recv = take(4)

    device = lax.axis_index("fsdp")
    plane = lax.axis_index("rep")
    core, chip = lax.rem(device, 2), lax.div(device, 2)
    place = ring_place(chip, chips)
    sibling = {"fsdp": device + 1 - 2 * core}
    twin = {"rep": 1 - plane}
    ways = [
        {"fsdp": 2 * ring_chip(lax.rem(place + step, chips), chips) + core}
        for step in (1, chips - 1)
    ]

    barrier = pltpu.get_barrier_semaphore()
    partners = (ways[0], ways[1], sibling, twin)
    for partner in partners:
        pl.semaphore_signal(barrier, inc=1, device_id=partner, device_id_type=MESH)
    pl.semaphore_wait(barrier, len(partners))

    def remote(source, target, send_sem, recv_sem, partner):
        return pltpu.make_async_remote_copy(
            src_ref=source,
            dst_ref=target,
            send_sem=send_sem,
            recv_sem=recv_sem,
            device_id=partner,
            device_id_type=MESH,
        )

    loads, swaps = {}, {}
    for number in range(lefts):
        ref = left_refs[number]
        by_rows = len(ref.shape) == 4
        mine = ref.at[:, core] if by_rows else ref
        other = ref.at[:, 1 - core] if by_rows else ref
        loads["l", number] = pltpu.make_async_copy(mine, own_left[number], load_sem.at[number])
        swaps["l", number] = remote(
            other, sib_left[number], swap_send.at[number], swap_recv.at[number], sibling
        )
    for number in range(rights):
        ref, at = right_refs[number], lefts + number
        width = own_right[number].shape[1]
        if width == ref.shape[1]:
            mine = other = ref
        else:
            second = ref.shape[1] - width
            mine = ref.at[:, pl.ds(pl.multiple_of(core * second, 128), width)]
            other = ref.at[:, pl.ds(pl.multiple_of((1 - core) * second, 128), width)]
        loads["r", number] = pltpu.make_async_copy(mine, own_right[number], load_sem.at[at])
        swaps["r", number] = remote(
            other, sib_right[number], swap_send.at[at], swap_recv.at[at], sibling
        )
    first_use = {}
    for term in sorted(terms, key=lambda term: term.start - term.split):
        for key in (("l", term.left), ("r", term.right)):
            first_use.setdefault(key, term.start - term.split)
    for key in first_use:
        loads[key].start()
        swaps[key].start()
    for number, term in enumerate(terms):
        landing[number][0] = jnp.zeros(landing[number].shape[1:], jnp.bfloat16)

    def chunk(term, owner, part):
        rows = pl.ds(term.row_from, term.rows)
        from_column = term.column_from
        if term.split:
            from_column = pl.multiple_of(from_column + part * term.columns, 128)
        columns = pl.ds(from_column, term.columns)
        own = jnp.dot(
            own_left[term.left][owner, rows, :],
            own_right[term.right][:, columns],
            preferred_element_type=jnp.float32,
        )
        return own + jnp.dot(
            sib_left[term.left][owner, rows, :],
            sib_right[term.right][:, columns],
            preferred_element_type=jnp.float32,
        )

    def owner_at(term, hop):
        back = hop + 1 if term.way == 0 else 2 * chips - 1 - hop
        return ring_chip(lax.rem(place + 2 * chips - back, chips), chips)

    def give_copy(at, hop):
        return remote(
            give[at].at[hop],
            got[at].at[hop],
            give_send.at[at, hop],
            got_recv.at[at, hop],
            twin,
        )

    def ring_copy(number, hop):
        return remote(
            landing[number].at[hop],
            landing[number].at[hop + 1],
            ring_send.at[number, hop],
            ring_recv.at[number, hop + 1],
            ways[terms[number].way],
        )

    def arrival(number, hop):
        return remote(
            landing[number].at[hop],
            landing[number].at[hop],
            ring_send.at[number, hop],
            ring_recv.at[number, hop],
            ways[terms[number].way],
        )

    def final_copy(number):
        return remote(
            landing[number].at[chips - 1],
            final[number],
            final_send.at[number],
            final_recv.at[number],
            twin,
        )

    def step(clock, carry):
        for moment in sorted(set(first_use.values())):

            @pl.when(clock == moment)
            def _():
                for key, use in first_use.items():
                    if use == moment:
                        loads[key].wait()
                        swaps[key].wait_recv()

        for at, number in enumerate(split_at):
            term = terms[number]
            later = clock - term.start + 1

            @pl.when((later >= 0) & (later < chips))
            def _():
                give[at][later] = chunk(term, owner_at(term, later), 1 - plane).astype(
                    jnp.bfloat16
                )
                give_copy(at, later).start()

        for number, term in enumerate(terms):
            hop = clock - term.start

            @pl.when((hop >= 0) & (hop < chips))
            def _():
                total = chunk(term, owner_at(term, hop), plane)
                if term.split:
                    at = split_at.index(number)
                    give_copy(at, hop).wait_recv()
                    total = total + got[at][hop].astype(jnp.float32)

                @pl.when(hop > 0)
                def _():
                    arrival(number, hop).wait_recv()

                landing[number][hop] = (
                    total + landing[number][hop].astype(jnp.float32)
                ).astype(jnp.bfloat16)

                @pl.when(hop < chips - 1)
                def _():
                    ring_copy(number, hop).start()

                @pl.when(hop == chips - 1)
                def _():
                    final_copy(number).start()

        return carry

    lax.fori_loop(0, max(term.start for term in terms) + chips, step, 0)
    for number, term in enumerate(terms):
        final_copy(number).wait()
        mine = landing[number][chips - 1].astype(jnp.float32)
        other = final[number][...].astype(jnp.float32)
        if term.split:
            width = term.columns
            outs[number][:, pl.ds(pl.multiple_of(plane * width, 128), width)] = mine
            outs[number][:, pl.ds(pl.multiple_of((1 - plane) * width, 128), width)] = other
        else:
            outs[number][...] = mine + other

    def settle(hop, carry):
        for number in range(len(terms)):

            @pl.when(hop < chips - 1)
            def _():
                ring_copy(number, hop).wait_send()

        for at in range(len(split_at)):
            give_copy(at, hop).wait_send()
        return carry

    lax.fori_loop(0, chips, settle, 0)
    for key in first_use:
        swaps[key].wait_send()


def core_columns(columns):
    return -(-columns // 256) * 128


def reduce_terms(terms, lefts, rights, identity):
    chips = lefts[0].shape[0]
    whole = {term.right for term in terms if lefts[term.left].ndim == 4}
    left_parts = [
        (left.shape[0],) + left.shape[-2:] for left in lefts
    ]
    right_parts = [
        (right.shape[0], right.shape[1] if number in whole else core_columns(right.shape[1]))
        for number, right in enumerate(rights)
    ]

    def vmem(shape):
        return pltpu.VMEM(shape, jnp.bfloat16)

    splits = [term for term in terms if term.split]
    operands = len(lefts) + len(rights)
    scratch = (
        [vmem(shape) for shape in left_parts + right_parts] * 2
        + [vmem((chips, term.rows, term.columns)) for term in terms]
        + [vmem((term.rows, term.columns)) for term in terms]
        + [vmem((chips, term.rows, term.columns)) for term in splits] * 2
        + [pltpu.SemaphoreType.DMA((operands,))] * 3
        + [pltpu.SemaphoreType.DMA((len(terms), chips))] * 2
        + [pltpu.SemaphoreType.DMA((len(splits), chips))] * 2
        + [pltpu.SemaphoreType.DMA((len(terms),))] * 2
    )
    return pl.pallas_call(
        partial(reduce_body, terms, chips, len(lefts), len(rights)),
        out_shape=[
            jax.ShapeDtypeStruct((term.rows, term.columns * (1 + term.split)), jnp.float32)
            for term in terms
        ],
        in_specs=[pl.BlockSpec(memory_space=pl.ANY)] * operands,
        out_specs=[pl.BlockSpec(memory_space=pltpu.VMEM)] * len(terms),
        scratch_shapes=scratch,
        compiler_params=pltpu.CompilerParams(
            collective_id=identity, has_side_effects=True, vmem_limit_bytes=60 * 1024 * 1024
        ),
    )(*lefts, *rights)


class Piece(NamedTuple):
    source: int
    rows: int
    columns: int
    row_core: int
    row_plane: int
    column_from: int
    column_core: int
    column_plane: int
    split: bool
    long_way: int


def gather_body(pieces, chips, count, *refs):
    sources, outs = refs[:count], refs[count : 2 * count]
    ring_send, ring_recv, pass_send, pass_recv, twin_send, twin_recv, own_sem = refs[2 * count :]
    device = lax.axis_index("fsdp")
    plane = lax.axis_index("rep")
    core, chip = lax.rem(device, 2), lax.div(device, 2)
    place = ring_place(chip, chips)
    sibling = {"fsdp": device + 1 - 2 * core}
    twin = {"rep": 1 - plane}

    def chip_back(way, hops):
        back = hops if way == 0 else chips - hops
        return ring_chip(lax.rem(place + chips - back, chips), chips)

    ways = [{"fsdp": 2 * chip_back(1 - way, 1) + core} for way in range(2)]

    barrier = pltpu.get_barrier_semaphore()
    partners = (ways[0], ways[1], sibling, twin)
    for partner in partners:
        pl.semaphore_signal(barrier, inc=1, device_id=partner, device_id_type=MESH)
    pl.semaphore_wait(barrier, len(partners))

    keep = [
        pltpu.make_async_copy(
            sources[number],
            outs[number].at[
                pl.ds(
                    pl.multiple_of(chip * sources[number].shape[0], 16), sources[number].shape[0]
                ),
                :,
            ],
            own_sem.at[number],
        )
        for number in range(count)
    ]
    for copy in keep:
        copy.start()

    def window(piece, ref, base, of_core, of_plane):
        row = base + of_core * piece.row_core + of_plane * piece.row_plane
        column = (
            piece.column_from + of_core * piece.column_core + of_plane * piece.column_plane
        )
        return ref.at[
            pl.ds(pl.multiple_of(row, 16), piece.rows),
            pl.ds(pl.multiple_of(column, 128), piece.columns),
        ]

    def landed(number, owner, of_core, of_plane):
        piece = pieces[number]
        height = sources[piece.source].shape[0]
        return window(piece, outs[piece.source], owner * height, of_core, of_plane)

    def remote(source, target, sems, index, partner):
        return pltpu.make_async_remote_copy(
            src_ref=source,
            dst_ref=target,
            send_sem=sems[0].at[index],
            recv_sem=sems[1].at[index],
            device_id=partner,
            device_id_type=MESH,
        )

    hops = [
        [chips // 2 if piece.long_way == way else (chips - 1) // 2 for way in range(2)]
        for piece in pieces
    ]
    splits = [number for number, piece in enumerate(pieces) if piece.split]
    sent = []

    def send(copy):
        copy.start()
        sent.append(copy)

    for number, piece in enumerate(pieces):
        for way in range(2):
            send(
                remote(
                    window(piece, sources[piece.source], 0, core, plane),
                    landed(number, chip, core, plane),
                    (ring_send, ring_recv),
                    (number, way, 0),
                    ways[way],
                )
            )

    def ring_arrivals(hop):
        for number, piece in enumerate(pieces):
            for way in range(2):
                if hop > hops[number][way]:
                    continue
                block = landed(number, chip_back(way, hop), core, plane)
                remote(
                    block, block, (ring_send, ring_recv), (number, way, hop - 1), ways[way]
                ).wait_recv()
                if hop < hops[number][way]:
                    send(
                        remote(
                            block, block, (ring_send, ring_recv), (number, way, hop), ways[way]
                        )
                    )
                send(
                    remote(
                        block, block, (pass_send, pass_recv), (number, way, hop - 1), sibling
                    )
                )
                if piece.split:
                    at = splits.index(number)
                    send(
                        remote(block, block, (twin_send, twin_recv), (at, way, hop - 1), twin)
                    )

    def twin_arrivals(hop):
        for at, number in enumerate(splits):
            for way in range(2):
                if hop > hops[number][way]:
                    continue
                block = landed(number, chip_back(way, hop), core, 1 - plane)
                remote(
                    block, block, (twin_send, twin_recv), (at, way, hop - 1), twin
                ).wait_recv()
                send(
                    remote(
                        block,
                        block,
                        (pass_send, pass_recv),
                        (len(pieces) + at, way, hop - 1),
                        sibling,
                    )
                )

    for hop in range(1, chips // 2 + 1):
        ring_arrivals(hop)
        if hop > 1:
            twin_arrivals(hop - 1)
    twin_arrivals(chips // 2)
    for number in range(len(pieces) + len(splits)):
        at = number if number < len(pieces) else splits[number - len(pieces)]
        of_plane = plane if number < len(pieces) else 1 - plane
        for way in range(2):
            for hop in range(1, hops[at][way] + 1):
                block = landed(at, chip_back(way, hop), 1 - core, of_plane)
                remote(
                    block, block, (pass_send, pass_recv), (number, way, hop - 1), sibling
                ).wait_recv()
    for copy in sent:
        copy.wait_send()
    for copy in keep:
        copy.wait()


def gather_pieces(pieces, sources, identity):
    chips = lax.axis_size("fsdp") // 2
    splits = sum(piece.split for piece in pieces)
    hops = chips // 2

    def sems(number):
        return [pltpu.SemaphoreType.DMA((number, 2, hops))] * 2

    return pl.pallas_call(
        partial(gather_body, pieces, chips, len(sources)),
        out_shape=[
            jax.ShapeDtypeStruct((chips * source.shape[0], source.shape[1]), source.dtype)
            for source in sources
        ],
        in_specs=[pl.BlockSpec(memory_space=pl.ANY)] * len(sources),
        out_specs=[pl.BlockSpec(memory_space=pl.ANY)] * len(sources),
        scratch_shapes=sems(len(pieces))
        + sems(len(pieces) + splits)
        + sems(splits)
        + [pltpu.SemaphoreType.DMA((len(sources),))],
        compiler_params=pltpu.CompilerParams(collective_id=identity, has_side_effects=True),
    )(*sources)


def chip_rows(shard):
    other = swap_cores(shard)
    core = lax.axis_index("fsdp") % 2
    return jnp.where(
        core == 0, jnp.concatenate([shard, other]), jnp.concatenate([other, shard])
    )


def by_chip(values):
    chips = lax.axis_size("fsdp") // 2
    return values.T.reshape(chips, -1, values.shape[0])


def by_device(values):
    chips = lax.axis_size("fsdp") // 2
    return values.T.reshape(chips, 2, -1, values.shape[0])


def join_cores(pieces):
    core = lax.axis_index("fsdp") % 2
    both = jnp.concatenate([piece for piece, _ in pieces], axis=1)
    rows = both.shape[0] // 2
    mine = lax.dynamic_slice_in_dim(both, core * rows, rows, axis=0)
    sent = lax.dynamic_slice_in_dim(both, (1 - core) * rows, rows, axis=0)
    other = swap_cores(sent)
    low = jnp.where(core == 0, mine, other)
    high = jnp.where(core == 0, other, mine)
    joined, at = [], 0
    for piece, columns in pieces:
        end = at + piece.shape[1]
        twice = 2 * piece.shape[1] - columns
        joined += [low[:, at:end], high[:, at + twice : end]]
        at = end
    return jnp.concatenate(joined, axis=1)


def plain_sum(left, right):
    total = lax.psum_scatter(
        outer_rows(left, right).astype(jnp.bfloat16), "fsdp", scatter_dimension=0, tiled=True
    )
    return lax.psum(total.astype(jnp.float32), "rep")


def kernels_fit(rows):
    return 2 * rows % 16 == 0 and lax.axis_size("rep") == 2


def sum_block_grads(
    normed, triple_grad, attended, branch_grad, mixed, pre_grad, active, feed_grad, identity
):
    rows = MODEL_WIDTH // lax.axis_size("fsdp")
    if not kernels_fit(rows):
        wide = jnp.concatenate(
            [
                plain_sum(normed, triple_grad),
                plain_sum(attended, branch_grad),
                plain_sum(mixed, pre_grad),
            ],
            axis=1,
        )
        return (wide, plain_sum(active, feed_grad))
    triple_half = core_columns(triple_grad.shape[1])
    branch_half = core_columns(branch_grad.shape[1])
    pre_half = core_columns(pre_grad.shape[1])
    plain_part = 8 * 128
    pre_part = (pre_half - plain_part) // 2
    deep_rows = active.shape[1] // lax.axis_size("fsdp") // 2
    terms = (
        Term(3, 3, deep_rows, 0, MODEL_WIDTH, 0, False, 0, 0),
        Term(3, 3, deep_rows, deep_rows, MODEL_WIDTH, 0, False, 1, 0),
        Term(2, 2, 2 * rows, 0, pre_part, plain_part, True, 1, 1),
        Term(0, 0, 2 * rows, 0, triple_half // 2, 0, True, 0, 2),
        Term(2, 2, 2 * rows, 0, plain_part, 0, False, 1, 2),
        Term(1, 1, 2 * rows, 0, branch_half, 0, False, 0, 3),
    )
    deep_low, deep_high, pre_late, triple, pre_early, branch = reduce_terms(
        terms,
        [by_chip(normed), by_chip(attended), by_chip(mixed), by_device(active)],
        [triple_grad, branch_grad, pre_grad, feed_grad],
        identity,
    )
    wide = join_cores(
        [
            (triple, triple_grad.shape[1]),
            (branch, branch_grad.shape[1]),
            (jnp.concatenate([pre_early, pre_late], axis=1), pre_grad.shape[1]),
        ]
    )
    return (wide, jnp.concatenate([deep_low, deep_high], axis=0))


def sum_head_grads(tapped, first_grad, first, second_grad, second, projected_grad, identity):
    count = lax.axis_size("fsdp")
    rows, head_rows = tapped.shape[1] // count, first.shape[1] // count
    if not kernels_fit(rows):
        return (
            plain_sum(tapped, first_grad),
            jnp.concatenate(
                [plain_sum(first, second_grad), plain_sum(second, projected_grad)], axis=1
            ),
        )
    half, last = first_grad.shape[1] // 2, projected_grad.shape[1] // 2
    terms = (
        Term(1, 1, 2 * head_rows, 0, half // 2, 0, True, 1, 1),
        Term(0, 0, 2 * rows, 0, half, 0, False, 0, 1),
        Term(2, 2, 2 * head_rows, 0, last - 128, 128, False, 1, 1),
        Term(2, 2, 2 * head_rows, 0, 128, 0, False, 0, 1),
    )
    second_out, first_out, third_late, third_early = reduce_terms(
        terms,
        [by_chip(tapped), by_chip(first), by_chip(second)],
        [first_grad, second_grad, projected_grad],
        identity,
    )
    return (
        join_cores([(first_out, first_grad.shape[1])]),
        join_cores(
            [
                (second_out, second_grad.shape[1]),
                (jnp.concatenate([third_early, third_late], axis=1), projected_grad.shape[1]),
            ]
        ),
    )


def pack_body(*refs):
    out, at = refs[-1], 0
    for ref in refs[:-1]:
        width = ref.shape[1]
        out[:, at : at + width] = ref[...].astype(jnp.float32)
        at += width


def pack_rows(pieces):
    rows = pieces[0].shape[0]
    width = sum(piece.shape[1] for piece in pieces)
    return pl.pallas_call(
        pack_body, out_shape=jax.ShapeDtypeStruct((rows, width), jnp.float32)
    )(*pieces)


def gathered_terms(row):
    return lax.all_gather(row, ("fsdp", "rep"), axis=0, tiled=True)


def fetch_block(wide_shard, deep_shard, identity):
    rest = wide_shard[:, 6 * MODEL_WIDTH :].astype(jnp.bfloat16)
    low = deep_shard.astype(jnp.bfloat16)
    rows = rest.shape[0]
    if identity is not None and kernels_fit(rows):
        unit = MODEL_WIDTH
        deep_rows = low.shape[0] // 2
        pieces = (
            Piece(0, 2 * rows, unit, 0, 0, 2 * unit, 4 * unit, unit, True, 0),
            Piece(1, deep_rows, unit, 2 * deep_rows, deep_rows, 0, 0, 0, True, 1),
            Piece(0, 2 * rows, unit, 0, 0, 0, 4 * unit, 0, False, 0),
            Piece(0, 2 * rows, unit, 0, 0, unit, 4 * unit, 0, False, 1),
        )
        whole, deep = gather_pieces(pieces, [chip_rows(rest), chip_rows(low)], identity)
    else:
        whole = lax.all_gather(rest, "fsdp", axis=0, tiled=True)
        deep = lax.all_gather(low, "fsdp", axis=0, tiled=True)
    split = (
        whole[:, : 3 * MODEL_WIDTH],
        whole[:, 3 * MODEL_WIDTH : 4 * MODEL_WIDTH],
        whole[:, 4 * MODEL_WIDTH :],
    )
    return (split, deep)


def plane_modulation(silu_low, wide_weight, block_bias):
    count = lax.axis_size("fsdp")
    sequences = silu_low.shape[0]
    rows = wide_weight.shape[1]
    device = lax.axis_index("fsdp")
    spread = jnp.broadcast_to(
        silu_low.reshape(1, sequences, count, rows).transpose(2, 0, 1, 3)[:, 0],
        (count, sequences, rows),
    )
    met = lax.all_to_all(spread, "fsdp", 0, 0, tiled=True)
    met = met.reshape(count * sequences, rows)
    partial = [
        jnp.dot(
            met,
            wide_weight[block, :, : 6 * MODEL_WIDTH].astype(jnp.bfloat16),
            preferred_element_type=jnp.float32,
        )
        for block in range(2)
    ]
    partial = jnp.stack(partial, axis=1).reshape(count, sequences, 2, 6 * MODEL_WIDTH)
    back = lax.all_to_all(partial, "fsdp", 0, 0, tiled=True)
    total = jnp.sum(back, axis=0)
    return [total[:, block] + block_bias[block, : 6 * MODEL_WIDTH] for block in range(2)]


HEAD_WINDOW = 256


def head_window(head, width):
    first = head * HEAD_DIM
    at = min(first // 128 * 128, width - HEAD_WINDOW)
    lane = lax.broadcasted_iota(jnp.int32, (1, HEAD_WINDOW), 1)
    return at, (lane >= first - at) & (lane < first - at + HEAD_DIM)


def only(mine, values):
    return jnp.where(mine, values, jnp.zeros_like(values))


def against(left, right):
    return lax.dot_general(
        left, right, (((1,), (1,)), ((), ())), preferred_element_type=jnp.float32
    )


def attend_body(lengths_ref, triple_ref, attended_ref, log_ref, total_ref):
    tokens, width = attended_ref.shape
    length = lengths_ref[pl.program_id(0)]
    seen = lax.broadcasted_iota(jnp.int32, (tokens, 1), 0) < length
    total_ref[...] = jnp.zeros_like(total_ref)
    for head in range(HEADS):
        at, mine = head_window(head, width)
        window = pl.ds(at, HEAD_WINDOW)
        keys = only(mine, triple_ref[:, pl.ds(width + at, HEAD_WINDOW)])
        values = only(mine, triple_ref[:, pl.ds(2 * width + at, HEAD_WINDOW)])
        scores = against(keys, triple_ref[:, window]) * HEAD_DIM ** (-0.5)
        scores = jnp.where(seen, scores, masked_score)
        largest = jnp.max(scores, axis=0, keepdims=True)
        expanded = jnp.exp(scores - largest)
        sums = jnp.sum(expanded, axis=0, keepdims=True)
        weights = (expanded * (1.0 / sums)).astype(jnp.bfloat16)
        total_ref[:, window] += lax.dot_general(
            weights, values, (((0,), (0,)), ((), ())), preferred_element_type=jnp.float32
        )
        log_ref[head : head + 1, :] = largest + jnp.log(sums)
    attended_ref[...] = total_ref[...].astype(jnp.bfloat16)


def attention_forward(triple, lengths):
    sequences, tokens, columns = triple.shape
    width = columns // 3
    return pl.pallas_call(
        attend_body,
        grid=(sequences,),
        out_shape=[
            jax.ShapeDtypeStruct((sequences, tokens, width), jnp.bfloat16),
            jax.ShapeDtypeStruct((sequences, HEADS, tokens), jnp.float32),
        ],
        in_specs=[
            pl.BlockSpec(memory_space=pltpu.SMEM),
            pl.BlockSpec((None, tokens, columns), lambda number: (number, 0, 0)),
        ],
        out_specs=[
            pl.BlockSpec((None, tokens, width), lambda number: (number, 0, 0)),
            pl.BlockSpec((None, HEADS, tokens), lambda number: (number, 0, 0)),
        ],
        scratch_shapes=[pltpu.VMEM((tokens, width), jnp.float32)],
        compiler_params=pltpu.CompilerParams(vmem_limit_bytes=48 * 1024 * 1024),
    )(lengths, triple)


def attend_back_body(lengths_ref, triple_ref, log_ref, upstream_ref, grad_ref, total_ref):
    tokens, width = upstream_ref.shape
    length = lengths_ref[pl.program_id(0)]
    factor = HEAD_DIM ** (-0.5)
    seen = lax.broadcasted_iota(jnp.int32, (tokens, 1), 0) < length
    total_ref[...] = jnp.zeros_like(total_ref)
    for head in range(HEADS):
        at, mine = head_window(head, width)
        query_at, key_at, value_at = (
            pl.ds(group * width + at, HEAD_WINDOW) for group in range(3)
        )
        queries = only(mine, triple_ref[:, query_at])
        keys = only(mine, triple_ref[:, key_at])
        values = only(mine, triple_ref[:, value_at])
        upstream = only(mine, upstream_ref[:, pl.ds(at, HEAD_WINDOW)])
        scores = against(keys, queries) * factor
        chances = jnp.where(seen, jnp.exp(scores - log_ref[head : head + 1, :]), 0.0)
        chance_grad = against(values, upstream)
        centre = jnp.sum(chance_grad * chances, axis=0, keepdims=True)
        score_grad = (chances * (chance_grad - centre)).astype(jnp.bfloat16)
        total_ref[:, value_at] += jnp.dot(
            chances.astype(jnp.bfloat16), upstream, preferred_element_type=jnp.float32
        )
        total_ref[:, key_at] += factor * jnp.dot(
            score_grad, queries, preferred_element_type=jnp.float32
        )
        total_ref[:, query_at] += factor * lax.dot_general(
            score_grad, keys, (((0,), (0,)), ((), ())), preferred_element_type=jnp.float32
        )
    grad_ref[...] = total_ref[...].astype(jnp.bfloat16)


def attention_backward(triple, logs, upstream, lengths):
    sequences, tokens, columns = triple.shape

    def spec(width):
        return pl.BlockSpec((None, tokens, width), lambda number: (number, 0, 0))

    return pl.pallas_call(
        attend_back_body,
        grid=(sequences,),
        out_shape=jax.ShapeDtypeStruct((sequences, tokens, columns), jnp.bfloat16),
        in_specs=[
            pl.BlockSpec(memory_space=pltpu.SMEM),
            spec(columns),
            pl.BlockSpec((None, HEADS, tokens), lambda number: (number, 0, 0)),
            spec(columns // 3),
        ],
        out_specs=spec(columns),
        scratch_shapes=[pltpu.VMEM((tokens, columns), jnp.float32)],
        compiler_params=pltpu.CompilerParams(vmem_limit_bytes=48 * 1024 * 1024),
    )(lengths, triple, logs, upstream)


def block_forward(hidden, modulation, wide_matrix, deep_matrix, bias, lengths):
    sequences = hidden.shape[0]
    offset_first, factor_first, gate_first, offset_second, factor_second, gate_second = (
        split_modulation(modulation)
    )
    normed_low = modulate(hidden, offset_first, factor_first).astype(jnp.bfloat16)
    triple_bias = jnp.concatenate(
        [
            bias[6 * MODEL_WIDTH : 7 * MODEL_WIDTH],
            jnp.zeros((MODEL_WIDTH,), jnp.float32),
            bias[7 * MODEL_WIDTH : 8 * MODEL_WIDTH],
        ]
    )
    triple = (
        jnp.dot(
            normed_low,
            wide_matrix[0],
            preferred_element_type=jnp.float32,
        )
        + triple_bias
    ).astype(jnp.bfloat16)
    attended_low, log_total = attention_forward(triple, lengths)
    branch = (
        jnp.dot(
            attended_low,
            wide_matrix[1],
            preferred_element_type=jnp.float32,
        )
        + bias[8 * MODEL_WIDTH : 9 * MODEL_WIDTH]
    )
    middle = hidden + gate_first * branch
    mixed_low = modulate(middle, offset_second, factor_second).astype(jnp.bfloat16)
    pre_active = (
        jnp.dot(mixed_low, wide_matrix[2], preferred_element_type=jnp.float32)
        + bias[9 * MODEL_WIDTH : 9 * MODEL_WIDTH + FF]
    )
    active_low = gelu_tanh(pre_active).astype(jnp.bfloat16)
    feed_out = (
        jnp.dot(active_low, deep_matrix, preferred_element_type=jnp.float32)
        + bias[9 * MODEL_WIDTH + FF :]
    )
    result = middle + gate_second * feed_out
    saved = (
        hidden,
        modulation,
        normed_low,
        triple,
        log_total,
        attended_low,
        branch,
        middle,
        mixed_low,
        pre_active,
        active_low,
        feed_out,
    )
    return (result, saved)


def block_backward(upstream, saved, wide_matrix, deep_matrix, lengths):
    (
        hidden,
        modulation,
        normed_low,
        triple,
        log_total,
        attended_low,
        branch,
        middle,
        mixed_low,
        pre_active,
        active_low,
        feed_out,
    ) = saved
    sequences = hidden.shape[0]
    offset_first, factor_first, gate_first, offset_second, factor_second, gate_second = (
        split_modulation(modulation)
    )
    feedforward_gradient = (upstream * gate_second).astype(jnp.bfloat16)
    gate_second_grad = jnp.sum(upstream * feed_out, axis=1)
    activation_gradient = jnp.einsum(
        "xjn,mn->xjm", feedforward_gradient, deep_matrix, preferred_element_type=jnp.float32
    )
    preactivation_gradient = jax.vjp(gelu_tanh, pre_active)[1](activation_gradient)[0].astype(
        jnp.bfloat16
    )
    mixed_grad = jnp.einsum(
        "qvm,am->qva",
        preactivation_gradient,
        wide_matrix[2],
        preferred_element_type=jnp.float32,
    )
    second_back = jax.vjp(modulate, middle, offset_second, factor_second)[1]
    middle_part, offset_second_grad, factor_second_grad = second_back(mixed_grad)
    middle_grad = upstream + middle_part
    gate_first_grad = jnp.sum(middle_grad * branch, axis=1)
    branch_gradient = (middle_grad * gate_first).astype(jnp.bfloat16)
    attended_grad = jnp.einsum(
        "tbr,ar->tba",
        branch_gradient,
        wide_matrix[1],
        preferred_element_type=jnp.float32,
    ).astype(jnp.bfloat16)
    triple_gradient = attention_backward(triple, log_total, attended_grad, lengths)
    normed_grad = jnp.einsum(
        "tbr,ar->tba",
        triple_gradient,
        wide_matrix[0],
        preferred_element_type=jnp.float32,
    )
    first_back = jax.vjp(modulate, hidden, offset_first, factor_first)[1]
    hidden_part, offset_first_grad, factor_first_grad = first_back(normed_grad)
    hidden_grad = middle_grad + hidden_part
    def column_sum(values):
        return jnp.sum(values, axis=(0, 1), dtype=jnp.float32)[None]

    triple_sum = column_sum(triple_gradient)
    row_pieces = [
        piece.reshape(1, -1).astype(jnp.bfloat16)
        for piece in (
            offset_first_grad,
            factor_first_grad,
            gate_first_grad,
            offset_second_grad,
            factor_second_grad,
            gate_second_grad,
        )
    ] + [
        triple_sum[:, :MODEL_WIDTH],
        triple_sum[:, 2 * MODEL_WIDTH :],
        column_sum(branch_gradient),
        column_sum(preactivation_gradient),
        column_sum(feedforward_gradient),
    ]

    def flat(values):
        return values.reshape(-1, values.shape[-1])

    factors = [
        flat(values)
        for values in (
            normed_low,
            triple_gradient,
            attended_low,
            branch_gradient,
            mixed_low,
            preactivation_gradient,
            active_low,
            feedforward_gradient,
        )
    ]
    return (hidden_grad, row_pieces, factors)


def adam_update(weight, grad, first, second, rate, decay):
    first_new = 0.9 * first + 0.1 * grad
    second_new = 0.999 * second + 0.001 * grad * grad
    first_hat = first_new / (1.0 - 0.9**STEP)
    second_hat = second_new / (1.0 - 0.999**STEP)
    updated = weight - rate * (first_hat / (jnp.sqrt(second_hat) + adam_epsilon) + decay * weight)
    return (first_new, second_new, updated)


def per_device(
    tokens,
    condition,
    lengths,
    targets,
    cotangent,
    wide_weight,
    deep_weight,
    head_first,
    head_second,
    block_bias,
    head_bias,
    wide_mean,
    deep_mean,
    head_first_mean,
    head_second_mean,
    block_bias_mean,
    head_bias_mean,
    wide_square,
    deep_square,
    head_first_square,
    head_second_square,
    block_bias_square,
    head_bias_square,
):
    sequences = condition.shape[0]
    hidden = tokens.astype(jnp.float32).reshape(sequences, SEQ_LEN, MODEL_WIDTH)
    silu_low = jax.nn.silu(condition.astype(jnp.float32)).astype(jnp.bfloat16)
    visible = jnp.arange(SEQ_LEN, dtype=jnp.int32)[None, :] < lengths[:, None]
    wide_early, deep_early = fetch_block(wide_weight[0], deep_weight[0], 3)
    modulation_early, modulation_late = plane_modulation(silu_low, wide_weight, block_bias)
    tapped, saved_early = block_forward(
        hidden, modulation_early, wide_early, deep_early, block_bias[0], lengths
    )
    wide_late, deep_late = fetch_block(wide_weight[1], deep_weight[1], None)
    first_matrix, second_w = (
        lax.all_gather(head_first.astype(jnp.bfloat16), "fsdp", axis=0, tiled=True),
        lax.all_gather(head_second.astype(jnp.bfloat16), "fsdp", axis=0, tiled=True),
    )
    final, saved_late = block_forward(
        tapped, modulation_late, wide_late, deep_late, block_bias[1], lengths
    )
    raw_targets = targets.astype(jnp.float32).reshape(sequences, SEQ_LEN, PZ)
    target_unit = raw_targets * lax.rsqrt(
        jnp.sum(raw_targets * raw_targets, axis=-1, keepdims=True) + norm_epsilon
    )

    def alignment(values):
        unit = values * lax.rsqrt(jnp.sum(values * values, axis=-1, keepdims=True) + norm_epsilon)
        return jnp.sum(unit * target_unit, axis=-1)

    upstream = cotangent.astype(jnp.float32).reshape(sequences, SEQ_LEN, MODEL_WIDTH)
    late_input_grad, late_row, late_factors = block_backward(
        upstream, saved_late, wide_late, deep_late, lengths
    )
    tapped_low, late_input_grad = lax.optimization_barrier(
        (tapped.astype(jnp.bfloat16), late_input_grad)
    )
    first_pre = (
        jnp.dot(tapped_low, first_matrix, preferred_element_type=jnp.float32) + head_bias[:PH]
    )
    first_low = jax.nn.silu(first_pre).astype(jnp.bfloat16)
    second_pre = (
        jnp.dot(first_low, second_w[:, :PH], preferred_element_type=jnp.float32)
        + head_bias[PH : 2 * PH]
    )
    second_low = jax.nn.silu(second_pre).astype(jnp.bfloat16)
    projected = (
        jnp.dot(second_low, second_w[:, PH:], preferred_element_type=jnp.float32)
        + head_bias[2 * PH :]
    )
    projected_grad = jax.vjp(alignment, projected)[1](-repa_weight * visible.astype(jnp.float32))[
        0
    ].astype(jnp.bfloat16)
    second_act_grad = jnp.einsum(
        "slz,hz->slh", projected_grad, second_w[:, PH:], preferred_element_type=jnp.float32
    )
    second_grad = jax.vjp(jax.nn.silu, second_pre)[1](second_act_grad)[0].astype(jnp.bfloat16)
    first_act_grad = jnp.einsum(
        "slh,gh->slg", second_grad, second_w[:, :PH], preferred_element_type=jnp.float32
    )
    first_gradient = jax.vjp(jax.nn.silu, first_pre)[1](first_act_grad)[0].astype(jnp.bfloat16)
    tapped_gradient = jnp.einsum(
        "ejk,rk->ejr", first_gradient, first_matrix, preferred_element_type=jnp.float32
    )

    def column_sum(values):
        return jnp.sum(values, axis=(0, 1), dtype=jnp.float32)[None]

    def flat(values):
        return values.reshape(-1, values.shape[-1])

    input_grad, early_row, early_factors = block_backward(
        late_input_grad + tapped_gradient, saved_early, wide_early, deep_early, lengths
    )
    row = pack_rows(
        [silu_low]
        + early_row
        + late_row
        + [column_sum(first_gradient), column_sum(second_grad), column_sum(projected_grad)]
    )
    row, early_factors, late_factors, first_gradient = lax.optimization_barrier(
        (row, early_factors, late_factors, first_gradient)
    )
    rows = gathered_terms(row)
    late_grads = sum_block_grads(*late_factors, 0)
    head_factors = (
        flat(tapped_low),
        flat(first_gradient),
        flat(first_low),
        flat(second_grad),
        flat(second_low),
        flat(projected_grad),
    )
    late_grads, head_factors = lax.optimization_barrier((late_grads, head_factors))
    first_weight_grad, second_weight_grad = sum_head_grads(*head_factors, 1)
    rows, early_factors, first_weight_grad = lax.optimization_barrier(
        (rows, early_factors, first_weight_grad)
    )
    early_grads = sum_block_grads(*early_factors, 2)
    own_silu = lax.dynamic_slice_in_dim(
        rows,
        lax.axis_index("fsdp") * wide_weight.shape[1],
        wide_weight.shape[1],
        axis=1,
    ).astype(jnp.bfloat16)
    bias_width = block_bias.shape[1]
    early_rows = rows[:, MODEL_WIDTH : MODEL_WIDTH + bias_width]
    late_rows = rows[:, MODEL_WIDTH + bias_width : MODEL_WIDTH + 2 * bias_width]

    def modulation_weight_grad(rows):
        return lax.dot_general(
            own_silu,
            rows[:, : 6 * MODEL_WIDTH].astype(jnp.bfloat16),
            (((0,), (0,)), ((), ())),
            preferred_element_type=jnp.float32,
        )

    wide_grad = jnp.stack(
        [
            jnp.concatenate(
                [modulation_weight_grad(early_rows), early_grads[0]],
                axis=1,
            ),
            jnp.concatenate(
                [modulation_weight_grad(late_rows), late_grads[0]],
                axis=1,
            ),
        ]
    )
    deep_grad = jnp.stack([early_grads[1], late_grads[1]])
    row_sum = jnp.sum(rows, axis=0)[MODEL_WIDTH:]
    block_bias_grad = row_sum[: 2 * bias_width].reshape(2, bias_width)
    head_bias_total = row_sum[2 * bias_width :]
    wide_m, wide_v, wide_new = adam_update(
        wide_weight, wide_grad, wide_mean, wide_square, matrix_rate, matrix_decay
    )
    deep_m, deep_v, deep_new = adam_update(
        deep_weight, deep_grad, deep_mean, deep_square, matrix_rate, matrix_decay
    )
    first_m, first_v, first_new = adam_update(
        head_first, first_weight_grad, head_first_mean, head_first_square, matrix_rate, matrix_decay
    )
    second_m, second_v, second_new = adam_update(
        head_second,
        second_weight_grad,
        head_second_mean,
        head_second_square,
        matrix_rate,
        matrix_decay,
    )
    bias_m, bias_v, bias_new = adam_update(
        block_bias, block_bias_grad, block_bias_mean, block_bias_square, bias_rate, 0.0
    )
    hbias_m, hbias_v, hbias_new = adam_update(
        head_bias, head_bias_total, head_bias_mean, head_bias_square, bias_rate, 0.0
    )
    output = final.reshape(sequences * SEQ_LEN, MODEL_WIDTH).astype(jnp.bfloat16)
    input_flat = input_grad.reshape(sequences * SEQ_LEN, MODEL_WIDTH)
    return (
        output,
        input_flat,
        wide_grad,
        deep_grad,
        first_weight_grad,
        second_weight_grad,
        block_bias_grad,
        head_bias_total,
        wide_m,
        deep_m,
        first_m,
        second_m,
        bias_m,
        hbias_m,
        wide_v,
        deep_v,
        first_v,
        second_v,
        bias_v,
        hbias_v,
        wide_new,
        deep_new,
        first_new,
        second_new,
        bias_new,
        hbias_new,
    )


def solution(mesh):
    in_specs = (
        P(("fsdp", "rep"), None),
        P(("fsdp", "rep"), None),
        P(("fsdp", "rep")),
        P(("fsdp", "rep"), None),
        P(("fsdp", "rep"), None),
        P(None, "fsdp", None),
        P(None, "fsdp", None),
        P("fsdp", None),
        P("fsdp", None),
        P(),
        P(),
        P(None, "fsdp", None),
        P(None, "fsdp", None),
        P("fsdp", None),
        P("fsdp", None),
        P(),
        P(),
        P(None, "fsdp", None),
        P(None, "fsdp", None),
        P("fsdp", None),
        P("fsdp", None),
        P(),
        P(),
    )
    out_specs = (
        P(("fsdp", "rep"), None),
        P(("fsdp", "rep"), None),
        P(None, "fsdp", None),
        P(None, "fsdp", None),
        P("fsdp", None),
        P("fsdp", None),
        P(),
        P(),
        P(None, "fsdp", None),
        P(None, "fsdp", None),
        P("fsdp", None),
        P("fsdp", None),
        P(),
        P(),
        P(None, "fsdp", None),
        P(None, "fsdp", None),
        P("fsdp", None),
        P("fsdp", None),
        P(),
        P(),
        P(None, "fsdp", None),
        P(None, "fsdp", None),
        P("fsdp", None),
        P("fsdp", None),
        P(),
        P(),
    )
    return jax.shard_map(
        per_device, mesh=mesh, in_specs=in_specs, out_specs=out_specs, check_vma=False
    )
```

```python
from functools import partial
from typing import NamedTuple

import jax
import jax.numpy as jnp
from jax import lax
from jax.experimental import pallas as pl
from jax.experimental.pallas import tpu as pltpu
from jax.sharding import PartitionSpec as P

MESH = pl.DeviceIdType.MESH
GIVE_SLOTS = 3

MODEL_WIDTH = 1152
HEADS = 16
HEAD_DIM = 72
FF = 4608
PH = 2048
PZ = 768
SEQ_LEN = 448
STEP = 10


norm_epsilon = 1e-06
adam_epsilon = 1e-08
masked_score = -1e30
repa_weight = 0.5
matrix_rate = 0.05
bias_rate = 0.3
matrix_decay = 0.01


def normalize(values):
    centred = values - jnp.mean(values, axis=-1, keepdims=True)
    spread = jnp.mean(centred * centred, axis=-1, keepdims=True)
    return centred * lax.rsqrt(spread + norm_epsilon)


def modulate(values, offset, factor):
    return normalize(values) * (1.0 + factor) + offset


def gelu_tanh(values):
    return jax.nn.gelu(values, approximate=True)


def split_modulation(modulation):
    columns = modulation.shape[-1] // 6
    return [modulation[:, None, number * columns : (number + 1) * columns] for number in range(6)]


def outer_rows(left, right):
    flat_left = left.reshape(-1, left.shape[-1])
    flat_right = right.reshape(-1, right.shape[-1])
    return lax.dot_general(
        flat_left, flat_right, (((0,), (0,)), ((), ())), preferred_element_type=jnp.float32
    )


def swap_cores(values):
    count = lax.axis_size("fsdp")
    return lax.ppermute(values, "fsdp", [(place, place ^ 1) for place in range(count)])


class Term(NamedTuple):
    left: int
    right: int
    rows: int
    row_from: int
    columns: int
    column_from: int
    split: bool
    way: int
    start: int
    out: int
    out_row: int
    out_column: int


def ring_place(chip, chips):
    return lax.div(chip, 2) + lax.rem(chip, 2) * (chips - 1 - 2 * lax.div(chip, 2))


def ring_chip(place, chips):
    upper = lax.div(place, (chips + 1) // 2)
    return 2 * place + upper * (2 * (chips - 1 - place) + 1 - 2 * place)


def reduce_body(terms, chips, lefts, rights, out_count, *refs):
    refs = list(refs)

    def take(count):
        taken = refs[:count]
        del refs[:count]
        return taken

    left_refs, right_refs = take(lefts), take(rights)
    outs = take(out_count)
    own_left, own_right = take(lefts), take(rights)
    sib_left, sib_right = take(lefts), take(rights)
    landing, final = take(len(terms)), take(len(terms))
    split_at = [number for number, term in enumerate(terms) if term.split]
    give, got = take(len(split_at)), take(len(split_at))
    load_sem, swap_send, swap_recv, ring_send, ring_recv = take(5)
    give_send, got_recv, final_send, final_recv = take(4)
    stage, stage_sem, share_send, share_recv = take(4)

    device = lax.axis_index("fsdp")
    plane = lax.axis_index("rep")
    core, chip = lax.rem(device, 2), lax.div(device, 2)
    place = ring_place(chip, chips)
    sibling = {"fsdp": device + 1 - 2 * core}
    twin = {"rep": 1 - plane}
    ways = [
        {"fsdp": 2 * ring_chip(lax.rem(place + step, chips), chips) + core}
        for step in (1, chips - 1)
    ]

    barrier = pltpu.get_barrier_semaphore()
    partners = (ways[0], ways[1], sibling, twin)
    for partner in partners:
        pl.semaphore_signal(barrier, inc=1, device_id=partner, device_id_type=MESH)
    pl.semaphore_wait(barrier, len(partners))

    def remote(source, target, send_sem, recv_sem, partner):
        return pltpu.make_async_remote_copy(
            src_ref=source,
            dst_ref=target,
            send_sem=send_sem,
            recv_sem=recv_sem,
            device_id=partner,
            device_id_type=MESH,
        )

    loads, swaps = {}, {}
    for number in range(lefts):
        ref = left_refs[number]
        by_rows = len(ref.shape) == 4
        mine = ref.at[:, core] if by_rows else ref
        other = ref.at[:, 1 - core] if by_rows else ref
        loads["l", number] = pltpu.make_async_copy(mine, own_left[number], load_sem.at[number])
        swaps["l", number] = remote(
            other, sib_left[number], swap_send.at[number], swap_recv.at[number], sibling
        )
    for number in range(rights):
        ref, at = right_refs[number], lefts + number
        width = own_right[number].shape[1]
        if width == ref.shape[1]:
            mine = other = ref
        else:
            second = ref.shape[1] - width
            mine = ref.at[:, pl.ds(pl.multiple_of(core * second, 128), width)]
            other = ref.at[:, pl.ds(pl.multiple_of((1 - core) * second, 128), width)]
        loads["r", number] = pltpu.make_async_copy(mine, own_right[number], load_sem.at[at])
        swaps["r", number] = remote(
            other, sib_right[number], swap_send.at[at], swap_recv.at[at], sibling
        )
    first_use = {}
    for term in sorted(terms, key=lambda term: term.start - term.split):
        for key in (("l", term.left), ("r", term.right)):
            first_use.setdefault(key, term.start - term.split)
    for key in first_use:
        loads[key].start()
        swaps[key].start()
    for number, term in enumerate(terms):
        landing[number][0] = jnp.zeros(landing[number].shape[1:], jnp.bfloat16)

    def chunk(term, owner, part):
        rows = pl.ds(term.row_from, term.rows)
        from_column = term.column_from
        if term.split:
            from_column = pl.multiple_of(from_column + part * term.columns, 128)
        columns = pl.ds(from_column, term.columns)
        own = jnp.dot(
            own_left[term.left][owner, rows, :],
            own_right[term.right][:, columns],
            preferred_element_type=jnp.float32,
        )
        return own + jnp.dot(
            sib_left[term.left][owner, rows, :],
            sib_right[term.right][:, columns],
            preferred_element_type=jnp.float32,
        )

    def owner_at(term, hop):
        back = hop + 1 if term.way == 0 else 2 * chips - 1 - hop
        return ring_chip(lax.rem(place + 2 * chips - back, chips), chips)

    def give_copy(at, hop):
        return remote(
            give[at].at[lax.rem(hop, GIVE_SLOTS)],
            got[at].at[hop],
            give_send.at[at, hop],
            got_recv.at[at, hop],
            twin,
        )

    def ring_copy(number, hop):
        return remote(
            landing[number].at[hop],
            landing[number].at[hop + 1],
            ring_send.at[number, hop],
            ring_recv.at[number, hop + 1],
            ways[terms[number].way],
        )

    def arrival(number, hop):
        return remote(
            landing[number].at[hop],
            landing[number].at[hop],
            ring_send.at[number, hop],
            ring_recv.at[number, hop],
            ways[terms[number].way],
        )

    def final_copy(number):
        return remote(
            landing[number].at[chips - 1],
            final[number],
            final_send.at[number],
            final_recv.at[number],
            twin,
        )

    def step(clock, carry):
        for moment in sorted(set(first_use.values())):

            @pl.when(clock == moment)
            def _():
                for key, use in first_use.items():
                    if use == moment:
                        loads[key].wait()
                        swaps[key].wait_recv()

        for at, number in enumerate(split_at):
            term = terms[number]
            later = clock - term.start + 1

            @pl.when((later >= GIVE_SLOTS) & (later < chips))
            def _():
                give_copy(at, later - GIVE_SLOTS).wait_send()

            @pl.when((later >= 0) & (later < chips))
            def _():
                give[at][lax.rem(later, GIVE_SLOTS)] = chunk(term, owner_at(term, later), 1 - plane).astype(
                    jnp.bfloat16
                )
                give_copy(at, later).start()

        for number, term in enumerate(terms):
            hop = clock - term.start

            @pl.when((hop >= 0) & (hop < chips))
            def _():
                total = chunk(term, owner_at(term, hop), plane)
                if term.split:
                    at = split_at.index(number)
                    give_copy(at, hop).wait_recv()
                    total = total + got[at][hop].astype(jnp.float32)

                @pl.when(hop > 0)
                def _():
                    arrival(number, hop).wait_recv()

                landing[number][hop] = (
                    total + landing[number][hop].astype(jnp.float32)
                ).astype(jnp.bfloat16)

                @pl.when(hop < chips - 1)
                def _():
                    ring_copy(number, hop).start()

                @pl.when(hop == chips - 1)
                def _():
                    final_copy(number).start()

        return carry

    lax.fori_loop(0, max(term.start for term in terms) + chips, step, 0)
    stores, shares = [], []

    def store(term, values, from_column):
        slot = len(stores) % 2
        if len(stores) >= 2:
            stores[-2]()
        stage[slot, : term.rows, : term.columns] = values
        columns = pl.ds(from_column, term.columns)
        if len(left_refs[term.left].shape) == 4:
            copy = pltpu.make_async_copy(
                stage.at[slot, pl.ds(0, term.rows), pl.ds(0, term.columns)],
                outs[term.out].at[0, pl.ds(term.out_row, term.rows), columns],
                stage_sem.at[slot],
            )
            copy.start()
            stores.append(copy.wait)
            return
        half = term.rows // 2

        def rows_of(owner):
            return stage.at[
                slot, pl.ds(pl.multiple_of(owner * half, 8), half), pl.ds(0, term.columns)
            ]

        target = outs[term.out].at[core, :, columns]
        copy = pltpu.make_async_copy(rows_of(core), target, stage_sem.at[slot])
        at = len(shares)
        share = remote(
            rows_of(1 - core), target, share_send.at[at], share_recv.at[at], sibling
        )
        copy.start()
        share.start()

        def settle_store():
            copy.wait()
            share.wait_send()

        stores.append(settle_store)
        arrived = outs[term.out].at[1 - core, :, columns]
        shares.append(remote(arrived, arrived, share_send.at[at], share_recv.at[at], sibling))

    for number, term in enumerate(terms):
        final_copy(number).wait()
        mine = landing[number][chips - 1].astype(jnp.float32)
        other = final[number][...].astype(jnp.float32)
        if term.split:
            for part, values in ((plane, mine), (1 - plane, other)):
                from_column = term.out_column + part * term.columns
                store(term, values, pl.multiple_of(from_column, 128))
        else:
            store(term, mine + other, term.out_column)
    for settle_store in stores[-2:]:
        settle_store()
    for share in shares:
        share.wait_recv()

    def settle(hop, carry):
        for number in range(len(terms)):

            @pl.when(hop < chips - 1)
            def _():
                ring_copy(number, hop).wait_send()

        for at in range(len(split_at)):

            @pl.when(hop >= chips - GIVE_SLOTS)
            def _():
                give_copy(at, hop).wait_send()

        return carry

    lax.fori_loop(0, chips, settle, 0)
    for key in first_use:
        swaps[key].wait_send()


def core_columns(columns):
    return -(-columns // 256) * 128


def reduce_terms(terms, lefts, rights, identity):
    chips = lefts[0].shape[0]
    whole = {term.right for term in terms if lefts[term.left].ndim == 4}
    left_parts = [
        (left.shape[0],) + left.shape[-2:] for left in lefts
    ]
    right_parts = [
        (right.shape[0], right.shape[1] if number in whole else core_columns(right.shape[1]))
        for number, right in enumerate(rights)
    ]

    def vmem(shape):
        return pltpu.VMEM(shape, jnp.bfloat16)

    splits = [term for term in terms if term.split]
    operands = len(lefts) + len(rights)
    scratch = (
        [vmem(shape) for shape in left_parts + right_parts] * 2
        + [vmem((chips, term.rows, term.columns)) for term in terms]
        + [vmem((term.rows, term.columns)) for term in terms]
        + [vmem((GIVE_SLOTS, term.rows, term.columns)) for term in splits]
        + [vmem((chips, term.rows, term.columns)) for term in splits]
        + [pltpu.SemaphoreType.DMA((operands,))] * 3
        + [pltpu.SemaphoreType.DMA((len(terms), chips))] * 2
        + [pltpu.SemaphoreType.DMA((len(splits), chips))] * 2
        + [pltpu.SemaphoreType.DMA((len(terms),))] * 2
        + [
            pltpu.VMEM(
                (2, max(term.rows for term in terms), max(term.columns for term in terms)),
                jnp.float32,
            ),
            pltpu.SemaphoreType.DMA((2,)),
        ]
        + [pltpu.SemaphoreType.DMA((len(terms) + len(splits),))] * 2
    )
    heights, widths, halves = {}, {}, {}
    for term in terms:
        out, width = term.out, term.columns * (1 + term.split)
        halves[out] = 1 if lefts[term.left].ndim == 4 else 2
        heights[out] = max(heights.get(out, 0), (term.out_row + term.rows) // halves[out])
        widths[out] = max(widths.get(out, 0), term.out_column + width)
    return pl.pallas_call(
        partial(reduce_body, terms, chips, len(lefts), len(rights), len(heights)),
        out_shape=[
            jax.ShapeDtypeStruct((halves[out], heights[out], widths[out]), jnp.float32)
            for out in range(len(heights))
        ],
        in_specs=[pl.BlockSpec(memory_space=pl.ANY)] * operands,
        out_specs=[pl.BlockSpec(memory_space=pl.ANY)] * len(heights),
        scratch_shapes=scratch,
        compiler_params=pltpu.CompilerParams(
            collective_id=identity, has_side_effects=True, vmem_limit_bytes=62 * 1024 * 1024
        ),
    )(*lefts, *rights)


class Piece(NamedTuple):
    source: int
    rows: int
    columns: int
    row_core: int
    row_plane: int
    column_from: int
    column_core: int
    column_plane: int
    split: bool
    long_way: int


def gather_body(pieces, chips, count, *refs):
    sources, outs = refs[:count], refs[count : 2 * count]
    ring_send, ring_recv, pass_send, pass_recv, twin_send, twin_recv, own_sem = refs[2 * count :]
    device = lax.axis_index("fsdp")
    plane = lax.axis_index("rep")
    core, chip = lax.rem(device, 2), lax.div(device, 2)
    place = ring_place(chip, chips)
    sibling = {"fsdp": device + 1 - 2 * core}
    twin = {"rep": 1 - plane}

    def chip_back(way, hops):
        back = hops if way == 0 else chips - hops
        return ring_chip(lax.rem(place + chips - back, chips), chips)

    ways = [{"fsdp": 2 * chip_back(1 - way, 1) + core} for way in range(2)]

    barrier = pltpu.get_barrier_semaphore()
    partners = (ways[0], ways[1], sibling, twin)
    for partner in partners:
        pl.semaphore_signal(barrier, inc=1, device_id=partner, device_id_type=MESH)
    pl.semaphore_wait(barrier, len(partners))

    keep = [
        pltpu.make_async_copy(
            sources[number],
            outs[number].at[
                pl.ds(
                    pl.multiple_of(chip * sources[number].shape[0], 16), sources[number].shape[0]
                ),
                :,
            ],
            own_sem.at[number],
        )
        for number in range(count)
    ]
    for copy in keep:
        copy.start()

    def window(piece, ref, base, of_core, of_plane):
        row = base + of_core * piece.row_core + of_plane * piece.row_plane
        column = (
            piece.column_from + of_core * piece.column_core + of_plane * piece.column_plane
        )
        return ref.at[
            pl.ds(pl.multiple_of(row, 16), piece.rows),
            pl.ds(pl.multiple_of(column, 128), piece.columns),
        ]

    def landed(number, owner, of_core, of_plane):
        piece = pieces[number]
        height = sources[piece.source].shape[0]
        return window(piece, outs[piece.source], owner * height, of_core, of_plane)

    def remote(source, target, sems, index, partner):
        return pltpu.make_async_remote_copy(
            src_ref=source,
            dst_ref=target,
            send_sem=sems[0].at[index],
            recv_sem=sems[1].at[index],
            device_id=partner,
            device_id_type=MESH,
        )

    hops = [
        [chips // 2 if piece.long_way == way else (chips - 1) // 2 for way in range(2)]
        for piece in pieces
    ]
    splits = [number for number, piece in enumerate(pieces) if piece.split]
    sent = []

    def send(copy):
        copy.start()
        sent.append(copy)

    for number, piece in enumerate(pieces):
        for way in range(2):
            send(
                remote(
                    window(piece, sources[piece.source], 0, core, plane),
                    landed(number, chip, core, plane),
                    (ring_send, ring_recv),
                    (number, way, 0),
                    ways[way],
                )
            )

    def ring_arrivals(hop):
        for number, piece in enumerate(pieces):
            for way in range(2):
                if hop > hops[number][way]:
                    continue
                block = landed(number, chip_back(way, hop), core, plane)
                remote(
                    block, block, (ring_send, ring_recv), (number, way, hop - 1), ways[way]
                ).wait_recv()
                if hop < hops[number][way]:
                    send(
                        remote(
                            block, block, (ring_send, ring_recv), (number, way, hop), ways[way]
                        )
                    )
                send(
                    remote(
                        block, block, (pass_send, pass_recv), (number, way, hop - 1), sibling
                    )
                )
                if piece.split:
                    at = splits.index(number)
                    send(
                        remote(block, block, (twin_send, twin_recv), (at, way, hop - 1), twin)
                    )

    def twin_arrivals(hop):
        for at, number in enumerate(splits):
            for way in range(2):
                if hop > hops[number][way]:
                    continue
                block = landed(number, chip_back(way, hop), core, 1 - plane)
                remote(
                    block, block, (twin_send, twin_recv), (at, way, hop - 1), twin
                ).wait_recv()
                send(
                    remote(
                        block,
                        block,
                        (pass_send, pass_recv),
                        (len(pieces) + at, way, hop - 1),
                        sibling,
                    )
                )

    for hop in range(1, chips // 2 + 1):
        ring_arrivals(hop)
        if hop > 1:
            twin_arrivals(hop - 1)
    twin_arrivals(chips // 2)
    for number in range(len(pieces) + len(splits)):
        at = number if number < len(pieces) else splits[number - len(pieces)]
        of_plane = plane if number < len(pieces) else 1 - plane
        for way in range(2):
            for hop in range(1, hops[at][way] + 1):
                block = landed(at, chip_back(way, hop), 1 - core, of_plane)
                remote(
                    block, block, (pass_send, pass_recv), (number, way, hop - 1), sibling
                ).wait_recv()
    for copy in sent:
        copy.wait_send()
    for copy in keep:
        copy.wait()


def gather_pieces(pieces, sources, identity):
    chips = lax.axis_size("fsdp") // 2
    splits = sum(piece.split for piece in pieces)
    hops = chips // 2

    def sems(number):
        return [pltpu.SemaphoreType.DMA((number, 2, hops))] * 2

    return pl.pallas_call(
        partial(gather_body, pieces, chips, len(sources)),
        out_shape=[
            jax.ShapeDtypeStruct((chips * source.shape[0], source.shape[1]), source.dtype)
            for source in sources
        ],
        in_specs=[pl.BlockSpec(memory_space=pl.ANY)] * len(sources),
        out_specs=[pl.BlockSpec(memory_space=pl.ANY)] * len(sources),
        scratch_shapes=sems(len(pieces))
        + sems(len(pieces) + splits)
        + sems(splits)
        + [pltpu.SemaphoreType.DMA((len(sources),))],
        compiler_params=pltpu.CompilerParams(collective_id=identity, has_side_effects=True),
    )(*sources)


def chip_rows(shard):
    other = swap_cores(shard)
    core = lax.axis_index("fsdp") % 2
    return jnp.where(
        core == 0, jnp.concatenate([shard, other]), jnp.concatenate([other, shard])
    )


def by_chip(values):
    chips = lax.axis_size("fsdp") // 2
    return values.T.reshape(chips, -1, values.shape[0])


def by_device(values):
    chips = lax.axis_size("fsdp") // 2
    return values.T.reshape(chips, 2, -1, values.shape[0])


def join_cores(both, columns):
    joined, at = [], 0
    for width in columns:
        end = at + core_columns(width)
        twice = 2 * core_columns(width) - width
        joined += [both[0, :, at:end], both[1, :, at + twice : end]]
        at = end
    return joined


def plain_sum(left, right):
    total = lax.psum_scatter(
        outer_rows(left, right).astype(jnp.bfloat16), "fsdp", scatter_dimension=0, tiled=True
    )
    return lax.psum(total.astype(jnp.float32), "rep")


def kernels_fit(rows):
    return 2 * rows % 16 == 0 and lax.axis_size("rep") == 2


def sum_grads(factors, first=None, second=None, third=None, identity=0):
    (normed, attended, mixed, active), (triple_grad, branch_grad, pre_grad, feed_grad) = factors
    count = lax.axis_size("fsdp")
    rows = MODEL_WIDTH // count
    extra = [pair for pair in (first, second, third) if pair is not None]
    if not kernels_fit(rows):
        wide = [
            plain_sum(left.reshape(-1, left.shape[-1]).T, right)
            for left, right in zip((normed, attended, mixed, active), factors[1])
        ]
        return (wide[:3], wide[3], [plain_sum(*pair) for pair in extra])
    triple_half = core_columns(triple_grad.shape[1])
    branch_half = core_columns(branch_grad.shape[1])
    pre_half = core_columns(pre_grad.shape[1])
    plain_part = 8 * 128
    pre_part = (pre_half - plain_part) // 2
    deep_rows = active.shape[2] // 2
    pre_at = triple_half + branch_half
    terms = [
        Term(3, 3, deep_rows, 0, MODEL_WIDTH, 0, False, 0, 0, 1, 0, 0),
        Term(3, 3, deep_rows, deep_rows, MODEL_WIDTH, 0, False, 1, 0, 1, deep_rows, 0),
        Term(2, 2, 2 * rows, 0, pre_part, plain_part, True, 1, 1, 0, 0, pre_at + plain_part),
        Term(0, 0, 2 * rows, 0, triple_half // 2, 0, True, 0, 2, 0, 0, 0),
        Term(2, 2, 2 * rows, 0, plain_part, 0, False, 1, 2, 0, 0, pre_at),
        Term(1, 1, 2 * rows, 0, branch_half, 0, False, 0, 3, 0, 0, triple_half),
    ]
    lefts = [normed, attended, mixed, active]
    rights = [triple_grad, branch_grad, pre_grad, feed_grad]
    columns = []
    for pair, ways in ((first, "s"), (second, "ps"), (third, "p")):
        if pair is None:
            continue
        at, out = len(lefts), 2 + len(columns)
        lefts.append(by_chip(pair[0]))
        rights.append(pair[1])
        height, half = lefts[-1].shape[1], core_columns(pair[1].shape[1])
        if ways == "s":
            terms.append(Term(at, at, height, 0, half // 2, 0, True, 0, 1, out, 0, 0))
        elif ways == "p":
            terms.append(Term(at, at, height, 0, half, 0, False, 1, 1, out, 0, 0))
        else:
            half = half // 2
            terms.append(Term(at, at, height, 0, half, 0, False, 0, 1, out, 0, 0))
            terms.append(Term(at, at, height, 0, half // 2, half, True, 1, 1, out, 0, half))
        columns.append(pair[1].shape[1])
    outs = reduce_terms(tuple(terms), lefts, rights, identity)
    wide = join_cores(outs[0], [triple_grad.shape[1], branch_grad.shape[1], pre_grad.shape[1]])
    rest = [
        jnp.concatenate(join_cores(out, [width]), axis=1)
        for out, width in zip(outs[2:], columns)
    ]
    return (wide, outs[1][0], rest)


def pack_body(*refs):
    out, at = refs[-1], 0
    for ref in refs[:-1]:
        width = ref.shape[1]
        out[:, at : at + width] = ref[...].astype(jnp.bfloat16).astype(out.dtype)
        at += width


def pack_rows(pieces, dtype):
    rows = pieces[0].shape[0]
    width = sum(piece.shape[1] for piece in pieces)
    return pl.pallas_call(
        pack_body, out_shape=jax.ShapeDtypeStruct((rows, width), dtype)
    )(*pieces)


def gathered_terms(row):
    return lax.all_gather(row, ("fsdp", "rep"), axis=0, tiled=True)


def fetch_block(wide_shard, deep_shard, identity):
    rest = wide_shard[:, 6 * MODEL_WIDTH :].astype(jnp.bfloat16)
    low = deep_shard.astype(jnp.bfloat16)
    rows = rest.shape[0]
    if kernels_fit(rows):
        unit = MODEL_WIDTH
        deep_rows = low.shape[0] // 2
        pieces = (
            Piece(0, 2 * rows, unit, 0, 0, 0, 4 * unit, unit, True, 0),
            Piece(1, deep_rows, unit, 2 * deep_rows, deep_rows, 0, 0, 0, True, 1),
            Piece(0, 2 * rows, unit, 0, 0, 2 * unit, 4 * unit, unit, True, 1),
        )
        whole, deep = gather_pieces(pieces, [chip_rows(rest), chip_rows(low)], identity)
    else:
        whole = lax.all_gather(rest, "fsdp", axis=0, tiled=True)
        deep = lax.all_gather(low, "fsdp", axis=0, tiled=True)
    split = (
        whole[:, : 3 * MODEL_WIDTH],
        whole[:, 3 * MODEL_WIDTH : 4 * MODEL_WIDTH],
        whole[:, 4 * MODEL_WIDTH :],
    )
    return (split, deep)


def fetch_block_and(wide_shard, deep_shard, other_shard):
    rest = jnp.concatenate(
        [other_shard.astype(jnp.bfloat16), wide_shard[:, 6 * MODEL_WIDTH :].astype(jnp.bfloat16)],
        axis=1,
    )
    whole = lax.all_gather(rest, "fsdp", axis=0, tiled=True)
    deep = lax.all_gather(deep_shard.astype(jnp.bfloat16), "fsdp", axis=0, tiled=True)
    at = other_shard.shape[1]
    split = (
        whole[:, at : at + 3 * MODEL_WIDTH],
        whole[:, at + 3 * MODEL_WIDTH : at + 4 * MODEL_WIDTH],
        whole[:, at + 4 * MODEL_WIDTH :],
    )
    return (split, deep, whole[:, :at])


def plane_modulation(silu_low, wide_weight, block_bias):
    count = lax.axis_size("fsdp")
    sequences = silu_low.shape[0]
    rows = wide_weight.shape[1]
    device = lax.axis_index("fsdp")
    spread = jnp.broadcast_to(
        silu_low.reshape(1, sequences, count, rows).transpose(2, 0, 1, 3)[:, 0],
        (count, sequences, rows),
    )
    met = lax.all_to_all(spread, "fsdp", 0, 0, tiled=True)
    met = met.reshape(count * sequences, rows)
    partial = [
        jnp.dot(
            met,
            wide_weight[block, :, : 6 * MODEL_WIDTH].astype(jnp.bfloat16),
            preferred_element_type=jnp.float32,
        )
        for block in range(2)
    ]
    partial = jnp.stack(partial, axis=1).reshape(count, sequences, 2, 6 * MODEL_WIDTH)
    back = lax.all_to_all(partial, "fsdp", 0, 0, tiled=True)
    total = jnp.sum(back, axis=0)
    return [total[:, block] + block_bias[block, : 6 * MODEL_WIDTH] for block in range(2)]


HEAD_WINDOW = 256


def head_window(head, width):
    first = head * HEAD_DIM
    at = min(first // 128 * 128, width - HEAD_WINDOW)
    lane = lax.broadcasted_iota(jnp.int32, (1, HEAD_WINDOW), 1)
    return at, (lane >= first - at) & (lane < first - at + HEAD_DIM)


def only(mine, values):
    return jnp.where(mine, values, jnp.zeros_like(values))


def against(left, right):
    return lax.dot_general(
        left, right, (((1,), (1,)), ((), ())), preferred_element_type=jnp.float32
    )


def attend_body(lengths_ref, triple_ref, attended_ref, log_ref, total_ref):
    tokens, width = attended_ref.shape
    length = lengths_ref[pl.program_id(0)]
    seen = lax.broadcasted_iota(jnp.int32, (tokens, 1), 0) < length
    total_ref[...] = jnp.zeros_like(total_ref)
    for head in range(HEADS):
        at, mine = head_window(head, width)
        window = pl.ds(at, HEAD_WINDOW)
        keys = only(mine, triple_ref[:, pl.ds(width + at, HEAD_WINDOW)])
        values = only(mine, triple_ref[:, pl.ds(2 * width + at, HEAD_WINDOW)])
        scores = against(keys, triple_ref[:, window]) * HEAD_DIM ** (-0.5)
        scores = jnp.where(seen, scores, masked_score)
        largest = jnp.max(scores, axis=0, keepdims=True)
        expanded = jnp.exp(scores - largest)
        sums = jnp.sum(expanded, axis=0, keepdims=True)
        weights = (expanded * (1.0 / sums)).astype(jnp.bfloat16)
        total_ref[:, window] += lax.dot_general(
            weights, values, (((0,), (0,)), ((), ())), preferred_element_type=jnp.float32
        )
        log_ref[head : head + 1, :] = largest + jnp.log(sums)
    attended_ref[...] = total_ref[...].astype(jnp.bfloat16)


def attention_forward(triple, lengths):
    sequences, tokens, columns = triple.shape
    width = columns // 3
    return pl.pallas_call(
        attend_body,
        grid=(sequences,),
        out_shape=[
            jax.ShapeDtypeStruct((sequences, tokens, width), jnp.bfloat16),
            jax.ShapeDtypeStruct((sequences, HEADS, tokens), jnp.float32),
        ],
        in_specs=[
            pl.BlockSpec(memory_space=pltpu.SMEM),
            pl.BlockSpec((None, tokens, columns), lambda number: (number, 0, 0)),
        ],
        out_specs=[
            pl.BlockSpec((None, tokens, width), lambda number: (number, 0, 0)),
            pl.BlockSpec((None, HEADS, tokens), lambda number: (number, 0, 0)),
        ],
        scratch_shapes=[pltpu.VMEM((tokens, width), jnp.float32)],
        compiler_params=pltpu.CompilerParams(vmem_limit_bytes=48 * 1024 * 1024),
    )(lengths, triple)


def attend_back_body(lengths_ref, triple_ref, log_ref, upstream_ref, grad_ref, total_ref):
    tokens, width = upstream_ref.shape
    length = lengths_ref[pl.program_id(0)]
    factor = HEAD_DIM ** (-0.5)
    seen = lax.broadcasted_iota(jnp.int32, (tokens, 1), 0) < length
    total_ref[...] = jnp.zeros_like(total_ref)
    for head in range(HEADS):
        at, mine = head_window(head, width)
        query_at, key_at, value_at = (
            pl.ds(group * width + at, HEAD_WINDOW) for group in range(3)
        )
        queries = only(mine, triple_ref[:, query_at])
        keys = only(mine, triple_ref[:, key_at])
        values = only(mine, triple_ref[:, value_at])
        upstream = only(mine, upstream_ref[:, pl.ds(at, HEAD_WINDOW)])
        scores = against(keys, queries) * factor
        chances = jnp.where(seen, jnp.exp(scores - log_ref[head : head + 1, :]), 0.0)
        chance_grad = against(values, upstream)
        centre = jnp.sum(chance_grad * chances, axis=0, keepdims=True)
        score_grad = (chances * (chance_grad - centre)).astype(jnp.bfloat16)
        total_ref[:, value_at] += jnp.dot(
            chances.astype(jnp.bfloat16), upstream, preferred_element_type=jnp.float32
        )
        total_ref[:, key_at] += factor * jnp.dot(
            score_grad, queries, preferred_element_type=jnp.float32
        )
        total_ref[:, query_at] += factor * lax.dot_general(
            score_grad, keys, (((0,), (0,)), ((), ())), preferred_element_type=jnp.float32
        )
    grad_ref[...] = total_ref[...].astype(jnp.bfloat16)


def attention_backward(triple, logs, upstream, lengths):
    sequences, tokens, columns = triple.shape

    def spec(width):
        return pl.BlockSpec((None, tokens, width), lambda number: (number, 0, 0))

    return pl.pallas_call(
        attend_back_body,
        grid=(sequences,),
        out_shape=jax.ShapeDtypeStruct((sequences, tokens, columns), jnp.bfloat16),
        in_specs=[
            pl.BlockSpec(memory_space=pltpu.SMEM),
            spec(columns),
            pl.BlockSpec((None, HEADS, tokens), lambda number: (number, 0, 0)),
            spec(columns // 3),
        ],
        out_specs=spec(columns),
        scratch_shapes=[pltpu.VMEM((tokens, columns), jnp.float32)],
        compiler_params=pltpu.CompilerParams(vmem_limit_bytes=48 * 1024 * 1024),
    )(lengths, triple, logs, upstream)


def block_forward(hidden, modulation, wide_matrix, deep_matrix, bias, lengths):
    sequences = hidden.shape[0]
    offset_first, factor_first, gate_first, offset_second, factor_second, gate_second = (
        split_modulation(modulation)
    )
    normed_low = modulate(hidden, offset_first, factor_first).astype(jnp.bfloat16)
    triple_bias = jnp.concatenate(
        [
            bias[6 * MODEL_WIDTH : 7 * MODEL_WIDTH],
            jnp.zeros((MODEL_WIDTH,), jnp.float32),
            bias[7 * MODEL_WIDTH : 8 * MODEL_WIDTH],
        ]
    )
    triple = (
        jnp.dot(
            normed_low,
            wide_matrix[0],
            preferred_element_type=jnp.float32,
        )
        + triple_bias
    ).astype(jnp.bfloat16)
    attended_low, log_total = attention_forward(triple, lengths)
    branch = (
        jnp.dot(
            attended_low,
            wide_matrix[1],
            preferred_element_type=jnp.float32,
        )
        + bias[8 * MODEL_WIDTH : 9 * MODEL_WIDTH]
    )
    middle = hidden + gate_first * branch
    mixed_low = modulate(middle, offset_second, factor_second).astype(jnp.bfloat16)
    pre_active = (
        jnp.dot(mixed_low, wide_matrix[2], preferred_element_type=jnp.float32)
        + bias[9 * MODEL_WIDTH : 9 * MODEL_WIDTH + FF]
    )
    active_low = gelu_tanh(pre_active).astype(jnp.bfloat16)
    feed_out = (
        jnp.dot(active_low, deep_matrix, preferred_element_type=jnp.float32)
        + bias[9 * MODEL_WIDTH + FF :]
    )
    result = middle + gate_second * feed_out
    saved = (
        hidden,
        modulation,
        normed_low,
        triple,
        log_total,
        attended_low,
        branch,
        middle,
        mixed_low,
        pre_active,
        active_low,
        feed_out,
    )
    return (result, saved)


def block_backward(upstream, saved, wide_matrix, deep_matrix, lengths):
    (
        hidden,
        modulation,
        normed_low,
        triple,
        log_total,
        attended_low,
        branch,
        middle,
        mixed_low,
        pre_active,
        active_low,
        feed_out,
    ) = saved
    sequences = hidden.shape[0]
    offset_first, factor_first, gate_first, offset_second, factor_second, gate_second = (
        split_modulation(modulation)
    )
    feedforward_gradient = (upstream * gate_second).astype(jnp.bfloat16)
    gate_second_grad = jnp.sum(upstream * feed_out, axis=1, keepdims=True)
    activation_gradient = jnp.einsum(
        "xjn,mn->xjm", feedforward_gradient, deep_matrix, preferred_element_type=jnp.float32
    )
    preactivation_gradient = jax.vjp(gelu_tanh, pre_active)[1](activation_gradient)[0].astype(
        jnp.bfloat16
    )
    mixed_grad = jnp.einsum(
        "qvm,am->qva",
        preactivation_gradient,
        wide_matrix[2],
        preferred_element_type=jnp.float32,
    )
    second_back = jax.vjp(modulate, middle, offset_second, factor_second)[1]
    middle_part, offset_second_grad, factor_second_grad = second_back(mixed_grad)
    middle_grad = upstream + middle_part
    gate_first_grad = jnp.sum(middle_grad * branch, axis=1, keepdims=True)
    branch_gradient = (middle_grad * gate_first).astype(jnp.bfloat16)
    attended_grad = jnp.einsum(
        "tbr,ar->tba",
        branch_gradient,
        wide_matrix[1],
        preferred_element_type=jnp.float32,
    ).astype(jnp.bfloat16)
    triple_gradient = attention_backward(triple, log_total, attended_grad, lengths)
    normed_grad = jnp.einsum(
        "tbr,ar->tba",
        triple_gradient,
        wide_matrix[0],
        preferred_element_type=jnp.float32,
    )
    first_back = jax.vjp(modulate, hidden, offset_first, factor_first)[1]
    hidden_part, offset_first_grad, factor_first_grad = first_back(normed_grad)
    hidden_grad = middle_grad + hidden_part
    def column_sum(values):
        return jnp.sum(values, axis=(0, 1), dtype=jnp.float32, keepdims=True)[0]

    triple_sum = column_sum(triple_gradient)
    row_pieces = [
        piece.reshape(1, -1)
        for piece in (
            offset_first_grad,
            factor_first_grad,
            gate_first_grad,
            offset_second_grad,
            factor_second_grad,
            gate_second_grad,
        )
    ] + [
        triple_sum[:, :MODEL_WIDTH],
        triple_sum[:, 2 * MODEL_WIDTH :],
        column_sum(branch_gradient),
        column_sum(preactivation_gradient),
        column_sum(feedforward_gradient),
    ]

    def flat(values):
        return values.reshape(-1, values.shape[-1])

    entering = [by_chip(flat(values)) for values in (normed_low, attended_low, mixed_low)]
    entering.append(by_device(flat(active_low)))
    returning = [
        flat(values)
        for values in (
            triple_gradient,
            branch_gradient,
            preactivation_gradient,
            feedforward_gradient,
        )
    ]
    factors = (entering, returning)
    return (hidden_grad, row_pieces, factors)


def adam_update(weight, grad, first, second, rate, decay):
    first_new = 0.9 * first + 0.1 * grad
    second_new = 0.999 * second + 0.001 * grad * grad
    first_hat = first_new / (1.0 - 0.9**STEP)
    second_hat = second_new / (1.0 - 0.999**STEP)
    updated = weight - rate * (first_hat / (jnp.sqrt(second_hat) + adam_epsilon) + decay * weight)
    return (first_new, second_new, updated)


def per_device(
    tokens,
    condition,
    lengths,
    targets,
    cotangent,
    wide_weight,
    deep_weight,
    head_first,
    head_second,
    block_bias,
    head_bias,
    wide_mean,
    deep_mean,
    head_first_mean,
    head_second_mean,
    block_bias_mean,
    head_bias_mean,
    wide_square,
    deep_square,
    head_first_square,
    head_second_square,
    block_bias_square,
    head_bias_square,
):
    sequences = condition.shape[0]
    hidden = tokens.astype(jnp.float32).reshape(sequences, SEQ_LEN, MODEL_WIDTH)
    silu_low = jax.nn.silu(condition.astype(jnp.float32)).astype(jnp.bfloat16)
    visible = jnp.arange(SEQ_LEN, dtype=jnp.int32)[None, :] < lengths[:, None]
    wide_early, deep_early = fetch_block(wide_weight[0], deep_weight[0], 3)
    modulation_early, modulation_late = plane_modulation(silu_low, wide_weight, block_bias)
    tapped, saved_early = block_forward(
        hidden, modulation_early, wide_early, deep_early, block_bias[0], lengths
    )
    wide_late, deep_late, first_matrix = fetch_block_and(
        wide_weight[1], deep_weight[1], head_first
    )
    second_w = lax.all_gather(head_second.astype(jnp.bfloat16), "fsdp", axis=0, tiled=True)
    final, saved_late = block_forward(
        tapped, modulation_late, wide_late, deep_late, block_bias[1], lengths
    )
    raw_targets = targets.astype(jnp.float32).reshape(sequences, SEQ_LEN, PZ)
    target_unit = raw_targets * lax.rsqrt(
        jnp.sum(raw_targets * raw_targets, axis=-1, keepdims=True) + norm_epsilon
    )

    def alignment(values):
        unit = values * lax.rsqrt(jnp.sum(values * values, axis=-1, keepdims=True) + norm_epsilon)
        return jnp.sum(unit * target_unit, axis=-1)

    upstream = cotangent.astype(jnp.float32).reshape(sequences, SEQ_LEN, MODEL_WIDTH)
    late_input_grad, late_row, late_factors = block_backward(
        upstream, saved_late, wide_late, deep_late, lengths
    )
    tapped_low, late_input_grad, late_factors = lax.optimization_barrier(
        (tapped.astype(jnp.bfloat16), late_input_grad, late_factors)
    )
    first_pre = (
        jnp.dot(tapped_low, first_matrix, preferred_element_type=jnp.float32) + head_bias[:PH]
    )
    first_low = jax.nn.silu(first_pre).astype(jnp.bfloat16)
    second_pre = (
        jnp.dot(first_low, second_w[:, :PH], preferred_element_type=jnp.float32)
        + head_bias[PH : 2 * PH]
    )
    second_low = jax.nn.silu(second_pre).astype(jnp.bfloat16)
    projected = (
        jnp.dot(second_low, second_w[:, PH:], preferred_element_type=jnp.float32)
        + head_bias[2 * PH :]
    )
    projected_grad = jax.vjp(alignment, projected)[1](-repa_weight * visible.astype(jnp.float32))[
        0
    ].astype(jnp.bfloat16)
    second_act_grad = jnp.einsum(
        "slz,hz->slh", projected_grad, second_w[:, PH:], preferred_element_type=jnp.float32
    )
    second_grad = jax.vjp(jax.nn.silu, second_pre)[1](second_act_grad)[0].astype(jnp.bfloat16)
    first_act_grad = jnp.einsum(
        "slh,gh->slg", second_grad, second_w[:, :PH], preferred_element_type=jnp.float32
    )
    first_gradient = jax.vjp(jax.nn.silu, first_pre)[1](first_act_grad)[0].astype(jnp.bfloat16)
    tapped_gradient = jnp.einsum(
        "ejk,rk->ejr", first_gradient, first_matrix, preferred_element_type=jnp.float32
    )

    def column_sum(values):
        return jnp.sum(values, axis=(0, 1), dtype=jnp.float32, keepdims=True)[0]

    def flat(values):
        return values.reshape(-1, values.shape[-1])

    late_packed = pack_rows(
        [silu_low]
        + late_row
        + [column_sum(first_gradient), column_sum(second_grad), column_sum(projected_grad)],
        jnp.bfloat16,
    )
    late_packed, late_input_grad = lax.optimization_barrier((late_packed, late_input_grad))
    late_rows = gathered_terms(late_packed)
    input_grad, early_row, early_factors = block_backward(
        late_input_grad + tapped_gradient, saved_early, wide_early, deep_early, lengths
    )
    early_packed = pack_rows(early_row, jnp.float32)
    first_pair = [flat(tapped_low), flat(first_gradient)]
    second_pair = [flat(first_low), flat(second_grad)]
    third_pair = [flat(second_low), flat(projected_grad)]
    early_packed, late_rows, early_factors, late_factors, second_pair = (
        lax.optimization_barrier(
            (early_packed, late_rows, early_factors, late_factors, second_pair)
        )
    )
    early_rows = gathered_terms(early_packed)
    late_wide_grad, late_deep_grad, (first_weight_grad, third_weight_grad) = sum_grads(
        late_factors, first=first_pair, third=third_pair, identity=0
    )
    early_rows, early_factors, late_deep_grad = lax.optimization_barrier(
        (early_rows, early_factors, late_deep_grad)
    )
    early_wide_grad, early_deep_grad, (second_weight_grad,) = sum_grads(
        early_factors, second=second_pair, identity=1
    )
    second_weight_grad = jnp.concatenate([second_weight_grad, third_weight_grad], axis=1)
    own_silu = lax.dynamic_slice_in_dim(
        late_rows,
        lax.axis_index("fsdp") * wide_weight.shape[1],
        wide_weight.shape[1],
        axis=1,
    )
    late_rows = late_rows[:, MODEL_WIDTH:]
    bias_width = block_bias.shape[1]

    def modulation_weight_grad(rows):
        return lax.dot_general(
            own_silu,
            rows[:, : 6 * MODEL_WIDTH].astype(jnp.bfloat16),
            (((0,), (0,)), ((), ())),
            preferred_element_type=jnp.float32,
        )

    wide_grad = jnp.stack(
        [
            jnp.concatenate(
                [modulation_weight_grad(early_rows)] + early_wide_grad,
                axis=1,
            ),
            jnp.concatenate(
                [modulation_weight_grad(late_rows)] + late_wide_grad,
                axis=1,
            ),
        ]
    )
    deep_grad = jnp.stack([early_deep_grad, late_deep_grad])
    late_sum = jnp.sum(late_rows, axis=0, dtype=jnp.float32)
    early_sum = jnp.sum(early_rows, axis=0, dtype=jnp.float32)
    block_bias_grad = jnp.stack([early_sum, late_sum[:bias_width]])
    head_bias_total = late_sum[bias_width:]
    wide_m, wide_v, wide_new = adam_update(
        wide_weight, wide_grad, wide_mean, wide_square, matrix_rate, matrix_decay
    )
    deep_m, deep_v, deep_new = adam_update(
        deep_weight, deep_grad, deep_mean, deep_square, matrix_rate, matrix_decay
    )
    first_m, first_v, first_new = adam_update(
        head_first, first_weight_grad, head_first_mean, head_first_square, matrix_rate, matrix_decay
    )
    second_m, second_v, second_new = adam_update(
        head_second,
        second_weight_grad,
        head_second_mean,
        head_second_square,
        matrix_rate,
        matrix_decay,
    )
    bias_m, bias_v, bias_new = adam_update(
        block_bias, block_bias_grad, block_bias_mean, block_bias_square, bias_rate, 0.0
    )
    hbias_m, hbias_v, hbias_new = adam_update(
        head_bias, head_bias_total, head_bias_mean, head_bias_square, bias_rate, 0.0
    )
    output = final.reshape(sequences * SEQ_LEN, MODEL_WIDTH).astype(jnp.bfloat16)
    input_flat = input_grad.reshape(sequences * SEQ_LEN, MODEL_WIDTH)
    return (
        output,
        input_flat,
        wide_grad,
        deep_grad,
        first_weight_grad,
        second_weight_grad,
        block_bias_grad,
        head_bias_total,
        wide_m,
        deep_m,
        first_m,
        second_m,
        bias_m,
        hbias_m,
        wide_v,
        deep_v,
        first_v,
        second_v,
        bias_v,
        hbias_v,
        wide_new,
        deep_new,
        first_new,
        second_new,
        bias_new,
        hbias_new,
    )


def solution(mesh):
    in_specs = (
        P(("fsdp", "rep"), None),
        P(("fsdp", "rep"), None),
        P(("fsdp", "rep")),
        P(("fsdp", "rep"), None),
        P(("fsdp", "rep"), None),
        P(None, "fsdp", None),
        P(None, "fsdp", None),
        P("fsdp", None),
        P("fsdp", None),
        P(),
        P(),
        P(None, "fsdp", None),
        P(None, "fsdp", None),
        P("fsdp", None),
        P("fsdp", None),
        P(),
        P(),
        P(None, "fsdp", None),
        P(None, "fsdp", None),
        P("fsdp", None),
        P("fsdp", None),
        P(),
        P(),
    )
    out_specs = (
        P(("fsdp", "rep"), None),
        P(("fsdp", "rep"), None),
        P(None, "fsdp", None),
        P(None, "fsdp", None),
        P("fsdp", None),
        P("fsdp", None),
        P(),
        P(),
        P(None, "fsdp", None),
        P(None, "fsdp", None),
        P("fsdp", None),
        P("fsdp", None),
        P(),
        P(),
        P(None, "fsdp", None),
        P(None, "fsdp", None),
        P("fsdp", None),
        P("fsdp", None),
        P(),
        P(),
        P(None, "fsdp", None),
        P(None, "fsdp", None),
        P("fsdp", None),
        P("fsdp", None),
        P(),
        P(),
    )
    return jax.shard_map(
        per_device, mesh=mesh, in_specs=in_specs, out_specs=out_specs, check_vma=False
    )
```

```python
from functools import partial
from typing import NamedTuple

import jax
import jax.numpy as jnp
from jax import lax
from jax.experimental import pallas as pl
from jax.experimental.pallas import tpu as pltpu
from jax.sharding import PartitionSpec as P

MESH = pl.DeviceIdType.MESH
GIVE_SLOTS = 3

MODEL_WIDTH = 1152
HEADS = 16
HEAD_DIM = 72
FF = 4608
PH = 2048
PZ = 768
SEQ_LEN = 448
STEP = 10


norm_epsilon = 1e-06
adam_epsilon = 1e-08
masked_score = -1e30
repa_weight = 0.5
matrix_rate = 0.05
bias_rate = 0.3
matrix_decay = 0.01


def normalize(values):
    centred = values - jnp.mean(values, axis=-1, keepdims=True)
    spread = jnp.mean(centred * centred, axis=-1, keepdims=True)
    return centred * lax.rsqrt(spread + norm_epsilon)


def modulate(values, offset, factor):
    return normalize(values) * (1.0 + factor) + offset


def gelu_tanh(values):
    return jax.nn.gelu(values, approximate=True)


def split_modulation(modulation):
    columns = modulation.shape[-1] // 6
    return [modulation[:, None, number * columns : (number + 1) * columns] for number in range(6)]


def outer_rows(left, right):
    flat_left = left.reshape(-1, left.shape[-1])
    flat_right = right.reshape(-1, right.shape[-1])
    return lax.dot_general(
        flat_left, flat_right, (((0,), (0,)), ((), ())), preferred_element_type=jnp.float32
    )


def swap_cores(values):
    count = lax.axis_size("fsdp")
    return lax.ppermute(values, "fsdp", [(place, place ^ 1) for place in range(count)])


class Term(NamedTuple):
    left: int
    right: int
    rows: int
    row_from: int
    columns: int
    column_from: int
    split: bool
    way: int
    start: int
    out: int
    out_row: int
    out_column: int


def ring_place(chip, chips):
    return lax.div(chip, 2) + lax.rem(chip, 2) * (chips - 1 - 2 * lax.div(chip, 2))


def ring_chip(place, chips):
    upper = lax.div(place, (chips + 1) // 2)
    return 2 * place + upper * (2 * (chips - 1 - place) + 1 - 2 * place)


def reduce_body(terms, chips, lefts, rights, out_count, *refs):
    refs = list(refs)

    def take(count):
        taken = refs[:count]
        del refs[:count]
        return taken

    left_refs, right_refs = take(lefts), take(rights)
    outs = take(out_count)
    own_left, own_right = take(lefts), take(rights)
    sib_left, sib_right = take(lefts), take(rights)
    landing, final = take(len(terms)), take(len(terms))
    split_at = [number for number, term in enumerate(terms) if term.split]
    give, got = take(len(split_at)), take(len(split_at))
    load_sem, swap_send, swap_recv, ring_send, ring_recv = take(5)
    give_send, got_recv, final_send, final_recv = take(4)
    stage, stage_sem, share_send, share_recv = take(4)

    device = lax.axis_index("fsdp")
    plane = lax.axis_index("rep")
    core, chip = lax.rem(device, 2), lax.div(device, 2)
    place = ring_place(chip, chips)
    sibling = {"fsdp": device + 1 - 2 * core}
    twin = {"rep": 1 - plane}
    ways = [
        {"fsdp": 2 * ring_chip(lax.rem(place + step, chips), chips) + core}
        for step in (1, chips - 1)
    ]

    barrier = pltpu.get_barrier_semaphore()
    partners = (ways[0], ways[1], sibling, twin)
    for partner in partners:
        pl.semaphore_signal(barrier, inc=1, device_id=partner, device_id_type=MESH)
    pl.semaphore_wait(barrier, len(partners))

    def remote(source, target, send_sem, recv_sem, partner):
        return pltpu.make_async_remote_copy(
            src_ref=source,
            dst_ref=target,
            send_sem=send_sem,
            recv_sem=recv_sem,
            device_id=partner,
            device_id_type=MESH,
        )

    loads, swaps = {}, {}
    for number in range(lefts):
        ref = left_refs[number]
        by_rows = len(ref.shape) == 4
        mine = ref.at[:, core] if by_rows else ref
        other = ref.at[:, 1 - core] if by_rows else ref
        loads["l", number] = pltpu.make_async_copy(mine, own_left[number], load_sem.at[number])
        swaps["l", number] = remote(
            other, sib_left[number], swap_send.at[number], swap_recv.at[number], sibling
        )
    for number in range(rights):
        ref, at = right_refs[number], lefts + number
        width = own_right[number].shape[1]
        if width == ref.shape[1]:
            mine = other = ref
        else:
            second = ref.shape[1] - width
            mine = ref.at[:, pl.ds(pl.multiple_of(core * second, 128), width)]
            other = ref.at[:, pl.ds(pl.multiple_of((1 - core) * second, 128), width)]
        loads["r", number] = pltpu.make_async_copy(mine, own_right[number], load_sem.at[at])
        swaps["r", number] = remote(
            other, sib_right[number], swap_send.at[at], swap_recv.at[at], sibling
        )
    first_use = {}
    for term in sorted(terms, key=lambda term: term.start - term.split):
        for key in (("l", term.left), ("r", term.right)):
            first_use.setdefault(key, term.start - term.split)
    for key in first_use:
        loads[key].start()
        swaps[key].start()
    for number, term in enumerate(terms):
        landing[number][0] = jnp.zeros(landing[number].shape[1:], jnp.bfloat16)

    def chunk(term, owner, part):
        rows = pl.ds(term.row_from, term.rows)
        from_column = term.column_from
        if term.split:
            from_column = pl.multiple_of(from_column + part * term.columns, 128)
        columns = pl.ds(from_column, term.columns)
        own = jnp.dot(
            own_left[term.left][owner, rows, :],
            own_right[term.right][:, columns],
            preferred_element_type=jnp.float32,
        )
        return own + jnp.dot(
            sib_left[term.left][owner, rows, :],
            sib_right[term.right][:, columns],
            preferred_element_type=jnp.float32,
        )

    def owner_at(term, hop):
        back = hop + 1 if term.way == 0 else 2 * chips - 1 - hop
        return ring_chip(lax.rem(place + 2 * chips - back, chips), chips)

    def give_copy(at, hop):
        return remote(
            give[at].at[lax.rem(hop, GIVE_SLOTS)],
            got[at].at[hop],
            give_send.at[at, hop],
            got_recv.at[at, hop],
            twin,
        )

    def ring_copy(number, hop):
        return remote(
            landing[number].at[hop],
            landing[number].at[hop + 1],
            ring_send.at[number, hop],
            ring_recv.at[number, hop + 1],
            ways[terms[number].way],
        )

    def arrival(number, hop):
        return remote(
            landing[number].at[hop],
            landing[number].at[hop],
            ring_send.at[number, hop],
            ring_recv.at[number, hop],
            ways[terms[number].way],
        )

    def final_copy(number):
        return remote(
            landing[number].at[chips - 1],
            final[number],
            final_send.at[number],
            final_recv.at[number],
            twin,
        )

    def step(clock, carry):
        for moment in sorted(set(first_use.values())):

            @pl.when(clock == moment)
            def _():
                for key, use in first_use.items():
                    if use == moment:
                        loads[key].wait()
                        swaps[key].wait_recv()

        for at, number in enumerate(split_at):
            term = terms[number]
            later = clock - term.start + 1

            @pl.when((later >= GIVE_SLOTS) & (later < chips))
            def _():
                give_copy(at, later - GIVE_SLOTS).wait_send()

            @pl.when((later >= 0) & (later < chips))
            def _():
                give[at][lax.rem(later, GIVE_SLOTS)] = chunk(term, owner_at(term, later), 1 - plane).astype(
                    jnp.bfloat16
                )
                give_copy(at, later).start()

        for number, term in enumerate(terms):
            hop = clock - term.start

            @pl.when((hop >= 0) & (hop < chips))
            def _():
                total = chunk(term, owner_at(term, hop), plane)
                if term.split:
                    at = split_at.index(number)
                    give_copy(at, hop).wait_recv()
                    total = total + got[at][hop].astype(jnp.float32)

                @pl.when(hop > 0)
                def _():
                    arrival(number, hop).wait_recv()

                landing[number][hop] = (
                    total + landing[number][hop].astype(jnp.float32)
                ).astype(jnp.bfloat16)

                @pl.when(hop < chips - 1)
                def _():
                    ring_copy(number, hop).start()

                @pl.when(hop == chips - 1)
                def _():
                    final_copy(number).start()

        return carry

    lax.fori_loop(0, max(term.start for term in terms) + chips, step, 0)
    stores, shares = [], []

    def store(term, values, from_column):
        slot = len(stores) % 2
        if len(stores) >= 2:
            stores[-2]()
        stage[slot, : term.rows, : term.columns] = values
        columns = pl.ds(from_column, term.columns)
        if len(left_refs[term.left].shape) == 4:
            copy = pltpu.make_async_copy(
                stage.at[slot, pl.ds(0, term.rows), pl.ds(0, term.columns)],
                outs[term.out].at[0, pl.ds(term.out_row, term.rows), columns],
                stage_sem.at[slot],
            )
            copy.start()
            stores.append(copy.wait)
            return
        half = term.rows // 2

        def rows_of(owner):
            return stage.at[
                slot, pl.ds(pl.multiple_of(owner * half, 8), half), pl.ds(0, term.columns)
            ]

        target = outs[term.out].at[core, :, columns]
        copy = pltpu.make_async_copy(rows_of(core), target, stage_sem.at[slot])
        at = len(shares)
        share = remote(
            rows_of(1 - core), target, share_send.at[at], share_recv.at[at], sibling
        )
        copy.start()
        share.start()

        def settle_store():
            copy.wait()
            share.wait_send()

        stores.append(settle_store)
        arrived = outs[term.out].at[1 - core, :, columns]
        shares.append(remote(arrived, arrived, share_send.at[at], share_recv.at[at], sibling))

    for number, term in enumerate(terms):
        final_copy(number).wait()
        mine = landing[number][chips - 1].astype(jnp.float32)
        other = final[number][...].astype(jnp.float32)
        if term.split:
            for part, values in ((plane, mine), (1 - plane, other)):
                from_column = term.out_column + part * term.columns
                store(term, values, pl.multiple_of(from_column, 128))
        else:
            store(term, mine + other, term.out_column)
    for settle_store in stores[-2:]:
        settle_store()
    for share in shares:
        share.wait_recv()

    def settle(hop, carry):
        for number in range(len(terms)):

            @pl.when(hop < chips - 1)
            def _():
                ring_copy(number, hop).wait_send()

        for at in range(len(split_at)):

            @pl.when(hop >= chips - GIVE_SLOTS)
            def _():
                give_copy(at, hop).wait_send()

        return carry

    lax.fori_loop(0, chips, settle, 0)
    for key in first_use:
        swaps[key].wait_send()


def core_columns(columns):
    return -(-columns // 256) * 128


def reduce_terms(terms, lefts, rights, identity):
    chips = lefts[0].shape[0]
    whole = {term.right for term in terms if lefts[term.left].ndim == 4}
    left_parts = [
        (left.shape[0],) + left.shape[-2:] for left in lefts
    ]
    right_parts = [
        (right.shape[0], right.shape[1] if number in whole else core_columns(right.shape[1]))
        for number, right in enumerate(rights)
    ]

    def vmem(shape):
        return pltpu.VMEM(shape, jnp.bfloat16)

    splits = [term for term in terms if term.split]
    operands = len(lefts) + len(rights)
    scratch = (
        [vmem(shape) for shape in left_parts + right_parts] * 2
        + [vmem((chips, term.rows, term.columns)) for term in terms]
        + [vmem((term.rows, term.columns)) for term in terms]
        + [vmem((GIVE_SLOTS, term.rows, term.columns)) for term in splits]
        + [vmem((chips, term.rows, term.columns)) for term in splits]
        + [pltpu.SemaphoreType.DMA((operands,))] * 3
        + [pltpu.SemaphoreType.DMA((len(terms), chips))] * 2
        + [pltpu.SemaphoreType.DMA((len(splits), chips))] * 2
        + [pltpu.SemaphoreType.DMA((len(terms),))] * 2
        + [
            pltpu.VMEM(
                (2, max(term.rows for term in terms), max(term.columns for term in terms)),
                jnp.float32,
            ),
            pltpu.SemaphoreType.DMA((2,)),
        ]
        + [pltpu.SemaphoreType.DMA((len(terms) + len(splits),))] * 2
    )
    heights, widths, halves = {}, {}, {}
    for term in terms:
        out, width = term.out, term.columns * (1 + term.split)
        halves[out] = 1 if lefts[term.left].ndim == 4 else 2
        heights[out] = max(heights.get(out, 0), (term.out_row + term.rows) // halves[out])
        widths[out] = max(widths.get(out, 0), term.out_column + width)
    return pl.pallas_call(
        partial(reduce_body, terms, chips, len(lefts), len(rights), len(heights)),
        out_shape=[
            jax.ShapeDtypeStruct((halves[out], heights[out], widths[out]), jnp.float32)
            for out in range(len(heights))
        ],
        in_specs=[pl.BlockSpec(memory_space=pl.ANY)] * operands,
        out_specs=[pl.BlockSpec(memory_space=pl.ANY)] * len(heights),
        scratch_shapes=scratch,
        compiler_params=pltpu.CompilerParams(
            collective_id=identity, has_side_effects=True, vmem_limit_bytes=62 * 1024 * 1024
        ),
    )(*lefts, *rights)


class Piece(NamedTuple):
    source: int
    rows: int
    columns: int
    row_core: int
    row_plane: int
    column_from: int
    column_core: int
    column_plane: int
    split: bool
    long_way: int


def gather_body(pieces, chips, count, *refs):
    sources, (tiles, weights) = refs[:count], refs[count : count + 2]
    outs, products = refs[count + 2 : 2 * count + 2], refs[2 * count + 2]
    refs = refs[2 * count + 3 :]
    ring_send, ring_recv, pass_send, pass_recv, twin_send, twin_recv, own_sem = refs[:7]
    met, partial_rows, met_rows, tile_send, tile_recv, row_send, row_recv = refs[7:]
    device = lax.axis_index("fsdp")
    plane = lax.axis_index("rep")
    core, chip = lax.rem(device, 2), lax.div(device, 2)
    place = ring_place(chip, chips)
    sibling = {"fsdp": device + 1 - 2 * core}
    twin = {"rep": 1 - plane}

    def chip_back(way, hops):
        back = hops if way == 0 else chips - hops
        return ring_chip(lax.rem(place + chips - back, chips), chips)

    ways = [{"fsdp": 2 * chip_back(1 - way, 1) + core} for way in range(2)]

    barrier = pltpu.get_barrier_semaphore()
    peers = [lax.rem(device + step, 2 * chips) for step in range(1, 2 * chips)]
    partners = [{"fsdp": peer} for peer in peers] + [twin]
    for partner in partners:
        pl.semaphore_signal(barrier, inc=1, device_id=partner, device_id_type=MESH)
    pl.semaphore_wait(barrier, len(partners))

    keep = [
        pltpu.make_async_copy(
            sources[number],
            outs[number].at[
                pl.ds(
                    pl.multiple_of(chip * sources[number].shape[0], 16), sources[number].shape[0]
                ),
                :,
            ],
            own_sem.at[number],
        )
        for number in range(count)
    ]
    for copy in keep:
        copy.start()

    def window(piece, ref, base, of_core, of_plane):
        row = base + of_core * piece.row_core + of_plane * piece.row_plane
        column = (
            piece.column_from + of_core * piece.column_core + of_plane * piece.column_plane
        )
        return ref.at[
            pl.ds(pl.multiple_of(row, 16), piece.rows),
            pl.ds(pl.multiple_of(column, 128), piece.columns),
        ]

    def landed(number, owner, of_core, of_plane):
        piece = pieces[number]
        height = sources[piece.source].shape[0]
        return window(piece, outs[piece.source], owner * height, of_core, of_plane)

    def remote(source, target, sems, index, partner):
        return pltpu.make_async_remote_copy(
            src_ref=source,
            dst_ref=target,
            send_sem=sems[0].at[index],
            recv_sem=sems[1].at[index],
            device_id=partner,
            device_id_type=MESH,
        )

    hops = [
        [chips // 2 if piece.long_way == way else (chips - 1) // 2 for way in range(2)]
        for piece in pieces
    ]
    splits = [number for number, piece in enumerate(pieces) if piece.split]
    sent = []

    def send(copy):
        copy.start()
        sent.append(copy)

    for number, piece in enumerate(pieces):
        for way in range(2):
            send(
                remote(
                    window(piece, sources[piece.source], 0, core, plane),
                    landed(number, chip, core, plane),
                    (ring_send, ring_recv),
                    (number, way, 0),
                    ways[way],
                )
            )

    def spread(target, sems, step):
        peer = peers[step]
        return remote(target[0].at[peer], target[1].at[step], sems, step, {"fsdp": peer})

    tile_sems, row_sems = (tile_send, tile_recv), (row_send, row_recv)
    steps = range(len(peers))
    for step in steps:
        send(spread((tiles, met), tile_sems, step))

    def ring_arrivals(hop):
        for number, piece in enumerate(pieces):
            for way in range(2):
                if hop > hops[number][way]:
                    continue
                block = landed(number, chip_back(way, hop), core, plane)
                remote(
                    block, block, (ring_send, ring_recv), (number, way, hop - 1), ways[way]
                ).wait_recv()
                if hop < hops[number][way]:
                    send(
                        remote(
                            block, block, (ring_send, ring_recv), (number, way, hop), ways[way]
                        )
                    )
                send(
                    remote(
                        block, block, (pass_send, pass_recv), (number, way, hop - 1), sibling
                    )
                )
                if piece.split:
                    at = splits.index(number)
                    send(
                        remote(block, block, (twin_send, twin_recv), (at, way, hop - 1), twin)
                    )

    def twin_arrivals(hop):
        for at, number in enumerate(splits):
            for way in range(2):
                if hop > hops[number][way]:
                    continue
                block = landed(number, chip_back(way, hop), core, 1 - plane)
                remote(
                    block, block, (twin_send, twin_recv), (at, way, hop - 1), twin
                ).wait_recv()
                send(
                    remote(
                        block,
                        block,
                        (pass_send, pass_recv),
                        (len(pieces) + at, way, hop - 1),
                        sibling,
                    )
                )

    ring_arrivals(1)
    for step in steps:
        spread((tiles, met), tile_sems, step).wait_recv()
    low = jnp.concatenate([met[step, :1, :] for step in steps] + [tiles[device, :1, :]])
    partial = jnp.dot(
        low.astype(jnp.bfloat16), weights[...], preferred_element_type=jnp.float32
    )
    for step in steps:
        sender = lax.rem(device + 2 * chips - 1 - step, 2 * chips)
        for at in range(partial_rows.shape[1]):
            partial_rows[sender, pl.ds(at, 1), :] = partial[
                step : step + 1, 128 * at : 128 * (at + 1)
            ]
    for step in steps:
        send(spread((partial_rows, met_rows), row_sems, step))

    for hop in range(2, chips // 2 + 1):
        ring_arrivals(hop)
        twin_arrivals(hop - 1)
    twin_arrivals(chips // 2)
    for number in range(len(pieces) + len(splits)):
        at = number if number < len(pieces) else splits[number - len(pieces)]
        of_plane = plane if number < len(pieces) else 1 - plane
        for way in range(2):
            for hop in range(1, hops[at][way] + 1):
                block = landed(at, chip_back(way, hop), 1 - core, of_plane)
                remote(
                    block, block, (pass_send, pass_recv), (number, way, hop - 1), sibling
                ).wait_recv()
    total = jnp.concatenate(
        [
            partial[len(peers) :, 128 * at : 128 * (at + 1)]
            for at in range(partial_rows.shape[1])
        ]
    )
    for step in steps:
        spread((partial_rows, met_rows), row_sems, step).wait_recv()
        total = total + met_rows[step]
    products[...] = total
    for copy in sent:
        copy.wait_send()
    for copy in keep:
        copy.wait()


def gather_pieces(pieces, sources, tiles, weights, identity):
    chips = lax.axis_size("fsdp") // 2
    splits = sum(piece.split for piece in pieces)
    hops = chips // 2
    peers = 2 * chips - 1
    lines = weights.shape[1] // 128

    def sems(number):
        return [pltpu.SemaphoreType.DMA((number, 2, hops))] * 2

    return pl.pallas_call(
        partial(gather_body, pieces, chips, len(sources)),
        out_shape=[
            jax.ShapeDtypeStruct((chips * source.shape[0], source.shape[1]), source.dtype)
            for source in sources
        ]
        + [jax.ShapeDtypeStruct((lines, 128), jnp.float32)],
        in_specs=[pl.BlockSpec(memory_space=pl.ANY)] * len(sources)
        + [pl.BlockSpec(memory_space=pltpu.VMEM)] * 2,
        out_specs=[pl.BlockSpec(memory_space=pl.ANY)] * len(sources)
        + [pl.BlockSpec(memory_space=pltpu.VMEM)],
        scratch_shapes=sems(len(pieces))
        + sems(len(pieces) + splits)
        + sems(splits)
        + [pltpu.SemaphoreType.DMA((len(sources),))]
        + [
            pltpu.VMEM((peers, 8, 128), jnp.float32),
            pltpu.VMEM((2 * chips, lines, 128), jnp.float32),
            pltpu.VMEM((peers, lines, 128), jnp.float32),
        ]
        + [pltpu.SemaphoreType.DMA((peers,))] * 4,
        compiler_params=pltpu.CompilerParams(
            collective_id=identity, has_side_effects=True, vmem_limit_bytes=32 * 1024 * 1024
        ),
    )(*sources, tiles, weights)


def chip_rows(shard):
    other = swap_cores(shard)
    core = lax.axis_index("fsdp") % 2
    return jnp.where(
        core == 0, jnp.concatenate([shard, other]), jnp.concatenate([other, shard])
    )


def by_chip(values):
    chips = lax.axis_size("fsdp") // 2
    return values.T.reshape(chips, -1, values.shape[0])


def by_device(turned):
    chips = lax.axis_size("fsdp") // 2
    return turned.reshape(chips, 2, -1, turned.shape[1])


def join_cores(both, columns):
    joined, at = [], 0
    for width in columns:
        end = at + core_columns(width)
        twice = 2 * core_columns(width) - width
        joined += [both[0, :, at:end], both[1, :, at + twice : end]]
        at = end
    return joined


def plain_sum(left, right):
    total = lax.psum_scatter(
        outer_rows(left, right).astype(jnp.bfloat16), "fsdp", scatter_dimension=0, tiled=True
    )
    return lax.psum(total.astype(jnp.float32), "rep")


def kernels_fit(rows):
    return 2 * rows % 16 == 0 and lax.axis_size("rep") == 2


def sum_grads(factors, first=None, second=None, third=None, identity=0):
    (normed, attended, mixed, active), (triple_grad, branch_grad, pre_grad, feed_grad) = factors
    count = lax.axis_size("fsdp")
    rows = MODEL_WIDTH // count
    extra = [pair for pair in (first, second, third) if pair is not None]
    if not kernels_fit(rows):
        wide = [
            plain_sum(left.reshape(-1, left.shape[-1]).T, right)
            for left, right in zip((normed, attended, mixed, active), factors[1])
        ]
        return (wide[:3], wide[3], [plain_sum(*pair) for pair in extra])
    triple_half = core_columns(triple_grad.shape[1])
    branch_half = core_columns(branch_grad.shape[1])
    pre_half = core_columns(pre_grad.shape[1])
    plain_part = 8 * 128
    pre_part = (pre_half - plain_part) // 2
    deep_rows = active.shape[2] // 2
    pre_at = triple_half + branch_half
    terms = [
        Term(3, 3, deep_rows, 0, MODEL_WIDTH, 0, False, 0, 0, 1, 0, 0),
        Term(3, 3, deep_rows, deep_rows, MODEL_WIDTH, 0, False, 1, 0, 1, deep_rows, 0),
        Term(2, 2, 2 * rows, 0, pre_part, plain_part, True, 1, 2, 0, 0, pre_at + plain_part),
        Term(0, 0, 2 * rows, 0, triple_half // 2, 0, True, 0, 3, 0, 0, 0),
        Term(2, 2, 2 * rows, 0, plain_part, 0, False, 1, 4, 0, 0, pre_at),
        Term(1, 1, 2 * rows, 0, branch_half, 0, False, 0, 5, 0, 0, triple_half),
    ]
    lefts = [normed, attended, mixed, active]
    rights = [triple_grad, branch_grad, pre_grad, feed_grad]
    columns = []
    for pair, ways in ((first, "s"), (second, "ps"), (third, "p")):
        if pair is None:
            continue
        at, out = len(lefts), 2 + len(columns)
        lefts.append(by_chip(pair[0]))
        rights.append(pair[1])
        height, half = lefts[-1].shape[1], core_columns(pair[1].shape[1])
        if ways == "s":
            terms.append(Term(at, at, height, 0, half // 2, 0, True, 0, 1, out, 0, 0))
        elif ways == "p":
            terms.append(Term(at, at, height, 0, half, 0, False, 1, 1, out, 0, 0))
        else:
            half = half // 2
            terms.append(Term(at, at, height, 0, half, 0, False, 0, 1, out, 0, 0))
            terms.append(Term(at, at, height, 0, half // 2, half, True, 1, 3, out, 0, half))
        columns.append(pair[1].shape[1])
    outs = reduce_terms(tuple(terms), lefts, rights, identity)
    wide = join_cores(outs[0], [triple_grad.shape[1], branch_grad.shape[1], pre_grad.shape[1]])
    rest = [
        jnp.concatenate(join_cores(out, [width]), axis=1)
        for out, width in zip(outs[2:], columns)
    ]
    return (wide, outs[1][0], rest)


def pack_body(*refs):
    out, at = refs[-1], 0
    for ref in refs[:-1]:
        width = ref.shape[1]
        out[:, at : at + width] = ref[...].astype(jnp.bfloat16).astype(out.dtype)
        at += width


def pack_rows(pieces, dtype):
    rows = pieces[0].shape[0]
    width = sum(piece.shape[1] for piece in pieces)
    return pl.pallas_call(
        pack_body, out_shape=jax.ShapeDtypeStruct((rows, width), dtype)
    )(*pieces)


def gathered_terms(row):
    return lax.all_gather(row, ("fsdp", "rep"), axis=0, tiled=True)


def fetch_first(wide_weight, deep_shard, silu_low, block_bias, identity):
    rest = wide_weight[0, :, 6 * MODEL_WIDTH :].astype(jnp.bfloat16)
    low = deep_shard.astype(jnp.bfloat16)
    rows = rest.shape[0]
    count = lax.axis_size("fsdp")
    if kernels_fit(rows) and silu_low.shape[0] == 1 and rows <= 128:
        unit = MODEL_WIDTH
        deep_rows = low.shape[0] // 2
        pieces = (
            Piece(0, 2 * rows, unit, 0, 0, 0, 4 * unit, unit, True, 0),
            Piece(1, deep_rows, unit, 2 * deep_rows, deep_rows, 0, 0, 0, True, 1),
            Piece(0, 2 * rows, unit, 0, 0, 2 * unit, 4 * unit, unit, True, 1),
        )
        tiles = jnp.pad(
            silu_low.astype(jnp.float32).reshape(count, 1, rows),
            ((0, 0), (0, 7), (0, 128 - rows)),
        )
        weights = jnp.concatenate(
            [wide_weight[block, :, : 6 * unit].astype(jnp.bfloat16) for block in range(2)], axis=1
        )
        weights = jnp.pad(weights, ((0, 128 - rows), (0, 0)))
        whole, deep, products = gather_pieces(
            pieces, [chip_rows(rest), chip_rows(low)], tiles, weights, identity
        )
        products = products.reshape(2, 1, 6 * unit)
        modulations = [products[block] + block_bias[block, : 6 * unit] for block in range(2)]
    else:
        whole = lax.all_gather(rest, "fsdp", axis=0, tiled=True)
        deep = lax.all_gather(low, "fsdp", axis=0, tiled=True)
        modulations = plane_modulation(silu_low, wide_weight, block_bias)
    split = (
        whole[:, : 3 * MODEL_WIDTH],
        whole[:, 3 * MODEL_WIDTH : 4 * MODEL_WIDTH],
        whole[:, 4 * MODEL_WIDTH :],
        whole,
    )
    return (split, deep, modulations)


def fetch_block_and(wide_shard, deep_shard, other_shard):
    rest = jnp.concatenate(
        [wide_shard[:, 6 * MODEL_WIDTH :].astype(jnp.bfloat16), other_shard.astype(jnp.bfloat16)],
        axis=1,
    )
    whole = lax.all_gather(rest, "fsdp", axis=0, tiled=True)
    deep = lax.all_gather(deep_shard.astype(jnp.bfloat16), "fsdp", axis=0, tiled=True)
    end = whole.shape[1] - other_shard.shape[1]
    split = (
        whole[:, : 3 * MODEL_WIDTH],
        whole[:, 3 * MODEL_WIDTH : 4 * MODEL_WIDTH],
        whole[:, 4 * MODEL_WIDTH : end],
        whole,
    )
    return (split, deep, whole[:, end:])


def plane_modulation(silu_low, wide_weight, block_bias):
    count = lax.axis_size("fsdp")
    sequences = silu_low.shape[0]
    rows = wide_weight.shape[1]
    device = lax.axis_index("fsdp")
    spread = jnp.broadcast_to(
        silu_low.reshape(1, sequences, count, rows).transpose(2, 0, 1, 3)[:, 0],
        (count, sequences, rows),
    )
    met = lax.all_to_all(spread, "fsdp", 0, 0, tiled=True)
    met = met.reshape(count * sequences, rows)
    partial = [
        jnp.dot(
            met,
            wide_weight[block, :, : 6 * MODEL_WIDTH].astype(jnp.bfloat16),
            preferred_element_type=jnp.float32,
        )
        for block in range(2)
    ]
    partial = jnp.stack(partial, axis=1).reshape(count, sequences, 2, 6 * MODEL_WIDTH)
    back = lax.all_to_all(partial, "fsdp", 0, 0, tiled=True)
    total = jnp.sum(back, axis=0)
    return [total[:, block] + block_bias[block, : 6 * MODEL_WIDTH] for block in range(2)]


HEAD_WINDOW = 256


def head_window(head, width):
    first = head * HEAD_DIM
    at = min(first // 128 * 128, width - HEAD_WINDOW)
    lane = lax.broadcasted_iota(jnp.int32, (1, HEAD_WINDOW), 1)
    return at, (lane >= first - at) & (lane < first - at + HEAD_DIM)


def only(mine, values):
    return jnp.where(mine, values, jnp.zeros_like(values))


def against(left, right):
    return lax.dot_general(
        left, right, (((1,), (1,)), ((), ())), preferred_element_type=jnp.float32
    )


def attend_body(lengths_ref, triple_ref, attended_ref, log_ref, total_ref):
    tokens, width = attended_ref.shape
    length = lengths_ref[pl.program_id(0)]
    seen = lax.broadcasted_iota(jnp.int32, (tokens, 1), 0) < length
    total_ref[...] = jnp.zeros_like(total_ref)
    for head in range(HEADS):
        at, mine = head_window(head, width)
        window = pl.ds(at, HEAD_WINDOW)
        keys = only(mine, triple_ref[:, pl.ds(width + at, HEAD_WINDOW)])
        values = only(mine, triple_ref[:, pl.ds(2 * width + at, HEAD_WINDOW)])
        scores = against(keys, triple_ref[:, window]) * HEAD_DIM ** (-0.5)
        scores = jnp.where(seen, scores, masked_score)
        largest = jnp.max(scores, axis=0, keepdims=True)
        expanded = jnp.exp(scores - largest)
        sums = jnp.sum(expanded, axis=0, keepdims=True)
        weights = (expanded * (1.0 / sums)).astype(jnp.bfloat16)
        total_ref[:, window] += lax.dot_general(
            weights, values, (((0,), (0,)), ((), ())), preferred_element_type=jnp.float32
        )
        log_ref[head : head + 1, :] = largest + jnp.log(sums)
    attended_ref[...] = total_ref[...].astype(jnp.bfloat16)


def attention_forward(triple, lengths):
    sequences, tokens, columns = triple.shape
    width = columns // 3
    return pl.pallas_call(
        attend_body,
        grid=(sequences,),
        out_shape=[
            jax.ShapeDtypeStruct((sequences, tokens, width), jnp.bfloat16),
            jax.ShapeDtypeStruct((sequences, HEADS, tokens), jnp.float32),
        ],
        in_specs=[
            pl.BlockSpec(memory_space=pltpu.SMEM),
            pl.BlockSpec((None, tokens, columns), lambda number: (number, 0, 0)),
        ],
        out_specs=[
            pl.BlockSpec((None, tokens, width), lambda number: (number, 0, 0)),
            pl.BlockSpec((None, HEADS, tokens), lambda number: (number, 0, 0)),
        ],
        scratch_shapes=[pltpu.VMEM((tokens, width), jnp.float32)],
        compiler_params=pltpu.CompilerParams(vmem_limit_bytes=48 * 1024 * 1024),
    )(lengths, triple)


def attend_back_body(lengths_ref, triple_ref, log_ref, upstream_ref, grad_ref, total_ref):
    tokens, width = upstream_ref.shape
    length = lengths_ref[pl.program_id(0)]
    factor = HEAD_DIM ** (-0.5)
    seen = lax.broadcasted_iota(jnp.int32, (tokens, 1), 0) < length
    total_ref[...] = jnp.zeros_like(total_ref)
    for head in range(HEADS):
        at, mine = head_window(head, width)
        query_at, key_at, value_at = (
            pl.ds(group * width + at, HEAD_WINDOW) for group in range(3)
        )
        queries = only(mine, triple_ref[:, query_at])
        keys = only(mine, triple_ref[:, key_at])
        values = only(mine, triple_ref[:, value_at])
        upstream = only(mine, upstream_ref[:, pl.ds(at, HEAD_WINDOW)])
        scores = against(keys, queries) * factor
        chances = jnp.where(seen, jnp.exp(scores - log_ref[head : head + 1, :]), 0.0)
        chance_grad = against(values, upstream)
        centre = jnp.sum(chance_grad * chances, axis=0, keepdims=True)
        score_grad = (chances * (chance_grad - centre)).astype(jnp.bfloat16)
        total_ref[:, value_at] += jnp.dot(
            chances.astype(jnp.bfloat16), upstream, preferred_element_type=jnp.float32
        )
        total_ref[:, key_at] += factor * jnp.dot(
            score_grad, queries, preferred_element_type=jnp.float32
        )
        total_ref[:, query_at] += factor * lax.dot_general(
            score_grad, keys, (((0,), (0,)), ((), ())), preferred_element_type=jnp.float32
        )
    grad_ref[...] = total_ref[...].astype(jnp.bfloat16)


def attention_backward(triple, logs, upstream, lengths):
    sequences, tokens, columns = triple.shape

    def spec(width):
        return pl.BlockSpec((None, tokens, width), lambda number: (number, 0, 0))

    return pl.pallas_call(
        attend_back_body,
        grid=(sequences,),
        out_shape=jax.ShapeDtypeStruct((sequences, tokens, columns), jnp.bfloat16),
        in_specs=[
            pl.BlockSpec(memory_space=pltpu.SMEM),
            spec(columns),
            pl.BlockSpec((None, HEADS, tokens), lambda number: (number, 0, 0)),
            spec(columns // 3),
        ],
        out_specs=spec(columns),
        scratch_shapes=[pltpu.VMEM((tokens, columns), jnp.float32)],
        compiler_params=pltpu.CompilerParams(vmem_limit_bytes=48 * 1024 * 1024),
    )(lengths, triple, logs, upstream)


def rise_body(mixed_ref, weight_ref, bias_ref, pre_ref, active_ref, turned_ref):
    pre = (
        jnp.dot(mixed_ref[...], weight_ref[...], preferred_element_type=jnp.float32)
        + bias_ref[...]
    )
    active = gelu_tanh(pre).astype(jnp.bfloat16)
    pre_ref[...] = pre
    active_ref[...] = active
    turned_ref[...] = active.T


def rise(mixed, wide, bias):
    tokens, width = mixed.shape
    columns = bias.shape[1]
    tile = width
    return pl.pallas_call(
        rise_body,
        grid=(columns // tile,),
        in_specs=[
            pl.BlockSpec((tokens, width), lambda at: (0, 0)),
            pl.BlockSpec((width, tile), lambda at: (0, 4 + at)),
            pl.BlockSpec((1, tile), lambda at: (0, at)),
        ],
        out_specs=[
            pl.BlockSpec((tokens, tile), lambda at: (0, at)),
            pl.BlockSpec((tokens, tile), lambda at: (0, at)),
            pl.BlockSpec((tile, tokens), lambda at: (at, 0)),
        ],
        out_shape=[
            jax.ShapeDtypeStruct((tokens, columns), jnp.float32),
            jax.ShapeDtypeStruct((tokens, columns), jnp.bfloat16),
            jax.ShapeDtypeStruct((columns, tokens), jnp.bfloat16),
        ],
        compiler_params=pltpu.CompilerParams(vmem_limit_bytes=40 * 1024 * 1024),
    )(mixed, wide, bias)


def fall_body(active_ref, weight_ref, bias_ref, middle_ref, gate_ref, feed_ref, result_ref):
    @pl.when(pl.program_id(0) == 0)
    def _():
        feed_ref[...] = jnp.broadcast_to(bias_ref[...], feed_ref.shape)

    feed_ref[...] += jnp.dot(
        active_ref[...], weight_ref[...], preferred_element_type=jnp.float32
    )

    @pl.when(pl.program_id(0) == pl.num_programs(0) - 1)
    def _():
        result_ref[...] = middle_ref[...] + gate_ref[...] * feed_ref[...]


def fall(active, weight, bias, middle, gate):
    tokens, depth = active.shape
    width = weight.shape[1]
    tile = depth // 3
    whole = pl.BlockSpec((tokens, width), lambda at: (0, 0))
    row = pl.BlockSpec((1, width), lambda at: (0, 0))
    return pl.pallas_call(
        fall_body,
        grid=(depth // tile,),
        in_specs=[
            pl.BlockSpec((tokens, tile), lambda at: (0, at)),
            pl.BlockSpec((tile, width), lambda at: (at, 0)),
            row,
            whole,
            row,
        ],
        out_specs=[whole, whole],
        out_shape=[jax.ShapeDtypeStruct((tokens, width), jnp.float32)] * 2,
        compiler_params=pltpu.CompilerParams(vmem_limit_bytes=40 * 1024 * 1024),
    )(active, weight, bias, middle, gate)


def block_forward(hidden, modulation, wide_matrix, deep_matrix, bias, lengths):
    sequences = hidden.shape[0]
    offset_first, factor_first, gate_first, offset_second, factor_second, gate_second = (
        split_modulation(modulation)
    )
    normed_low = modulate(hidden, offset_first, factor_first).astype(jnp.bfloat16)
    triple_bias = jnp.concatenate(
        [
            bias[6 * MODEL_WIDTH : 7 * MODEL_WIDTH],
            jnp.zeros((MODEL_WIDTH,), jnp.float32),
            bias[7 * MODEL_WIDTH : 8 * MODEL_WIDTH],
        ]
    )
    triple = (
        jnp.dot(
            normed_low,
            wide_matrix[0],
            preferred_element_type=jnp.float32,
        )
        + triple_bias
    ).astype(jnp.bfloat16)
    attended_low, log_total = attention_forward(triple, lengths)
    branch = (
        jnp.dot(
            attended_low,
            wide_matrix[1],
            preferred_element_type=jnp.float32,
        )
        + bias[8 * MODEL_WIDTH : 9 * MODEL_WIDTH]
    )
    middle = hidden + gate_first * branch
    mixed_low = modulate(middle, offset_second, factor_second).astype(jnp.bfloat16)
    pre_bias = bias[None, 9 * MODEL_WIDTH : 9 * MODEL_WIDTH + FF]
    feed_bias = bias[None, 9 * MODEL_WIDTH + FF :]
    if sequences == 1:
        pre_active, active_low, active_turned = rise(mixed_low[0], wide_matrix[3], pre_bias)
        feed_out, result = fall(
            active_low, deep_matrix, feed_bias, middle[0], gate_second[0]
        )
        pre_active, active_low, feed_out, result = (
            pre_active[None],
            active_low[None],
            feed_out[None],
            result[None],
        )
    else:
        pre_active = (
            jnp.dot(mixed_low, wide_matrix[2], preferred_element_type=jnp.float32) + pre_bias
        )
        active_low = gelu_tanh(pre_active).astype(jnp.bfloat16)
        active_turned = active_low.reshape(-1, FF).T
        feed_out = (
            jnp.dot(active_low, deep_matrix, preferred_element_type=jnp.float32) + feed_bias
        )
        result = middle + gate_second * feed_out
    saved = (
        hidden,
        modulation,
        normed_low,
        triple,
        log_total,
        attended_low,
        branch,
        middle,
        mixed_low,
        pre_active,
        active_turned,
        feed_out,
    )
    return (result, saved)


def block_backward(upstream, saved, wide_matrix, deep_matrix, lengths):
    (
        hidden,
        modulation,
        normed_low,
        triple,
        log_total,
        attended_low,
        branch,
        middle,
        mixed_low,
        pre_active,
        active_turned,
        feed_out,
    ) = saved
    sequences = hidden.shape[0]
    offset_first, factor_first, gate_first, offset_second, factor_second, gate_second = (
        split_modulation(modulation)
    )
    feedforward_gradient = (upstream * gate_second).astype(jnp.bfloat16)
    gate_second_grad = jnp.sum(upstream * feed_out, axis=1, keepdims=True)
    activation_gradient = jnp.einsum(
        "xjn,mn->xjm", feedforward_gradient, deep_matrix, preferred_element_type=jnp.float32
    )
    preactivation_gradient = jax.vjp(gelu_tanh, pre_active)[1](activation_gradient)[0].astype(
        jnp.bfloat16
    )
    mixed_grad = jnp.einsum(
        "qvm,am->qva",
        preactivation_gradient,
        wide_matrix[2],
        preferred_element_type=jnp.float32,
    )
    second_back = jax.vjp(modulate, middle, offset_second, factor_second)[1]
    middle_part, offset_second_grad, factor_second_grad = second_back(mixed_grad)
    middle_grad = upstream + middle_part
    gate_first_grad = jnp.sum(middle_grad * branch, axis=1, keepdims=True)
    branch_gradient = (middle_grad * gate_first).astype(jnp.bfloat16)
    attended_grad = jnp.einsum(
        "tbr,ar->tba",
        branch_gradient,
        wide_matrix[1],
        preferred_element_type=jnp.float32,
    ).astype(jnp.bfloat16)
    triple_gradient = attention_backward(triple, log_total, attended_grad, lengths)
    normed_grad = jnp.einsum(
        "tbr,ar->tba",
        triple_gradient,
        wide_matrix[0],
        preferred_element_type=jnp.float32,
    )
    first_back = jax.vjp(modulate, hidden, offset_first, factor_first)[1]
    hidden_part, offset_first_grad, factor_first_grad = first_back(normed_grad)
    hidden_grad = middle_grad + hidden_part
    def column_sum(values):
        return jnp.sum(values, axis=(0, 1), dtype=jnp.float32, keepdims=True)[0]

    triple_sum = column_sum(triple_gradient)
    row_pieces = [
        piece.reshape(1, -1)
        for piece in (
            offset_first_grad,
            factor_first_grad,
            gate_first_grad,
            offset_second_grad,
            factor_second_grad,
            gate_second_grad,
        )
    ] + [
        triple_sum[:, :MODEL_WIDTH],
        triple_sum[:, 2 * MODEL_WIDTH :],
        column_sum(branch_gradient),
        column_sum(preactivation_gradient),
        column_sum(feedforward_gradient),
    ]

    def flat(values):
        return values.reshape(-1, values.shape[-1])

    entering = [by_chip(flat(values)) for values in (normed_low, attended_low, mixed_low)]
    entering.append(by_device(active_turned))
    returning = [
        flat(values)
        for values in (
            triple_gradient,
            branch_gradient,
            preactivation_gradient,
            feedforward_gradient,
        )
    ]
    factors = (entering, returning)
    return (hidden_grad, row_pieces, factors)


def adam_update(weight, grad, first, second, rate, decay):
    first_new = 0.9 * first + 0.1 * grad
    second_new = 0.999 * second + 0.001 * grad * grad
    first_hat = first_new / (1.0 - 0.9**STEP)
    second_hat = second_new / (1.0 - 0.999**STEP)
    updated = weight - rate * (first_hat / (jnp.sqrt(second_hat) + adam_epsilon) + decay * weight)
    return (first_new, second_new, updated)


def per_device(
    tokens,
    condition,
    lengths,
    targets,
    cotangent,
    wide_weight,
    deep_weight,
    head_first,
    head_second,
    block_bias,
    head_bias,
    wide_mean,
    deep_mean,
    head_first_mean,
    head_second_mean,
    block_bias_mean,
    head_bias_mean,
    wide_square,
    deep_square,
    head_first_square,
    head_second_square,
    block_bias_square,
    head_bias_square,
):
    sequences = condition.shape[0]
    hidden = tokens.astype(jnp.float32).reshape(sequences, SEQ_LEN, MODEL_WIDTH)
    silu_low = jax.nn.silu(condition.astype(jnp.float32)).astype(jnp.bfloat16)
    visible = jnp.arange(SEQ_LEN, dtype=jnp.int32)[None, :] < lengths[:, None]
    wide_early, deep_early, (modulation_early, modulation_late) = fetch_first(
        wide_weight, deep_weight[0], silu_low, block_bias, 3
    )
    tapped, saved_early = block_forward(
        hidden, modulation_early, wide_early, deep_early, block_bias[0], lengths
    )
    wide_late, deep_late, first_matrix = fetch_block_and(
        wide_weight[1], deep_weight[1], head_first
    )
    second_w = lax.all_gather(head_second.astype(jnp.bfloat16), "fsdp", axis=0, tiled=True)
    final, saved_late = block_forward(
        tapped, modulation_late, wide_late, deep_late, block_bias[1], lengths
    )
    raw_targets = targets.astype(jnp.float32).reshape(sequences, SEQ_LEN, PZ)
    target_unit = raw_targets * lax.rsqrt(
        jnp.sum(raw_targets * raw_targets, axis=-1, keepdims=True) + norm_epsilon
    )

    def alignment(values):
        unit = values * lax.rsqrt(jnp.sum(values * values, axis=-1, keepdims=True) + norm_epsilon)
        return jnp.sum(unit * target_unit, axis=-1)

    upstream = cotangent.astype(jnp.float32).reshape(sequences, SEQ_LEN, MODEL_WIDTH)
    late_input_grad, late_row, late_factors = block_backward(
        upstream, saved_late, wide_late, deep_late, lengths
    )
    tapped_low, late_input_grad, late_factors = lax.optimization_barrier(
        (tapped.astype(jnp.bfloat16), late_input_grad, late_factors)
    )
    first_pre = (
        jnp.dot(tapped_low, first_matrix, preferred_element_type=jnp.float32) + head_bias[:PH]
    )
    first_low = jax.nn.silu(first_pre).astype(jnp.bfloat16)
    second_pre = (
        jnp.dot(first_low, second_w[:, :PH], preferred_element_type=jnp.float32)
        + head_bias[PH : 2 * PH]
    )
    second_low = jax.nn.silu(second_pre).astype(jnp.bfloat16)
    projected = (
        jnp.dot(second_low, second_w[:, PH:], preferred_element_type=jnp.float32)
        + head_bias[2 * PH :]
    )
    projected_grad = jax.vjp(alignment, projected)[1](-repa_weight * visible.astype(jnp.float32))[
        0
    ].astype(jnp.bfloat16)
    second_act_grad = jnp.einsum(
        "slz,hz->slh", projected_grad, second_w[:, PH:], preferred_element_type=jnp.float32
    )
    second_grad = jax.vjp(jax.nn.silu, second_pre)[1](second_act_grad)[0].astype(jnp.bfloat16)
    first_act_grad = jnp.einsum(
        "slh,gh->slg", second_grad, second_w[:, :PH], preferred_element_type=jnp.float32
    )
    first_gradient = jax.vjp(jax.nn.silu, first_pre)[1](first_act_grad)[0].astype(jnp.bfloat16)
    tapped_gradient = jnp.einsum(
        "ejk,rk->ejr", first_gradient, first_matrix, preferred_element_type=jnp.float32
    )

    def column_sum(values):
        return jnp.sum(values, axis=(0, 1), dtype=jnp.float32, keepdims=True)[0]

    def flat(values):
        return values.reshape(-1, values.shape[-1])

    late_packed = pack_rows(
        [silu_low]
        + late_row
        + [column_sum(first_gradient), column_sum(second_grad), column_sum(projected_grad)],
        jnp.float32,
    )
    late_packed, late_input_grad = lax.optimization_barrier((late_packed, late_input_grad))
    late_rows = gathered_terms(late_packed)
    input_grad, early_row, early_factors = block_backward(
        late_input_grad + tapped_gradient, saved_early, wide_early, deep_early, lengths
    )
    early_packed = pack_rows(early_row, jnp.float32)
    first_pair = [flat(tapped_low), flat(first_gradient)]
    second_pair = [flat(first_low), flat(second_grad)]
    third_pair = [flat(second_low), flat(projected_grad)]
    early_packed, early_factors, late_factors, second_pair = lax.optimization_barrier(
        (early_packed, early_factors, late_factors, second_pair)
    )
    early_rows = gathered_terms(early_packed)
    late_wide_grad, late_deep_grad, (first_weight_grad, third_weight_grad) = sum_grads(
        late_factors, first=first_pair, third=third_pair, identity=0
    )
    early_rows, early_factors, late_deep_grad = lax.optimization_barrier(
        (early_rows, early_factors, late_deep_grad)
    )
    early_wide_grad, early_deep_grad, (second_weight_grad,) = sum_grads(
        early_factors, second=second_pair, identity=1
    )
    second_weight_grad = jnp.concatenate([second_weight_grad, third_weight_grad], axis=1)
    own_silu = lax.dynamic_slice_in_dim(
        late_rows,
        lax.axis_index("fsdp") * wide_weight.shape[1],
        wide_weight.shape[1],
        axis=1,
    ).astype(jnp.bfloat16)
    late_rows = late_rows[:, MODEL_WIDTH:]
    bias_width = block_bias.shape[1]

    def modulation_weight_grad(rows):
        return lax.dot_general(
            own_silu,
            rows[:, : 6 * MODEL_WIDTH].astype(jnp.bfloat16),
            (((0,), (0,)), ((), ())),
            preferred_element_type=jnp.float32,
        )

    wide_grad = jnp.stack(
        [
            jnp.concatenate(
                [modulation_weight_grad(early_rows)] + early_wide_grad,
                axis=1,
            ),
            jnp.concatenate(
                [modulation_weight_grad(late_rows)] + late_wide_grad,
                axis=1,
            ),
        ]
    )
    deep_grad = jnp.stack([early_deep_grad, late_deep_grad])
    late_sum = jnp.sum(late_rows, axis=0, dtype=jnp.float32)
    early_sum = jnp.sum(early_rows, axis=0, dtype=jnp.float32)
    block_bias_grad = jnp.stack([early_sum, late_sum[:bias_width]])
    head_bias_total = late_sum[bias_width:]
    wide_m, wide_v, wide_new = adam_update(
        wide_weight, wide_grad, wide_mean, wide_square, matrix_rate, matrix_decay
    )
    deep_m, deep_v, deep_new = adam_update(
        deep_weight, deep_grad, deep_mean, deep_square, matrix_rate, matrix_decay
    )
    first_m, first_v, first_new = adam_update(
        head_first, first_weight_grad, head_first_mean, head_first_square, matrix_rate, matrix_decay
    )
    second_m, second_v, second_new = adam_update(
        head_second,
        second_weight_grad,
        head_second_mean,
        head_second_square,
        matrix_rate,
        matrix_decay,
    )
    bias_m, bias_v, bias_new = adam_update(
        block_bias, block_bias_grad, block_bias_mean, block_bias_square, bias_rate, 0.0
    )
    hbias_m, hbias_v, hbias_new = adam_update(
        head_bias, head_bias_total, head_bias_mean, head_bias_square, bias_rate, 0.0
    )
    output = final.reshape(sequences * SEQ_LEN, MODEL_WIDTH).astype(jnp.bfloat16)
    input_flat = input_grad.reshape(sequences * SEQ_LEN, MODEL_WIDTH)
    return (
        output,
        input_flat,
        wide_grad,
        deep_grad,
        first_weight_grad,
        second_weight_grad,
        block_bias_grad,
        head_bias_total,
        wide_m,
        deep_m,
        first_m,
        second_m,
        bias_m,
        hbias_m,
        wide_v,
        deep_v,
        first_v,
        second_v,
        bias_v,
        hbias_v,
        wide_new,
        deep_new,
        first_new,
        second_new,
        bias_new,
        hbias_new,
    )


def solution(mesh):
    in_specs = (
        P(("fsdp", "rep"), None),
        P(("fsdp", "rep"), None),
        P(("fsdp", "rep")),
        P(("fsdp", "rep"), None),
        P(("fsdp", "rep"), None),
        P(None, "fsdp", None),
        P(None, "fsdp", None),
        P("fsdp", None),
        P("fsdp", None),
        P(),
        P(),
        P(None, "fsdp", None),
        P(None, "fsdp", None),
        P("fsdp", None),
        P("fsdp", None),
        P(),
        P(),
        P(None, "fsdp", None),
        P(None, "fsdp", None),
        P("fsdp", None),
        P("fsdp", None),
        P(),
        P(),
    )
    out_specs = (
        P(("fsdp", "rep"), None),
        P(("fsdp", "rep"), None),
        P(None, "fsdp", None),
        P(None, "fsdp", None),
        P("fsdp", None),
        P("fsdp", None),
        P(),
        P(),
        P(None, "fsdp", None),
        P(None, "fsdp", None),
        P("fsdp", None),
        P("fsdp", None),
        P(),
        P(),
        P(None, "fsdp", None),
        P(None, "fsdp", None),
        P("fsdp", None),
        P("fsdp", None),
        P(),
        P(),
        P(None, "fsdp", None),
        P(None, "fsdp", None),
        P("fsdp", None),
        P("fsdp", None),
        P(),
        P(),
    )
    return jax.shard_map(
        per_device, mesh=mesh, in_specs=in_specs, out_specs=out_specs, check_vma=False
    )
```

```python
from functools import partial
from typing import NamedTuple

import jax
import jax.numpy as jnp
from jax import lax
from jax.experimental import pallas as pl
from jax.experimental.pallas import tpu as pltpu
from jax.sharding import PartitionSpec as P

MESH = pl.DeviceIdType.MESH
GIVE_SLOTS = 3

MODEL_WIDTH = 1152
HEADS = 16
HEAD_DIM = 72
FF = 4608
PH = 2048
PZ = 768
SEQ_LEN = 448
STEP = 10


norm_epsilon = 1e-06
adam_epsilon = 1e-08
masked_score = -1e30
repa_weight = 0.5
matrix_rate = 0.05
bias_rate = 0.3
matrix_decay = 0.01


def normalize(values):
    centred = values - jnp.mean(values, axis=-1, keepdims=True)
    spread = jnp.mean(centred * centred, axis=-1, keepdims=True)
    return centred * lax.rsqrt(spread + norm_epsilon)


def modulate(values, offset, factor):
    return normalize(values) * (1.0 + factor) + offset


def gelu_tanh(values):
    return jax.nn.gelu(values, approximate=True)


def split_modulation(modulation):
    columns = modulation.shape[-1] // 6
    return [modulation[:, None, number * columns : (number + 1) * columns] for number in range(6)]


def outer_rows(left, right):
    flat_left = left.reshape(-1, left.shape[-1])
    flat_right = right.reshape(-1, right.shape[-1])
    return lax.dot_general(
        flat_left, flat_right, (((0,), (0,)), ((), ())), preferred_element_type=jnp.float32
    )


def swap_cores(values):
    count = lax.axis_size("fsdp")
    return lax.ppermute(values, "fsdp", [(place, place ^ 1) for place in range(count)])


class Term(NamedTuple):
    left: int
    right: int
    rows: int
    row_from: int
    columns: int
    column_from: int
    split: bool
    way: int
    start: int
    out: int
    out_row: int
    out_column: int


def ring_place(chip, chips):
    return lax.div(chip, 2) + lax.rem(chip, 2) * (chips - 1 - 2 * lax.div(chip, 2))


def ring_chip(place, chips):
    upper = lax.div(place, (chips + 1) // 2)
    return 2 * place + upper * (2 * (chips - 1 - place) + 1 - 2 * place)


def reduce_body(terms, chips, lefts, rights, out_count, *refs):
    refs = list(refs)

    def take(count):
        taken = refs[:count]
        del refs[:count]
        return taken

    left_refs, right_refs = take(lefts), take(rights)
    outs = take(out_count)
    own_left, own_right = take(lefts), take(rights)
    sib_left, sib_right = take(lefts), take(rights)
    landing, final = take(len(terms)), take(len(terms))
    split_at = [number for number, term in enumerate(terms) if term.split]
    give, got = take(len(split_at)), take(len(split_at))
    load_sem, swap_send, swap_recv, ring_send, ring_recv = take(5)
    give_send, got_recv, final_send, final_recv = take(4)
    stage, stage_sem, share_send, share_recv = take(4)

    device = lax.axis_index("fsdp")
    plane = lax.axis_index("rep")
    core, chip = lax.rem(device, 2), lax.div(device, 2)
    place = ring_place(chip, chips)
    sibling = {"fsdp": device + 1 - 2 * core}
    twin = {"rep": 1 - plane}
    ways = [
        {"fsdp": 2 * ring_chip(lax.rem(place + step, chips), chips) + core}
        for step in (1, chips - 1)
    ]

    barrier = pltpu.get_barrier_semaphore()
    partners = (ways[0], ways[1], sibling, twin)
    for partner in partners:
        pl.semaphore_signal(barrier, inc=1, device_id=partner, device_id_type=MESH)
    pl.semaphore_wait(barrier, len(partners))

    def remote(source, target, send_sem, recv_sem, partner):
        return pltpu.make_async_remote_copy(
            src_ref=source,
            dst_ref=target,
            send_sem=send_sem,
            recv_sem=recv_sem,
            device_id=partner,
            device_id_type=MESH,
        )

    loads, swaps = {}, {}
    for number in range(lefts):
        ref = left_refs[number]
        by_rows = len(ref.shape) == 4
        mine = ref.at[:, core] if by_rows else ref
        other = ref.at[:, 1 - core] if by_rows else ref
        loads["l", number] = pltpu.make_async_copy(mine, own_left[number], load_sem.at[number])
        swaps["l", number] = remote(
            other, sib_left[number], swap_send.at[number], swap_recv.at[number], sibling
        )
    for number in range(rights):
        ref, at = right_refs[number], lefts + number
        width = own_right[number].shape[1]
        if width == ref.shape[1]:
            mine = other = ref
        else:
            second = ref.shape[1] - width
            mine = ref.at[:, pl.ds(pl.multiple_of(core * second, 128), width)]
            other = ref.at[:, pl.ds(pl.multiple_of((1 - core) * second, 128), width)]
        loads["r", number] = pltpu.make_async_copy(mine, own_right[number], load_sem.at[at])
        swaps["r", number] = remote(
            other, sib_right[number], swap_send.at[at], swap_recv.at[at], sibling
        )
    first_use = {}
    for term in sorted(terms, key=lambda term: term.start - term.split):
        for key in (("l", term.left), ("r", term.right)):
            first_use.setdefault(key, term.start - term.split)
    for key in first_use:
        loads[key].start()
        swaps[key].start()
    for number, term in enumerate(terms):
        landing[number][0] = jnp.zeros(landing[number].shape[1:], jnp.bfloat16)

    def chunk(term, owner, part):
        rows = pl.ds(term.row_from, term.rows)
        from_column = term.column_from
        if term.split:
            from_column = pl.multiple_of(from_column + part * term.columns, 128)
        columns = pl.ds(from_column, term.columns)
        own = jnp.dot(
            own_left[term.left][owner, rows, :],
            own_right[term.right][:, columns],
            preferred_element_type=jnp.float32,
        )
        return own + jnp.dot(
            sib_left[term.left][owner, rows, :],
            sib_right[term.right][:, columns],
            preferred_element_type=jnp.float32,
        )

    def owner_at(term, hop):
        back = hop + 1 if term.way == 0 else 2 * chips - 1 - hop
        return ring_chip(lax.rem(place + 2 * chips - back, chips), chips)

    def give_copy(at, hop):
        return remote(
            give[at].at[lax.rem(hop, GIVE_SLOTS)],
            got[at].at[hop],
            give_send.at[at, hop],
            got_recv.at[at, hop],
            twin,
        )

    def ring_copy(number, hop):
        return remote(
            landing[number].at[hop],
            landing[number].at[hop + 1],
            ring_send.at[number, hop],
            ring_recv.at[number, hop + 1],
            ways[terms[number].way],
        )

    def arrival(number, hop):
        return remote(
            landing[number].at[hop],
            landing[number].at[hop],
            ring_send.at[number, hop],
            ring_recv.at[number, hop],
            ways[terms[number].way],
        )

    def final_copy(number):
        return remote(
            landing[number].at[chips - 1],
            final[number],
            final_send.at[number],
            final_recv.at[number],
            twin,
        )

    def step(clock, carry):
        for moment in sorted(set(first_use.values())):

            @pl.when(clock == moment)
            def _():
                for key, use in first_use.items():
                    if use == moment:
                        loads[key].wait()
                        swaps[key].wait_recv()

        for at, number in enumerate(split_at):
            term = terms[number]
            later = clock - term.start + 1

            @pl.when((later >= GIVE_SLOTS) & (later < chips))
            def _():
                give_copy(at, later - GIVE_SLOTS).wait_send()

            @pl.when((later >= 0) & (later < chips))
            def _():
                give[at][lax.rem(later, GIVE_SLOTS)] = chunk(term, owner_at(term, later), 1 - plane).astype(
                    jnp.bfloat16
                )
                give_copy(at, later).start()

        for number, term in enumerate(terms):
            hop = clock - term.start

            @pl.when((hop >= 0) & (hop < chips))
            def _():
                total = chunk(term, owner_at(term, hop), plane)
                if term.split:
                    at = split_at.index(number)
                    give_copy(at, hop).wait_recv()
                    total = total + got[at][hop].astype(jnp.float32)

                @pl.when(hop > 0)
                def _():
                    arrival(number, hop).wait_recv()

                landing[number][hop] = (
                    total + landing[number][hop].astype(jnp.float32)
                ).astype(jnp.bfloat16)

                @pl.when(hop < chips - 1)
                def _():
                    ring_copy(number, hop).start()

                @pl.when(hop == chips - 1)
                def _():
                    final_copy(number).start()

        return carry

    lax.fori_loop(0, max(term.start for term in terms) + chips, step, 0)
    stores, shares = [], []

    def store(term, values, from_column):
        slot = len(stores) % 2
        if len(stores) >= 2:
            stores[-2]()
        stage[slot, : term.rows, : term.columns] = values
        columns = pl.ds(from_column, term.columns)
        if len(left_refs[term.left].shape) == 4:
            copy = pltpu.make_async_copy(
                stage.at[slot, pl.ds(0, term.rows), pl.ds(0, term.columns)],
                outs[term.out].at[0, pl.ds(term.out_row, term.rows), columns],
                stage_sem.at[slot],
            )
            copy.start()
            stores.append(copy.wait)
            return
        half = term.rows // 2

        def rows_of(owner):
            return stage.at[
                slot, pl.ds(pl.multiple_of(owner * half, 8), half), pl.ds(0, term.columns)
            ]

        target = outs[term.out].at[core, :, columns]
        copy = pltpu.make_async_copy(rows_of(core), target, stage_sem.at[slot])
        at = len(shares)
        share = remote(
            rows_of(1 - core), target, share_send.at[at], share_recv.at[at], sibling
        )
        copy.start()
        share.start()

        def settle_store():
            copy.wait()
            share.wait_send()

        stores.append(settle_store)
        arrived = outs[term.out].at[1 - core, :, columns]
        shares.append(remote(arrived, arrived, share_send.at[at], share_recv.at[at], sibling))

    for number, term in enumerate(terms):
        final_copy(number).wait()
        mine = landing[number][chips - 1].astype(jnp.float32)
        other = final[number][...].astype(jnp.float32)
        if term.split:
            for part, values in ((plane, mine), (1 - plane, other)):
                from_column = term.out_column + part * term.columns
                store(term, values, pl.multiple_of(from_column, 128))
        else:
            store(term, mine + other, term.out_column)
    for settle_store in stores[-2:]:
        settle_store()
    for share in shares:
        share.wait_recv()

    def settle(hop, carry):
        for number in range(len(terms)):

            @pl.when(hop < chips - 1)
            def _():
                ring_copy(number, hop).wait_send()

        for at in range(len(split_at)):

            @pl.when(hop >= chips - GIVE_SLOTS)
            def _():
                give_copy(at, hop).wait_send()

        return carry

    lax.fori_loop(0, chips, settle, 0)
    for key in first_use:
        swaps[key].wait_send()


def core_columns(columns):
    return -(-columns // 256) * 128


def reduce_terms(terms, lefts, rights, identity):
    chips = lefts[0].shape[0]
    whole = {term.right for term in terms if lefts[term.left].ndim == 4}
    left_parts = [
        (left.shape[0],) + left.shape[-2:] for left in lefts
    ]
    right_parts = [
        (right.shape[0], right.shape[1] if number in whole else core_columns(right.shape[1]))
        for number, right in enumerate(rights)
    ]

    def vmem(shape):
        return pltpu.VMEM(shape, jnp.bfloat16)

    splits = [term for term in terms if term.split]
    operands = len(lefts) + len(rights)
    scratch = (
        [vmem(shape) for shape in left_parts + right_parts] * 2
        + [vmem((chips, term.rows, term.columns)) for term in terms]
        + [vmem((term.rows, term.columns)) for term in terms]
        + [vmem((GIVE_SLOTS, term.rows, term.columns)) for term in splits]
        + [vmem((chips, term.rows, term.columns)) for term in splits]
        + [pltpu.SemaphoreType.DMA((operands,))] * 3
        + [pltpu.SemaphoreType.DMA((len(terms), chips))] * 2
        + [pltpu.SemaphoreType.DMA((len(splits), chips))] * 2
        + [pltpu.SemaphoreType.DMA((len(terms),))] * 2
        + [
            pltpu.VMEM(
                (2, max(term.rows for term in terms), max(term.columns for term in terms)),
                jnp.float32,
            ),
            pltpu.SemaphoreType.DMA((2,)),
        ]
        + [pltpu.SemaphoreType.DMA((len(terms) + len(splits),))] * 2
    )
    heights, widths, halves = {}, {}, {}
    for term in terms:
        out, width = term.out, term.columns * (1 + term.split)
        halves[out] = 1 if lefts[term.left].ndim == 4 else 2
        heights[out] = max(heights.get(out, 0), (term.out_row + term.rows) // halves[out])
        widths[out] = max(widths.get(out, 0), term.out_column + width)
    return pl.pallas_call(
        partial(reduce_body, terms, chips, len(lefts), len(rights), len(heights)),
        out_shape=[
            jax.ShapeDtypeStruct((halves[out], heights[out], widths[out]), jnp.float32)
            for out in range(len(heights))
        ],
        in_specs=[pl.BlockSpec(memory_space=pl.ANY)] * operands,
        out_specs=[pl.BlockSpec(memory_space=pl.ANY)] * len(heights),
        scratch_shapes=scratch,
        compiler_params=pltpu.CompilerParams(
            collective_id=identity, has_side_effects=True, vmem_limit_bytes=62 * 1024 * 1024
        ),
    )(*lefts, *rights)


class Piece(NamedTuple):
    source: int
    rows: int
    columns: int
    row_core: int
    row_plane: int
    column_from: int
    column_core: int
    column_plane: int
    split: bool
    long_way: int


def gather_body(pieces, chips, count, *refs):
    sources, (tiles, weights) = refs[:count], refs[count : count + 2]
    outs, products = refs[count + 2 : 2 * count + 2], refs[2 * count + 2]
    refs = refs[2 * count + 3 :]
    ring_send, ring_recv, pass_send, pass_recv, twin_send, twin_recv, own_sem = refs[:7]
    met, partial_rows, met_rows, tile_send, tile_recv, row_send, row_recv = refs[7:]
    device = lax.axis_index("fsdp")
    plane = lax.axis_index("rep")
    core, chip = lax.rem(device, 2), lax.div(device, 2)
    place = ring_place(chip, chips)
    sibling = {"fsdp": device + 1 - 2 * core}
    twin = {"rep": 1 - plane}

    def chip_back(way, hops):
        back = hops if way == 0 else chips - hops
        return ring_chip(lax.rem(place + chips - back, chips), chips)

    ways = [{"fsdp": 2 * chip_back(1 - way, 1) + core} for way in range(2)]

    barrier = pltpu.get_barrier_semaphore()
    peers = [lax.rem(device + step, 2 * chips) for step in range(1, 2 * chips)]
    partners = [{"fsdp": peer} for peer in peers] + [twin]
    for partner in partners:
        pl.semaphore_signal(barrier, inc=1, device_id=partner, device_id_type=MESH)
    pl.semaphore_wait(barrier, len(partners))

    keep = [
        pltpu.make_async_copy(
            sources[number],
            outs[number].at[
                pl.ds(
                    pl.multiple_of(chip * sources[number].shape[0], 16), sources[number].shape[0]
                ),
                :,
            ],
            own_sem.at[number],
        )
        for number in range(count)
    ]
    for copy in keep:
        copy.start()

    def window(piece, ref, base, of_core, of_plane):
        row = base + of_core * piece.row_core + of_plane * piece.row_plane
        column = (
            piece.column_from + of_core * piece.column_core + of_plane * piece.column_plane
        )
        return ref.at[
            pl.ds(pl.multiple_of(row, 16), piece.rows),
            pl.ds(pl.multiple_of(column, 128), piece.columns),
        ]

    def landed(number, owner, of_core, of_plane):
        piece = pieces[number]
        height = sources[piece.source].shape[0]
        return window(piece, outs[piece.source], owner * height, of_core, of_plane)

    def remote(source, target, sems, index, partner):
        return pltpu.make_async_remote_copy(
            src_ref=source,
            dst_ref=target,
            send_sem=sems[0].at[index],
            recv_sem=sems[1].at[index],
            device_id=partner,
            device_id_type=MESH,
        )

    hops = [
        [chips // 2 if piece.long_way == way else (chips - 1) // 2 for way in range(2)]
        for piece in pieces
    ]
    splits = [number for number, piece in enumerate(pieces) if piece.split]
    sent = []

    def send(copy):
        copy.start()
        sent.append(copy)

    for number, piece in enumerate(pieces):
        for way in range(2):
            send(
                remote(
                    window(piece, sources[piece.source], 0, core, plane),
                    landed(number, chip, core, plane),
                    (ring_send, ring_recv),
                    (number, way, 0),
                    ways[way],
                )
            )

    def spread(target, sems, step):
        peer = peers[step]
        return remote(target[0].at[peer], target[1].at[step], sems, step, {"fsdp": peer})

    tile_sems, row_sems = (tile_send, tile_recv), (row_send, row_recv)
    steps = range(len(peers))
    for step in steps:
        send(spread((tiles, met), tile_sems, step))

    def ring_arrivals(hop):
        for number, piece in enumerate(pieces):
            for way in range(2):
                if hop > hops[number][way]:
                    continue
                block = landed(number, chip_back(way, hop), core, plane)
                remote(
                    block, block, (ring_send, ring_recv), (number, way, hop - 1), ways[way]
                ).wait_recv()
                if hop < hops[number][way]:
                    send(
                        remote(
                            block, block, (ring_send, ring_recv), (number, way, hop), ways[way]
                        )
                    )
                send(
                    remote(
                        block, block, (pass_send, pass_recv), (number, way, hop - 1), sibling
                    )
                )
                if piece.split:
                    at = splits.index(number)
                    send(
                        remote(block, block, (twin_send, twin_recv), (at, way, hop - 1), twin)
                    )

    def twin_arrivals(hop):
        for at, number in enumerate(splits):
            for way in range(2):
                if hop > hops[number][way]:
                    continue
                block = landed(number, chip_back(way, hop), core, 1 - plane)
                remote(
                    block, block, (twin_send, twin_recv), (at, way, hop - 1), twin
                ).wait_recv()
                send(
                    remote(
                        block,
                        block,
                        (pass_send, pass_recv),
                        (len(pieces) + at, way, hop - 1),
                        sibling,
                    )
                )

    ring_arrivals(1)
    for step in steps:
        spread((tiles, met), tile_sems, step).wait_recv()
    low = jnp.concatenate([met[step, :1, :] for step in steps] + [tiles[device, :1, :]])
    partial = jnp.dot(
        low.astype(jnp.bfloat16), weights[...], preferred_element_type=jnp.float32
    )
    for step in steps:
        sender = lax.rem(device + 2 * chips - 1 - step, 2 * chips)
        for at in range(partial_rows.shape[1]):
            partial_rows[sender, pl.ds(at, 1), :] = partial[
                step : step + 1, 128 * at : 128 * (at + 1)
            ]
    for step in steps:
        send(spread((partial_rows, met_rows), row_sems, step))

    for hop in range(2, chips // 2 + 1):
        ring_arrivals(hop)
        twin_arrivals(hop - 1)
    twin_arrivals(chips // 2)
    for number in range(len(pieces) + len(splits)):
        at = number if number < len(pieces) else splits[number - len(pieces)]
        of_plane = plane if number < len(pieces) else 1 - plane
        for way in range(2):
            for hop in range(1, hops[at][way] + 1):
                block = landed(at, chip_back(way, hop), 1 - core, of_plane)
                remote(
                    block, block, (pass_send, pass_recv), (number, way, hop - 1), sibling
                ).wait_recv()
    total = jnp.concatenate(
        [
            partial[len(peers) :, 128 * at : 128 * (at + 1)]
            for at in range(partial_rows.shape[1])
        ]
    )
    for step in steps:
        spread((partial_rows, met_rows), row_sems, step).wait_recv()
        total = total + met_rows[step]
    products[...] = total
    for copy in sent:
        copy.wait_send()
    for copy in keep:
        copy.wait()


def gather_pieces(pieces, sources, tiles, weights, identity):
    chips = lax.axis_size("fsdp") // 2
    splits = sum(piece.split for piece in pieces)
    hops = chips // 2
    peers = 2 * chips - 1
    lines = weights.shape[1] // 128

    def sems(number):
        return [pltpu.SemaphoreType.DMA((number, 2, hops))] * 2

    return pl.pallas_call(
        partial(gather_body, pieces, chips, len(sources)),
        out_shape=[
            jax.ShapeDtypeStruct((chips * source.shape[0], source.shape[1]), source.dtype)
            for source in sources
        ]
        + [jax.ShapeDtypeStruct((lines, 128), jnp.float32)],
        in_specs=[pl.BlockSpec(memory_space=pl.ANY)] * len(sources)
        + [pl.BlockSpec(memory_space=pltpu.VMEM)] * 2,
        out_specs=[pl.BlockSpec(memory_space=pl.ANY)] * len(sources)
        + [pl.BlockSpec(memory_space=pltpu.VMEM)],
        scratch_shapes=sems(len(pieces))
        + sems(len(pieces) + splits)
        + sems(splits)
        + [pltpu.SemaphoreType.DMA((len(sources),))]
        + [
            pltpu.VMEM((peers, 8, 128), jnp.float32),
            pltpu.VMEM((2 * chips, lines, 128), jnp.float32),
            pltpu.VMEM((peers, lines, 128), jnp.float32),
        ]
        + [pltpu.SemaphoreType.DMA((peers,))] * 4,
        compiler_params=pltpu.CompilerParams(
            collective_id=identity, has_side_effects=True, vmem_limit_bytes=32 * 1024 * 1024
        ),
    )(*sources, tiles, weights)


def chip_rows(shard):
    other = swap_cores(shard)
    core = lax.axis_index("fsdp") % 2
    return jnp.where(
        core == 0, jnp.concatenate([shard, other]), jnp.concatenate([other, shard])
    )


def by_chip(turned):
    chips = lax.axis_size("fsdp") // 2
    return turned.reshape(chips, -1, turned.shape[1])


def by_device(turned):
    chips = lax.axis_size("fsdp") // 2
    return turned.reshape(chips, 2, -1, turned.shape[1])


def join_cores(both, columns):
    joined, at = [], 0
    for width in columns:
        end = at + core_columns(width)
        twice = 2 * core_columns(width) - width
        joined += [both[0, :, at:end], both[1, :, at + twice : end]]
        at = end
    return joined


def plain_sum(left, right):
    total = lax.psum_scatter(
        outer_rows(left, right).astype(jnp.bfloat16), "fsdp", scatter_dimension=0, tiled=True
    )
    return lax.psum(total.astype(jnp.float32), "rep")


def kernels_fit(rows):
    return 2 * rows % 16 == 0 and lax.axis_size("rep") == 2


def sum_grads(factors, first=None, second=None, third=None, identity=0):
    (normed, attended, mixed, active), (triple_grad, branch_grad, pre_grad, feed_grad) = factors
    count = lax.axis_size("fsdp")
    rows = MODEL_WIDTH // count
    extra = [pair for pair in (first, second, third) if pair is not None]
    if not kernels_fit(rows):
        wide = [
            plain_sum(left.reshape(-1, left.shape[-1]).T, right)
            for left, right in zip((normed, attended, mixed, active), factors[1])
        ]
        return (wide[:3], wide[3], [plain_sum(left.T, right) for left, right in extra])
    triple_half = core_columns(triple_grad.shape[1])
    branch_half = core_columns(branch_grad.shape[1])
    pre_half = core_columns(pre_grad.shape[1])
    plain_part = 8 * 128
    pre_part = (pre_half - plain_part) // 2
    deep_rows = active.shape[2] // 2
    pre_at = triple_half + branch_half
    terms = [
        Term(3, 3, deep_rows, 0, MODEL_WIDTH, 0, False, 0, 0, 1, 0, 0),
        Term(3, 3, deep_rows, deep_rows, MODEL_WIDTH, 0, False, 1, 0, 1, deep_rows, 0),
        Term(2, 2, 2 * rows, 0, pre_part, plain_part, True, 1, 2, 0, 0, pre_at + plain_part),
        Term(0, 0, 2 * rows, 0, triple_half // 2, 0, True, 0, 3, 0, 0, 0),
        Term(2, 2, 2 * rows, 0, plain_part, 0, False, 1, 4, 0, 0, pre_at),
        Term(1, 1, 2 * rows, 0, branch_half, 0, False, 0, 5, 0, 0, triple_half),
    ]
    lefts = [normed, attended, mixed, active]
    rights = [triple_grad, branch_grad, pre_grad, feed_grad]
    columns = []
    for pair, ways in ((first, "s"), (second, "ps"), (third, "p")):
        if pair is None:
            continue
        at, out = len(lefts), 2 + len(columns)
        lefts.append(by_chip(pair[0]))
        rights.append(pair[1])
        height, half = lefts[-1].shape[1], core_columns(pair[1].shape[1])
        if ways == "s":
            terms.append(Term(at, at, height, 0, half // 2, 0, True, 0, 1, out, 0, 0))
        elif ways == "p":
            terms.append(Term(at, at, height, 0, half, 0, False, 1, 1, out, 0, 0))
        else:
            alike, split = half // 4, 3 * half // 8
            terms.append(Term(at, at, height, 0, alike, 0, False, 0, 1, out, 0, 0))
            terms.append(Term(at, at, height, 0, split, alike, True, 1, 3, out, 0, alike))
        columns.append(pair[1].shape[1])
    outs = reduce_terms(tuple(terms), lefts, rights, identity)
    wide = join_cores(outs[0], [triple_grad.shape[1], branch_grad.shape[1], pre_grad.shape[1]])
    rest = [
        jnp.concatenate(join_cores(out, [width]), axis=1)
        for out, width in zip(outs[2:], columns)
    ]
    return (wide, outs[1][0], rest)


def pack_body(*refs):
    out, at = refs[-1], 0
    for ref in refs[:-1]:
        width = ref.shape[1]
        out[:, at : at + width] = ref[...].astype(jnp.bfloat16).astype(out.dtype)
        at += width


def pack_rows(pieces, dtype):
    rows = pieces[0].shape[0]
    width = sum(piece.shape[1] for piece in pieces)
    return pl.pallas_call(
        pack_body, out_shape=jax.ShapeDtypeStruct((rows, width), dtype)
    )(*pieces)


def gathered_terms(row):
    return lax.all_gather(row, ("fsdp", "rep"), axis=0, tiled=True)


def fetch_first(wide_weight, deep_shard, silu_low, block_bias, identity):
    rest = wide_weight[0, :, 6 * MODEL_WIDTH :].astype(jnp.bfloat16)
    low = deep_shard.astype(jnp.bfloat16)
    rows = rest.shape[0]
    count = lax.axis_size("fsdp")
    if kernels_fit(rows) and silu_low.shape[0] == 1 and rows <= 128:
        unit = MODEL_WIDTH
        deep_rows = low.shape[0] // 2
        pieces = (
            Piece(0, 2 * rows, unit, 0, 0, 0, 4 * unit, unit, True, 0),
            Piece(1, deep_rows, unit, 2 * deep_rows, deep_rows, 0, 0, 0, True, 1),
            Piece(0, 2 * rows, unit, 0, 0, 2 * unit, 4 * unit, unit, True, 1),
        )
        tiles = jnp.pad(
            silu_low.astype(jnp.float32).reshape(count, 1, rows),
            ((0, 0), (0, 7), (0, 128 - rows)),
        )
        weights = jnp.concatenate(
            [wide_weight[block, :, : 6 * unit].astype(jnp.bfloat16) for block in range(2)], axis=1
        )
        weights = jnp.pad(weights, ((0, 128 - rows), (0, 0)))
        whole, deep, products = gather_pieces(
            pieces, [chip_rows(rest), chip_rows(low)], tiles, weights, identity
        )
        products = products.reshape(2, 1, 6 * unit)
        modulations = [products[block] + block_bias[block, : 6 * unit] for block in range(2)]
    else:
        whole = lax.all_gather(rest, "fsdp", axis=0, tiled=True)
        deep = lax.all_gather(low, "fsdp", axis=0, tiled=True)
        modulations = plane_modulation(silu_low, wide_weight, block_bias)
    split = (
        whole[:, : 3 * MODEL_WIDTH],
        whole[:, 3 * MODEL_WIDTH : 4 * MODEL_WIDTH],
        whole[:, 4 * MODEL_WIDTH :],
        whole,
    )
    return (split, deep, modulations)


def fetch_block_and(wide_shard, deep_shard, other_shard):
    rest = jnp.concatenate(
        [wide_shard[:, 6 * MODEL_WIDTH :].astype(jnp.bfloat16), other_shard.astype(jnp.bfloat16)],
        axis=1,
    )
    whole = lax.all_gather(rest, "fsdp", axis=0, tiled=True)
    deep = lax.all_gather(deep_shard.astype(jnp.bfloat16), "fsdp", axis=0, tiled=True)
    end = whole.shape[1] - other_shard.shape[1]
    split = (
        whole[:, : 3 * MODEL_WIDTH],
        whole[:, 3 * MODEL_WIDTH : 4 * MODEL_WIDTH],
        whole[:, 4 * MODEL_WIDTH : end],
        whole,
    )
    return (split, deep, whole, end)


def plane_modulation(silu_low, wide_weight, block_bias):
    count = lax.axis_size("fsdp")
    sequences = silu_low.shape[0]
    rows = wide_weight.shape[1]
    device = lax.axis_index("fsdp")
    spread = jnp.broadcast_to(
        silu_low.reshape(1, sequences, count, rows).transpose(2, 0, 1, 3)[:, 0],
        (count, sequences, rows),
    )
    met = lax.all_to_all(spread, "fsdp", 0, 0, tiled=True)
    met = met.reshape(count * sequences, rows)
    partial = [
        jnp.dot(
            met,
            wide_weight[block, :, : 6 * MODEL_WIDTH].astype(jnp.bfloat16),
            preferred_element_type=jnp.float32,
        )
        for block in range(2)
    ]
    partial = jnp.stack(partial, axis=1).reshape(count, sequences, 2, 6 * MODEL_WIDTH)
    back = lax.all_to_all(partial, "fsdp", 0, 0, tiled=True)
    total = jnp.sum(back, axis=0)
    return [total[:, block] + block_bias[block, : 6 * MODEL_WIDTH] for block in range(2)]


HEAD_WINDOW = 256


def head_window(head, width):
    first = head * HEAD_DIM
    at = min(first // 128 * 128, width - HEAD_WINDOW)
    lane = lax.broadcasted_iota(jnp.int32, (1, HEAD_WINDOW), 1)
    return at, (lane >= first - at) & (lane < first - at + HEAD_DIM)


def only(mine, values):
    return jnp.where(mine, values, jnp.zeros_like(values))


def against(left, right):
    return lax.dot_general(
        left, right, (((1,), (1,)), ((), ())), preferred_element_type=jnp.float32
    )


def attend_body(lengths_ref, triple_ref, attended_ref, log_ref, total_ref):
    tokens, width = attended_ref.shape
    length = lengths_ref[pl.program_id(0)]
    seen = lax.broadcasted_iota(jnp.int32, (tokens, 1), 0) < length
    total_ref[...] = jnp.zeros_like(total_ref)
    for head in range(HEADS):
        at, mine = head_window(head, width)
        window = pl.ds(at, HEAD_WINDOW)
        keys = only(mine, triple_ref[:, pl.ds(width + at, HEAD_WINDOW)])
        values = only(mine, triple_ref[:, pl.ds(2 * width + at, HEAD_WINDOW)])
        scores = against(keys, triple_ref[:, window]) * HEAD_DIM ** (-0.5)
        scores = jnp.where(seen, scores, masked_score)
        largest = jnp.max(scores, axis=0, keepdims=True)
        expanded = jnp.exp(scores - largest)
        sums = jnp.sum(expanded, axis=0, keepdims=True)
        weights = (expanded * (1.0 / sums)).astype(jnp.bfloat16)
        total_ref[:, window] += lax.dot_general(
            weights, values, (((0,), (0,)), ((), ())), preferred_element_type=jnp.float32
        )
        log_ref[head : head + 1, :] = largest + jnp.log(sums)
    attended_ref[...] = total_ref[...].astype(jnp.bfloat16)


def attention_forward(triple, lengths):
    sequences, tokens, columns = triple.shape
    width = columns // 3
    return pl.pallas_call(
        attend_body,
        grid=(sequences,),
        out_shape=[
            jax.ShapeDtypeStruct((sequences, tokens, width), jnp.bfloat16),
            jax.ShapeDtypeStruct((sequences, HEADS, tokens), jnp.float32),
        ],
        in_specs=[
            pl.BlockSpec(memory_space=pltpu.SMEM),
            pl.BlockSpec((None, tokens, columns), lambda number: (number, 0, 0)),
        ],
        out_specs=[
            pl.BlockSpec((None, tokens, width), lambda number: (number, 0, 0)),
            pl.BlockSpec((None, HEADS, tokens), lambda number: (number, 0, 0)),
        ],
        scratch_shapes=[pltpu.VMEM((tokens, width), jnp.float32)],
        compiler_params=pltpu.CompilerParams(vmem_limit_bytes=48 * 1024 * 1024),
    )(lengths, triple)


def attend_back_body(lengths_ref, triple_ref, log_ref, upstream_ref, grad_ref, total_ref):
    tokens, width = upstream_ref.shape
    length = lengths_ref[pl.program_id(0)]
    factor = HEAD_DIM ** (-0.5)
    seen = lax.broadcasted_iota(jnp.int32, (tokens, 1), 0) < length
    total_ref[...] = jnp.zeros_like(total_ref)
    for head in range(HEADS):
        at, mine = head_window(head, width)
        query_at, key_at, value_at = (
            pl.ds(group * width + at, HEAD_WINDOW) for group in range(3)
        )
        queries = only(mine, triple_ref[:, query_at])
        keys = only(mine, triple_ref[:, key_at])
        values = only(mine, triple_ref[:, value_at])
        upstream = only(mine, upstream_ref[:, pl.ds(at, HEAD_WINDOW)])
        scores = against(keys, queries) * factor
        chances = jnp.where(seen, jnp.exp(scores - log_ref[head : head + 1, :]), 0.0)
        chance_grad = against(values, upstream)
        centre = jnp.sum(chance_grad * chances, axis=0, keepdims=True)
        score_grad = (chances * (chance_grad - centre)).astype(jnp.bfloat16)
        total_ref[:, value_at] += jnp.dot(
            chances.astype(jnp.bfloat16), upstream, preferred_element_type=jnp.float32
        )
        total_ref[:, key_at] += factor * jnp.dot(
            score_grad, queries, preferred_element_type=jnp.float32
        )
        total_ref[:, query_at] += factor * lax.dot_general(
            score_grad, keys, (((0,), (0,)), ((), ())), preferred_element_type=jnp.float32
        )
    grad_ref[...] = total_ref[...].astype(jnp.bfloat16)


def attention_backward(triple, logs, upstream, lengths):
    sequences, tokens, columns = triple.shape

    def spec(width):
        return pl.BlockSpec((None, tokens, width), lambda number: (number, 0, 0))

    return pl.pallas_call(
        attend_back_body,
        grid=(sequences,),
        out_shape=jax.ShapeDtypeStruct((sequences, tokens, columns), jnp.bfloat16),
        in_specs=[
            pl.BlockSpec(memory_space=pltpu.SMEM),
            spec(columns),
            pl.BlockSpec((None, HEADS, tokens), lambda number: (number, 0, 0)),
            spec(columns // 3),
        ],
        out_specs=spec(columns),
        scratch_shapes=[pltpu.VMEM((tokens, columns), jnp.float32)],
        compiler_params=pltpu.CompilerParams(vmem_limit_bytes=48 * 1024 * 1024),
    )(lengths, triple, logs, upstream)


def rise_body(activation, low_ref, weight_ref, bias_ref, pre_ref, active_ref, turned_ref):
    pre = (
        jnp.dot(low_ref[...], weight_ref[...], preferred_element_type=jnp.float32)
        + bias_ref[...]
    )
    active = activation(pre).astype(jnp.bfloat16)
    pre_ref[...] = pre
    active_ref[...] = active
    turned_ref[...] = active.T


def rise(activation, low, weight, bias, tile, first):
    tokens, depth = low.shape
    columns = bias.shape[1]
    return pl.pallas_call(
        partial(rise_body, activation),
        grid=(columns // tile,),
        in_specs=[
            pl.BlockSpec((tokens, depth), lambda at: (0, 0)),
            pl.BlockSpec((depth, tile), lambda at: (0, first + at)),
            pl.BlockSpec((1, tile), lambda at: (0, at)),
        ],
        out_specs=[
            pl.BlockSpec((tokens, tile), lambda at: (0, at)),
            pl.BlockSpec((tokens, tile), lambda at: (0, at)),
            pl.BlockSpec((tile, tokens), lambda at: (at, 0)),
        ],
        out_shape=[
            jax.ShapeDtypeStruct((tokens, columns), jnp.float32),
            jax.ShapeDtypeStruct((tokens, columns), jnp.bfloat16),
            jax.ShapeDtypeStruct((columns, tokens), jnp.bfloat16),
        ],
        compiler_params=pltpu.CompilerParams(vmem_limit_bytes=40 * 1024 * 1024),
    )(low, weight, bias)


def sink_body(gradient_ref, weight_ref, pre_ref, out_ref, sum_ref):
    active_grad = against(gradient_ref[...], weight_ref[...])
    pre = pre_ref[...]
    scale, cubic = 0.7978845608028654, 0.044715
    bent = jnp.tanh(scale * (pre + cubic * pre * pre * pre))
    slope = 0.5 * (1.0 + bent) + 0.5 * pre * (1.0 - bent * bent) * scale * (
        1.0 + 3.0 * cubic * pre * pre
    )
    low = (active_grad * slope).astype(jnp.bfloat16)
    out_ref[...] = low
    sum_ref[...] = jnp.sum(low.astype(jnp.float32), axis=0, keepdims=True)


def sink(gradient, weight, pre):
    tokens, width = gradient.shape
    depth = pre.shape[1]
    tile = depth // 6
    return pl.pallas_call(
        sink_body,
        grid=(depth // tile,),
        in_specs=[
            pl.BlockSpec((tokens, width), lambda at: (0, 0)),
            pl.BlockSpec((tile, width), lambda at: (at, 0)),
            pl.BlockSpec((tokens, tile), lambda at: (0, at)),
        ],
        out_specs=[
            pl.BlockSpec((tokens, tile), lambda at: (0, at)),
            pl.BlockSpec((1, tile), lambda at: (0, at)),
        ],
        out_shape=[
            jax.ShapeDtypeStruct((tokens, depth), jnp.bfloat16),
            jax.ShapeDtypeStruct((1, depth), jnp.float32),
        ],
        compiler_params=pltpu.CompilerParams(vmem_limit_bytes=40 * 1024 * 1024),
    )(gradient, weight, pre)


def project_body(normed_ref, weight_ref, bias_ref, triple_ref):
    triple_ref[...] = (
        jnp.dot(normed_ref[...], weight_ref[...], preferred_element_type=jnp.float32)
        + bias_ref[...]
    ).astype(jnp.bfloat16)


def project(normed, wide, bias):
    tokens, width = normed.shape
    columns = bias.shape[1]
    tile = width
    return pl.pallas_call(
        project_body,
        grid=(columns // tile,),
        in_specs=[
            pl.BlockSpec((tokens, width), lambda at: (0, 0)),
            pl.BlockSpec((width, tile), lambda at: (0, at)),
            pl.BlockSpec((1, tile), lambda at: (0, at)),
        ],
        out_specs=pl.BlockSpec((tokens, tile), lambda at: (0, at)),
        out_shape=jax.ShapeDtypeStruct((tokens, columns), jnp.bfloat16),
        compiler_params=pltpu.CompilerParams(vmem_limit_bytes=32 * 1024 * 1024),
    )(normed, wide, bias)


def fall_body(active_ref, weight_ref, bias_ref, middle_ref, gate_ref, feed_ref, result_ref):
    @pl.when(pl.program_id(0) == 0)
    def _():
        feed_ref[...] = jnp.broadcast_to(bias_ref[...], feed_ref.shape)

    feed_ref[...] += jnp.dot(
        active_ref[...], weight_ref[...], preferred_element_type=jnp.float32
    )

    @pl.when(pl.program_id(0) == pl.num_programs(0) - 1)
    def _():
        result_ref[...] = middle_ref[...] + gate_ref[...] * feed_ref[...]


def fall(active, weight, bias, middle, gate):
    tokens, depth = active.shape
    width = weight.shape[1]
    tile = depth // 3
    whole = pl.BlockSpec((tokens, width), lambda at: (0, 0))
    row = pl.BlockSpec((1, width), lambda at: (0, 0))
    return pl.pallas_call(
        fall_body,
        grid=(depth // tile,),
        in_specs=[
            pl.BlockSpec((tokens, tile), lambda at: (0, at)),
            pl.BlockSpec((tile, width), lambda at: (at, 0)),
            row,
            whole,
            row,
        ],
        out_specs=[whole, whole],
        out_shape=[jax.ShapeDtypeStruct((tokens, width), jnp.float32)] * 2,
        compiler_params=pltpu.CompilerParams(vmem_limit_bytes=40 * 1024 * 1024),
    )(active, weight, bias, middle, gate)


def block_forward(hidden, modulation, wide_matrix, deep_matrix, bias, lengths):
    sequences = hidden.shape[0]
    offset_first, factor_first, gate_first, offset_second, factor_second, gate_second = (
        split_modulation(modulation)
    )
    normed_low = modulate(hidden, offset_first, factor_first).astype(jnp.bfloat16)
    triple_bias = jnp.concatenate(
        [
            bias[6 * MODEL_WIDTH : 7 * MODEL_WIDTH],
            jnp.zeros((MODEL_WIDTH,), jnp.float32),
            bias[7 * MODEL_WIDTH : 8 * MODEL_WIDTH],
        ]
    )
    if sequences == 1:
        triple = project(normed_low[0], wide_matrix[3], triple_bias[None])[None]
    else:
        triple = (
            jnp.dot(normed_low, wide_matrix[0], preferred_element_type=jnp.float32) + triple_bias
        ).astype(jnp.bfloat16)
    attended_low, log_total = attention_forward(triple, lengths)
    branch = (
        jnp.dot(
            attended_low,
            wide_matrix[1],
            preferred_element_type=jnp.float32,
        )
        + bias[8 * MODEL_WIDTH : 9 * MODEL_WIDTH]
    )
    middle = hidden + gate_first * branch
    mixed_low = modulate(middle, offset_second, factor_second).astype(jnp.bfloat16)
    pre_bias = bias[None, 9 * MODEL_WIDTH : 9 * MODEL_WIDTH + FF]
    feed_bias = bias[None, 9 * MODEL_WIDTH + FF :]
    if sequences == 1:
        pre_active, active_low, active_turned = rise(
            gelu_tanh, mixed_low[0], wide_matrix[3], pre_bias, MODEL_WIDTH, 4
        )
        feed_out, result = fall(
            active_low, deep_matrix, feed_bias, middle[0], gate_second[0]
        )
        pre_active, active_low, feed_out, result = (
            pre_active[None],
            active_low[None],
            feed_out[None],
            result[None],
        )
    else:
        pre_active = (
            jnp.dot(mixed_low, wide_matrix[2], preferred_element_type=jnp.float32) + pre_bias
        )
        active_low = gelu_tanh(pre_active).astype(jnp.bfloat16)
        active_turned = active_low.reshape(-1, FF).T
        feed_out = (
            jnp.dot(active_low, deep_matrix, preferred_element_type=jnp.float32) + feed_bias
        )
        result = middle + gate_second * feed_out
    saved = (
        hidden,
        modulation,
        normed_low,
        triple,
        log_total,
        attended_low,
        branch,
        middle,
        mixed_low,
        pre_active,
        active_turned,
        feed_out,
    )
    return (result, saved)


def block_backward(upstream, saved, wide_matrix, deep_matrix, lengths):
    (
        hidden,
        modulation,
        normed_low,
        triple,
        log_total,
        attended_low,
        branch,
        middle,
        mixed_low,
        pre_active,
        active_turned,
        feed_out,
    ) = saved
    sequences = hidden.shape[0]
    offset_first, factor_first, gate_first, offset_second, factor_second, gate_second = (
        split_modulation(modulation)
    )
    feedforward_gradient = (upstream * gate_second).astype(jnp.bfloat16)
    gate_second_grad = jnp.sum(upstream * feed_out, axis=1, keepdims=True)
    if sequences == 1:
        preactivation_gradient, pre_sum = sink(
            feedforward_gradient[0], deep_matrix, pre_active[0]
        )
        preactivation_gradient = preactivation_gradient[None]
    else:
        activation_gradient = jnp.einsum(
            "xjn,mn->xjm", feedforward_gradient, deep_matrix, preferred_element_type=jnp.float32
        )
        preactivation_gradient = jax.vjp(gelu_tanh, pre_active)[1](activation_gradient)[
            0
        ].astype(jnp.bfloat16)
        pre_sum = jnp.sum(
            preactivation_gradient, axis=(0, 1), dtype=jnp.float32, keepdims=True
        )[0]
    mixed_grad = jnp.einsum(
        "qvm,am->qva",
        preactivation_gradient,
        wide_matrix[2],
        preferred_element_type=jnp.float32,
    )
    second_back = jax.vjp(modulate, middle, offset_second, factor_second)[1]
    middle_part, offset_second_grad, factor_second_grad = second_back(mixed_grad)
    middle_grad = upstream + middle_part
    gate_first_grad = jnp.sum(middle_grad * branch, axis=1, keepdims=True)
    branch_gradient = (middle_grad * gate_first).astype(jnp.bfloat16)
    attended_grad = jnp.einsum(
        "tbr,ar->tba",
        branch_gradient,
        wide_matrix[1],
        preferred_element_type=jnp.float32,
    ).astype(jnp.bfloat16)
    triple_gradient = attention_backward(triple, log_total, attended_grad, lengths)
    normed_grad = jnp.einsum(
        "tbr,ar->tba",
        triple_gradient,
        wide_matrix[0],
        preferred_element_type=jnp.float32,
    )
    first_back = jax.vjp(modulate, hidden, offset_first, factor_first)[1]
    hidden_part, offset_first_grad, factor_first_grad = first_back(normed_grad)
    hidden_grad = middle_grad + hidden_part
    def column_sum(values):
        return jnp.sum(values, axis=(0, 1), dtype=jnp.float32, keepdims=True)[0]

    triple_sum = column_sum(triple_gradient)
    row_pieces = [
        piece.reshape(1, -1)
        for piece in (
            offset_first_grad,
            factor_first_grad,
            gate_first_grad,
            offset_second_grad,
            factor_second_grad,
            gate_second_grad,
        )
    ] + [
        triple_sum[:, :MODEL_WIDTH],
        triple_sum[:, 2 * MODEL_WIDTH :],
        column_sum(branch_gradient),
        pre_sum,
        column_sum(feedforward_gradient),
    ]

    def flat(values):
        return values.reshape(-1, values.shape[-1])

    entering = [by_chip(flat(values).T) for values in (normed_low, attended_low, mixed_low)]
    entering.append(by_device(active_turned))
    returning = [
        flat(values)
        for values in (
            triple_gradient,
            branch_gradient,
            preactivation_gradient,
            feedforward_gradient,
        )
    ]
    factors = (entering, returning)
    return (hidden_grad, row_pieces, factors)


def adam_update(weight, grad, first, second, rate, decay):
    first_new = 0.9 * first + 0.1 * grad
    second_new = 0.999 * second + 0.001 * grad * grad
    first_hat = first_new / (1.0 - 0.9**STEP)
    second_hat = second_new / (1.0 - 0.999**STEP)
    updated = weight - rate * (first_hat / (jnp.sqrt(second_hat) + adam_epsilon) + decay * weight)
    return (first_new, second_new, updated)


def per_device(
    tokens,
    condition,
    lengths,
    targets,
    cotangent,
    wide_weight,
    deep_weight,
    head_first,
    head_second,
    block_bias,
    head_bias,
    wide_mean,
    deep_mean,
    head_first_mean,
    head_second_mean,
    block_bias_mean,
    head_bias_mean,
    wide_square,
    deep_square,
    head_first_square,
    head_second_square,
    block_bias_square,
    head_bias_square,
):
    sequences = condition.shape[0]
    hidden = tokens.astype(jnp.float32).reshape(sequences, SEQ_LEN, MODEL_WIDTH)
    silu_low = jax.nn.silu(condition.astype(jnp.float32)).astype(jnp.bfloat16)
    visible = jnp.arange(SEQ_LEN, dtype=jnp.int32)[None, :] < lengths[:, None]
    wide_early, deep_early, (modulation_early, modulation_late) = fetch_first(
        wide_weight, deep_weight[0], silu_low, block_bias, 3
    )
    tapped, saved_early = block_forward(
        hidden, modulation_early, wide_early, deep_early, block_bias[0], lengths
    )
    wide_late, deep_late, joint, first_at = fetch_block_and(
        wide_weight[1], deep_weight[1], head_first
    )
    first_matrix = joint[:, first_at:]
    second_w = lax.all_gather(head_second.astype(jnp.bfloat16), "fsdp", axis=0, tiled=True)
    final, saved_late = block_forward(
        tapped, modulation_late, wide_late, deep_late, block_bias[1], lengths
    )
    raw_targets = targets.astype(jnp.float32).reshape(sequences, SEQ_LEN, PZ)
    target_unit = raw_targets * lax.rsqrt(
        jnp.sum(raw_targets * raw_targets, axis=-1, keepdims=True) + norm_epsilon
    )

    def alignment(values):
        unit = values * lax.rsqrt(jnp.sum(values * values, axis=-1, keepdims=True) + norm_epsilon)
        return jnp.sum(unit * target_unit, axis=-1)

    upstream = cotangent.astype(jnp.float32).reshape(sequences, SEQ_LEN, MODEL_WIDTH)
    late_input_grad, late_row, late_factors = block_backward(
        upstream, saved_late, wide_late, deep_late, lengths
    )
    tapped_low, late_input_grad, late_factors = lax.optimization_barrier(
        (tapped.astype(jnp.bfloat16), late_input_grad, late_factors)
    )
    first_bias, second_bias = head_bias[None, :PH], head_bias[None, PH : 2 * PH]
    if sequences == 1:
        tile = PH // 2
        first_pre, first_low, first_turned = rise(
            jax.nn.silu, tapped_low[0], joint, first_bias, tile, first_at // tile
        )
        second_pre, second_low, second_turned = rise(
            jax.nn.silu, first_low, second_w, second_bias, tile, 0
        )
        first_pre, first_low, second_pre, second_low = (
            first_pre[None],
            first_low[None],
            second_pre[None],
            second_low[None],
        )
    else:
        first_pre = (
            jnp.dot(tapped_low, first_matrix, preferred_element_type=jnp.float32) + first_bias
        )
        first_low = jax.nn.silu(first_pre).astype(jnp.bfloat16)
        second_pre = (
            jnp.dot(first_low, second_w[:, :PH], preferred_element_type=jnp.float32)
            + second_bias
        )
        second_low = jax.nn.silu(second_pre).astype(jnp.bfloat16)
        first_turned = first_low.reshape(-1, PH).T
        second_turned = second_low.reshape(-1, PH).T
    projected = (
        jnp.dot(second_low, second_w[:, PH:], preferred_element_type=jnp.float32)
        + head_bias[2 * PH :]
    )
    projected_grad = jax.vjp(alignment, projected)[1](-repa_weight * visible.astype(jnp.float32))[
        0
    ].astype(jnp.bfloat16)
    second_act_grad = jnp.einsum(
        "slz,hz->slh", projected_grad, second_w[:, PH:], preferred_element_type=jnp.float32
    )
    second_grad = jax.vjp(jax.nn.silu, second_pre)[1](second_act_grad)[0].astype(jnp.bfloat16)
    first_act_grad = jnp.einsum(
        "slh,gh->slg", second_grad, second_w[:, :PH], preferred_element_type=jnp.float32
    )
    first_gradient = jax.vjp(jax.nn.silu, first_pre)[1](first_act_grad)[0].astype(jnp.bfloat16)
    tapped_gradient = jnp.einsum(
        "ejk,rk->ejr", first_gradient, first_matrix, preferred_element_type=jnp.float32
    )

    def column_sum(values):
        return jnp.sum(values, axis=(0, 1), dtype=jnp.float32, keepdims=True)[0]

    def flat(values):
        return values.reshape(-1, values.shape[-1])

    late_packed = pack_rows(
        [silu_low]
        + late_row
        + [column_sum(first_gradient), column_sum(second_grad), column_sum(projected_grad)],
        jnp.float32,
    )
    late_packed, late_input_grad = lax.optimization_barrier((late_packed, late_input_grad))
    late_rows = gathered_terms(late_packed)
    input_grad, early_row, early_factors = block_backward(
        late_input_grad + tapped_gradient, saved_early, wide_early, deep_early, lengths
    )
    early_packed = pack_rows(early_row, jnp.float32)
    first_pair = [flat(tapped_low).T, flat(first_gradient)]
    second_pair = [first_turned, flat(second_grad)]
    third_pair = [second_turned, flat(projected_grad)]
    early_packed, early_factors, late_factors, second_pair = lax.optimization_barrier(
        (early_packed, early_factors, late_factors, second_pair)
    )
    early_rows = gathered_terms(early_packed)
    late_wide_grad, late_deep_grad, (first_weight_grad, third_weight_grad) = sum_grads(
        late_factors, first=first_pair, third=third_pair, identity=0
    )
    early_rows, early_factors, late_deep_grad = lax.optimization_barrier(
        (early_rows, early_factors, late_deep_grad)
    )
    early_wide_grad, early_deep_grad, (second_weight_grad,) = sum_grads(
        early_factors, second=second_pair, identity=1
    )
    second_weight_grad = jnp.concatenate([second_weight_grad, third_weight_grad], axis=1)
    own_silu = lax.dynamic_slice_in_dim(
        late_rows,
        lax.axis_index("fsdp") * wide_weight.shape[1],
        wide_weight.shape[1],
        axis=1,
    ).astype(jnp.bfloat16)
    late_rows = late_rows[:, MODEL_WIDTH:]
    bias_width = block_bias.shape[1]

    def modulation_weight_grad(rows):
        return lax.dot_general(
            own_silu,
            rows[:, : 6 * MODEL_WIDTH].astype(jnp.bfloat16),
            (((0,), (0,)), ((), ())),
            preferred_element_type=jnp.float32,
        )

    wide_grad = jnp.stack(
        [
            jnp.concatenate(
                [modulation_weight_grad(early_rows)] + early_wide_grad,
                axis=1,
            ),
            jnp.concatenate(
                [modulation_weight_grad(late_rows)] + late_wide_grad,
                axis=1,
            ),
        ]
    )
    deep_grad = jnp.stack([early_deep_grad, late_deep_grad])
    late_sum = jnp.sum(late_rows, axis=0, dtype=jnp.float32)
    early_sum = jnp.sum(early_rows, axis=0, dtype=jnp.float32)
    block_bias_grad = jnp.stack([early_sum, late_sum[:bias_width]])
    head_bias_total = late_sum[bias_width:]
    wide_m, wide_v, wide_new = adam_update(
        wide_weight, wide_grad, wide_mean, wide_square, matrix_rate, matrix_decay
    )
    deep_m, deep_v, deep_new = adam_update(
        deep_weight, deep_grad, deep_mean, deep_square, matrix_rate, matrix_decay
    )
    first_m, first_v, first_new = adam_update(
        head_first, first_weight_grad, head_first_mean, head_first_square, matrix_rate, matrix_decay
    )
    second_m, second_v, second_new = adam_update(
        head_second,
        second_weight_grad,
        head_second_mean,
        head_second_square,
        matrix_rate,
        matrix_decay,
    )
    bias_m, bias_v, bias_new = adam_update(
        block_bias, block_bias_grad, block_bias_mean, block_bias_square, bias_rate, 0.0
    )
    hbias_m, hbias_v, hbias_new = adam_update(
        head_bias, head_bias_total, head_bias_mean, head_bias_square, bias_rate, 0.0
    )
    output = final.reshape(sequences * SEQ_LEN, MODEL_WIDTH).astype(jnp.bfloat16)
    input_flat = input_grad.reshape(sequences * SEQ_LEN, MODEL_WIDTH)
    return (
        output,
        input_flat,
        wide_grad,
        deep_grad,
        first_weight_grad,
        second_weight_grad,
        block_bias_grad,
        head_bias_total,
        wide_m,
        deep_m,
        first_m,
        second_m,
        bias_m,
        hbias_m,
        wide_v,
        deep_v,
        first_v,
        second_v,
        bias_v,
        hbias_v,
        wide_new,
        deep_new,
        first_new,
        second_new,
        bias_new,
        hbias_new,
    )


def solution(mesh):
    in_specs = (
        P(("fsdp", "rep"), None),
        P(("fsdp", "rep"), None),
        P(("fsdp", "rep")),
        P(("fsdp", "rep"), None),
        P(("fsdp", "rep"), None),
        P(None, "fsdp", None),
        P(None, "fsdp", None),
        P("fsdp", None),
        P("fsdp", None),
        P(),
        P(),
        P(None, "fsdp", None),
        P(None, "fsdp", None),
        P("fsdp", None),
        P("fsdp", None),
        P(),
        P(),
        P(None, "fsdp", None),
        P(None, "fsdp", None),
        P("fsdp", None),
        P("fsdp", None),
        P(),
        P(),
    )
    out_specs = (
        P(("fsdp", "rep"), None),
        P(("fsdp", "rep"), None),
        P(None, "fsdp", None),
        P(None, "fsdp", None),
        P("fsdp", None),
        P("fsdp", None),
        P(),
        P(),
        P(None, "fsdp", None),
        P(None, "fsdp", None),
        P("fsdp", None),
        P("fsdp", None),
        P(),
        P(),
        P(None, "fsdp", None),
        P(None, "fsdp", None),
        P("fsdp", None),
        P("fsdp", None),
        P(),
        P(),
        P(None, "fsdp", None),
        P(None, "fsdp", None),
        P("fsdp", None),
        P("fsdp", None),
        P(),
        P(),
    )
    return jax.shard_map(
        per_device, mesh=mesh, in_specs=in_specs, out_specs=out_specs, check_vma=False
    )
```

```python
from functools import partial
from typing import NamedTuple

import jax
import jax.numpy as jnp
from jax import lax
from jax.experimental import pallas as pl
from jax.experimental.pallas import tpu as pltpu
from jax.sharding import PartitionSpec as P

MESH = pl.DeviceIdType.MESH
GIVE_SLOTS = 3

MODEL_WIDTH = 1152
HEADS = 16
HEAD_DIM = 72
FF = 4608
PH = 2048
PZ = 768
SEQ_LEN = 448
STEP = 10


norm_epsilon = 1e-06
adam_epsilon = 1e-08
masked_score = -1e30
repa_weight = 0.5
matrix_rate = 0.05
bias_rate = 0.3
matrix_decay = 0.01


def normalize(values):
    centred = values - jnp.mean(values, axis=-1, keepdims=True)
    spread = jnp.mean(centred * centred, axis=-1, keepdims=True)
    return centred * lax.rsqrt(spread + norm_epsilon)


def modulate(values, offset, factor):
    return normalize(values) * (1.0 + factor) + offset


def gelu_tanh(values):
    return jax.nn.gelu(values, approximate=True)


def split_modulation(modulation):
    columns = modulation.shape[-1] // 6
    return [modulation[:, None, number * columns : (number + 1) * columns] for number in range(6)]


def outer_rows(left, right):
    flat_left = left.reshape(-1, left.shape[-1])
    flat_right = right.reshape(-1, right.shape[-1])
    return lax.dot_general(
        flat_left, flat_right, (((0,), (0,)), ((), ())), preferred_element_type=jnp.float32
    )


def swap_cores(values):
    count = lax.axis_size("fsdp")
    return lax.ppermute(values, "fsdp", [(place, place ^ 1) for place in range(count)])


class Term(NamedTuple):
    left: int
    right: int
    rows: int
    row_from: int
    columns: int
    column_from: int
    split: bool
    way: int
    start: int
    out: int
    out_row: int
    out_column: int


def ring_place(chip, chips):
    return lax.div(chip, 2) + lax.rem(chip, 2) * (chips - 1 - 2 * lax.div(chip, 2))


def ring_chip(place, chips):
    upper = lax.div(place, (chips + 1) // 2)
    return 2 * place + upper * (2 * (chips - 1 - place) + 1 - 2 * place)


def reduce_body(terms, chips, lefts, rights, out_count, *refs):
    refs = list(refs)

    def take(count):
        taken = refs[:count]
        del refs[:count]
        return taken

    left_refs, right_refs = take(lefts), take(rights)
    outs = take(out_count)
    own_left, own_right = take(lefts), take(rights)
    sib_left, sib_right = take(lefts), take(rights)
    landing, final = take(len(terms)), take(len(terms))
    split_at = [number for number, term in enumerate(terms) if term.split]
    give, got = take(len(split_at)), take(len(split_at))
    load_sem, swap_send, swap_recv, ring_send, ring_recv = take(5)
    give_send, got_recv, final_send, final_recv = take(4)
    stage, stage_sem, share_send, share_recv = take(4)

    device = lax.axis_index("fsdp")
    plane = lax.axis_index("rep")
    core, chip = lax.rem(device, 2), lax.div(device, 2)
    place = ring_place(chip, chips)
    sibling = {"fsdp": device + 1 - 2 * core}
    twin = {"rep": 1 - plane}
    ways = [
        {"fsdp": 2 * ring_chip(lax.rem(place + step, chips), chips) + core}
        for step in (1, chips - 1)
    ]

    barrier = pltpu.get_barrier_semaphore()
    partners = (ways[0], ways[1], sibling, twin)
    for partner in partners:
        pl.semaphore_signal(barrier, inc=1, device_id=partner, device_id_type=MESH)
    pl.semaphore_wait(barrier, len(partners))

    def remote(source, target, send_sem, recv_sem, partner):
        return pltpu.make_async_remote_copy(
            src_ref=source,
            dst_ref=target,
            send_sem=send_sem,
            recv_sem=recv_sem,
            device_id=partner,
            device_id_type=MESH,
        )

    loads, swaps = {}, {}
    for number in range(lefts):
        ref = left_refs[number]
        by_rows = len(ref.shape) == 4
        mine = ref.at[:, core] if by_rows else ref
        other = ref.at[:, 1 - core] if by_rows else ref
        loads["l", number] = pltpu.make_async_copy(mine, own_left[number], load_sem.at[number])
        swaps["l", number] = remote(
            other, sib_left[number], swap_send.at[number], swap_recv.at[number], sibling
        )
    for number in range(rights):
        ref, at = right_refs[number], lefts + number
        width = own_right[number].shape[1]
        if width == ref.shape[1]:
            mine = other = ref
        else:
            second = ref.shape[1] - width
            mine = ref.at[:, pl.ds(pl.multiple_of(core * second, 128), width)]
            other = ref.at[:, pl.ds(pl.multiple_of((1 - core) * second, 128), width)]
        loads["r", number] = pltpu.make_async_copy(mine, own_right[number], load_sem.at[at])
        swaps["r", number] = remote(
            other, sib_right[number], swap_send.at[at], swap_recv.at[at], sibling
        )
    first_use = {}
    for term in sorted(terms, key=lambda term: term.start - term.split):
        for key in (("l", term.left), ("r", term.right)):
            first_use.setdefault(key, term.start - term.split)
    for key in first_use:
        loads[key].start()
        swaps[key].start()
    for number, term in enumerate(terms):
        landing[number][0] = jnp.zeros(landing[number].shape[1:], jnp.bfloat16)

    def chunk(term, owner, part):
        rows = pl.ds(term.row_from, term.rows)
        from_column = term.column_from
        if term.split:
            from_column = pl.multiple_of(from_column + part * term.columns, 128)
        columns = pl.ds(from_column, term.columns)
        own = jnp.dot(
            own_left[term.left][owner, rows, :],
            own_right[term.right][:, columns],
            preferred_element_type=jnp.float32,
        )
        return own + jnp.dot(
            sib_left[term.left][owner, rows, :],
            sib_right[term.right][:, columns],
            preferred_element_type=jnp.float32,
        )

    def owner_at(term, hop):
        back = hop + 1 if term.way == 0 else 2 * chips - 1 - hop
        return ring_chip(lax.rem(place + 2 * chips - back, chips), chips)

    def give_copy(at, hop):
        return remote(
            give[at].at[lax.rem(hop, GIVE_SLOTS)],
            got[at].at[hop],
            give_send.at[at, hop],
            got_recv.at[at, hop],
            twin,
        )

    def ring_copy(number, hop):
        return remote(
            landing[number].at[hop],
            landing[number].at[hop + 1],
            ring_send.at[number, hop],
            ring_recv.at[number, hop + 1],
            ways[terms[number].way],
        )

    def arrival(number, hop):
        return remote(
            landing[number].at[hop],
            landing[number].at[hop],
            ring_send.at[number, hop],
            ring_recv.at[number, hop],
            ways[terms[number].way],
        )

    def final_copy(number):
        return remote(
            landing[number].at[chips - 1],
            final[number],
            final_send.at[number],
            final_recv.at[number],
            twin,
        )

    def step(clock, carry):
        for moment in sorted(set(first_use.values())):

            @pl.when(clock == moment)
            def _():
                for key, use in first_use.items():
                    if use == moment:
                        loads[key].wait()
                        swaps[key].wait_recv()

        for at, number in enumerate(split_at):
            term = terms[number]
            later = clock - term.start + 1

            @pl.when((later >= GIVE_SLOTS) & (later < chips))
            def _():
                give_copy(at, later - GIVE_SLOTS).wait_send()

            @pl.when((later >= 0) & (later < chips))
            def _():
                give[at][lax.rem(later, GIVE_SLOTS)] = chunk(term, owner_at(term, later), 1 - plane).astype(
                    jnp.bfloat16
                )
                give_copy(at, later).start()

        for number, term in enumerate(terms):
            hop = clock - term.start

            @pl.when((hop >= 0) & (hop < chips))
            def _():
                total = chunk(term, owner_at(term, hop), plane)
                if term.split:
                    at = split_at.index(number)
                    give_copy(at, hop).wait_recv()
                    total = total + got[at][hop].astype(jnp.float32)

                @pl.when(hop > 0)
                def _():
                    arrival(number, hop).wait_recv()

                landing[number][hop] = (
                    total + landing[number][hop].astype(jnp.float32)
                ).astype(jnp.bfloat16)

                @pl.when(hop < chips - 1)
                def _():
                    ring_copy(number, hop).start()

                @pl.when(hop == chips - 1)
                def _():
                    final_copy(number).start()

        return carry

    lax.fori_loop(0, max(term.start for term in terms) + chips, step, 0)
    stores, shares = [], []

    def store(term, values, from_column):
        slot = len(stores) % 2
        if len(stores) >= 2:
            stores[-2]()
        stage[slot, : term.rows, : term.columns] = values
        columns = pl.ds(from_column, term.columns)
        if len(left_refs[term.left].shape) == 4:
            copy = pltpu.make_async_copy(
                stage.at[slot, pl.ds(0, term.rows), pl.ds(0, term.columns)],
                outs[term.out].at[0, pl.ds(term.out_row, term.rows), columns],
                stage_sem.at[slot],
            )
            copy.start()
            stores.append(copy.wait)
            return
        half = term.rows // 2

        def rows_of(owner):
            return stage.at[
                slot, pl.ds(pl.multiple_of(owner * half, 8), half), pl.ds(0, term.columns)
            ]

        target = outs[term.out].at[core, :, columns]
        copy = pltpu.make_async_copy(rows_of(core), target, stage_sem.at[slot])
        at = len(shares)
        share = remote(
            rows_of(1 - core), target, share_send.at[at], share_recv.at[at], sibling
        )
        copy.start()
        share.start()

        def settle_store():
            copy.wait()
            share.wait_send()

        stores.append(settle_store)
        arrived = outs[term.out].at[1 - core, :, columns]
        shares.append(remote(arrived, arrived, share_send.at[at], share_recv.at[at], sibling))

    for number, term in enumerate(terms):
        final_copy(number).wait()
        mine = landing[number][chips - 1].astype(jnp.float32)
        other = final[number][...].astype(jnp.float32)
        if term.split:
            for part, values in ((plane, mine), (1 - plane, other)):
                from_column = term.out_column + part * term.columns
                store(term, values, pl.multiple_of(from_column, 128))
        else:
            store(term, mine + other, term.out_column)
    for settle_store in stores[-2:]:
        settle_store()
    for share in shares:
        share.wait_recv()

    def settle(hop, carry):
        for number in range(len(terms)):

            @pl.when(hop < chips - 1)
            def _():
                ring_copy(number, hop).wait_send()

        for at in range(len(split_at)):

            @pl.when(hop >= chips - GIVE_SLOTS)
            def _():
                give_copy(at, hop).wait_send()

        return carry

    lax.fori_loop(0, chips, settle, 0)
    for key in first_use:
        swaps[key].wait_send()


def core_columns(columns):
    return -(-columns // 256) * 128


def reduce_terms(terms, lefts, rights, identity):
    chips = lefts[0].shape[0]
    whole = {term.right for term in terms if lefts[term.left].ndim == 4}
    left_parts = [
        (left.shape[0],) + left.shape[-2:] for left in lefts
    ]
    right_parts = [
        (right.shape[0], right.shape[1] if number in whole else core_columns(right.shape[1]))
        for number, right in enumerate(rights)
    ]

    def vmem(shape):
        return pltpu.VMEM(shape, jnp.bfloat16)

    splits = [term for term in terms if term.split]
    operands = len(lefts) + len(rights)
    scratch = (
        [vmem(shape) for shape in left_parts + right_parts] * 2
        + [vmem((chips, term.rows, term.columns)) for term in terms]
        + [vmem((term.rows, term.columns)) for term in terms]
        + [vmem((GIVE_SLOTS, term.rows, term.columns)) for term in splits]
        + [vmem((chips, term.rows, term.columns)) for term in splits]
        + [pltpu.SemaphoreType.DMA((operands,))] * 3
        + [pltpu.SemaphoreType.DMA((len(terms), chips))] * 2
        + [pltpu.SemaphoreType.DMA((len(splits), chips))] * 2
        + [pltpu.SemaphoreType.DMA((len(terms),))] * 2
        + [
            pltpu.VMEM(
                (2, max(term.rows for term in terms), max(term.columns for term in terms)),
                jnp.float32,
            ),
            pltpu.SemaphoreType.DMA((2,)),
        ]
        + [pltpu.SemaphoreType.DMA((len(terms) + len(splits),))] * 2
    )
    heights, widths, halves = {}, {}, {}
    for term in terms:
        out, width = term.out, term.columns * (1 + term.split)
        halves[out] = 1 if lefts[term.left].ndim == 4 else 2
        heights[out] = max(heights.get(out, 0), (term.out_row + term.rows) // halves[out])
        widths[out] = max(widths.get(out, 0), term.out_column + width)
    return pl.pallas_call(
        partial(reduce_body, terms, chips, len(lefts), len(rights), len(heights)),
        out_shape=[
            jax.ShapeDtypeStruct((halves[out], heights[out], widths[out]), jnp.float32)
            for out in range(len(heights))
        ],
        in_specs=[pl.BlockSpec(memory_space=pl.ANY)] * operands,
        out_specs=[pl.BlockSpec(memory_space=pl.ANY)] * len(heights),
        scratch_shapes=scratch,
        compiler_params=pltpu.CompilerParams(
            collective_id=identity, has_side_effects=True, vmem_limit_bytes=62 * 1024 * 1024
        ),
    )(*lefts, *rights)


class Piece(NamedTuple):
    source: int
    rows: int
    columns: int
    row_core: int
    row_plane: int
    column_from: int
    column_core: int
    column_plane: int
    split: bool
    long_way: int


def gather_body(pieces, chips, count, *refs):
    sources, (tiles, weights) = refs[:count], refs[count : count + 2]
    outs, products = refs[count + 2 : 2 * count + 2], refs[2 * count + 2]
    refs = refs[2 * count + 3 :]
    ring_send, ring_recv, pass_send, pass_recv, twin_send, twin_recv, own_sem = refs[:7]
    met, partial_rows, met_rows, tile_send, tile_recv, row_send, row_recv = refs[7:]
    device = lax.axis_index("fsdp")
    plane = lax.axis_index("rep")
    core, chip = lax.rem(device, 2), lax.div(device, 2)
    place = ring_place(chip, chips)
    sibling = {"fsdp": device + 1 - 2 * core}
    twin = {"rep": 1 - plane}

    def chip_back(way, hops):
        back = hops if way == 0 else chips - hops
        return ring_chip(lax.rem(place + chips - back, chips), chips)

    ways = [{"fsdp": 2 * chip_back(1 - way, 1) + core} for way in range(2)]

    barrier = pltpu.get_barrier_semaphore()
    peers = [lax.rem(device + step, 2 * chips) for step in range(1, 2 * chips)]
    partners = [{"fsdp": peer} for peer in peers] + [twin]
    for partner in partners:
        pl.semaphore_signal(barrier, inc=1, device_id=partner, device_id_type=MESH)
    pl.semaphore_wait(barrier, len(partners))

    keep = [
        pltpu.make_async_copy(
            sources[number],
            outs[number].at[
                pl.ds(
                    pl.multiple_of(chip * sources[number].shape[0], 16), sources[number].shape[0]
                ),
                :,
            ],
            own_sem.at[number],
        )
        for number in range(count)
    ]
    for copy in keep:
        copy.start()

    def window(piece, ref, base, of_core, of_plane):
        row = base + of_core * piece.row_core + of_plane * piece.row_plane
        column = (
            piece.column_from + of_core * piece.column_core + of_plane * piece.column_plane
        )
        return ref.at[
            pl.ds(pl.multiple_of(row, 16), piece.rows),
            pl.ds(pl.multiple_of(column, 128), piece.columns),
        ]

    def landed(number, owner, of_core, of_plane):
        piece = pieces[number]
        height = sources[piece.source].shape[0]
        return window(piece, outs[piece.source], owner * height, of_core, of_plane)

    def remote(source, target, sems, index, partner):
        return pltpu.make_async_remote_copy(
            src_ref=source,
            dst_ref=target,
            send_sem=sems[0].at[index],
            recv_sem=sems[1].at[index],
            device_id=partner,
            device_id_type=MESH,
        )

    hops = [
        [chips // 2 if piece.long_way == way else (chips - 1) // 2 for way in range(2)]
        for piece in pieces
    ]
    splits = [number for number, piece in enumerate(pieces) if piece.split]
    sent = []

    def send(copy):
        copy.start()
        sent.append(copy)

    for number, piece in enumerate(pieces):
        for way in range(2):
            send(
                remote(
                    window(piece, sources[piece.source], 0, core, plane),
                    landed(number, chip, core, plane),
                    (ring_send, ring_recv),
                    (number, way, 0),
                    ways[way],
                )
            )

    def spread(target, sems, step):
        peer = peers[step]
        return remote(target[0].at[peer], target[1].at[step], sems, step, {"fsdp": peer})

    tile_sems, row_sems = (tile_send, tile_recv), (row_send, row_recv)
    steps = range(len(peers))
    for step in steps:
        send(spread((tiles, met), tile_sems, step))

    def ring_arrivals(hop):
        for number, piece in enumerate(pieces):
            for way in range(2):
                if hop > hops[number][way]:
                    continue
                block = landed(number, chip_back(way, hop), core, plane)
                remote(
                    block, block, (ring_send, ring_recv), (number, way, hop - 1), ways[way]
                ).wait_recv()
                if hop < hops[number][way]:
                    send(
                        remote(
                            block, block, (ring_send, ring_recv), (number, way, hop), ways[way]
                        )
                    )
                send(
                    remote(
                        block, block, (pass_send, pass_recv), (number, way, hop - 1), sibling
                    )
                )
                if piece.split:
                    at = splits.index(number)
                    send(
                        remote(block, block, (twin_send, twin_recv), (at, way, hop - 1), twin)
                    )

    def twin_arrivals(hop):
        for at, number in enumerate(splits):
            for way in range(2):
                if hop > hops[number][way]:
                    continue
                block = landed(number, chip_back(way, hop), core, 1 - plane)
                remote(
                    block, block, (twin_send, twin_recv), (at, way, hop - 1), twin
                ).wait_recv()
                send(
                    remote(
                        block,
                        block,
                        (pass_send, pass_recv),
                        (len(pieces) + at, way, hop - 1),
                        sibling,
                    )
                )

    ring_arrivals(1)
    for step in steps:
        spread((tiles, met), tile_sems, step).wait_recv()
    low = jnp.concatenate([met[step, :1, :] for step in steps] + [tiles[device, :1, :]])
    partial = jnp.dot(
        low.astype(jnp.bfloat16), weights[...], preferred_element_type=jnp.float32
    )
    for step in steps:
        sender = lax.rem(device + 2 * chips - 1 - step, 2 * chips)
        for at in range(partial_rows.shape[1]):
            partial_rows[sender, pl.ds(at, 1), :] = partial[
                step : step + 1, 128 * at : 128 * (at + 1)
            ]
    for step in steps:
        send(spread((partial_rows, met_rows), row_sems, step))

    for hop in range(2, chips // 2 + 1):
        ring_arrivals(hop)
        twin_arrivals(hop - 1)
    twin_arrivals(chips // 2)
    for number in range(len(pieces) + len(splits)):
        at = number if number < len(pieces) else splits[number - len(pieces)]
        of_plane = plane if number < len(pieces) else 1 - plane
        for way in range(2):
            for hop in range(1, hops[at][way] + 1):
                block = landed(at, chip_back(way, hop), 1 - core, of_plane)
                remote(
                    block, block, (pass_send, pass_recv), (number, way, hop - 1), sibling
                ).wait_recv()
    total = jnp.concatenate(
        [
            partial[len(peers) :, 128 * at : 128 * (at + 1)]
            for at in range(partial_rows.shape[1])
        ]
    )
    for step in steps:
        spread((partial_rows, met_rows), row_sems, step).wait_recv()
        total = total + met_rows[step]
    products[...] = total
    for copy in sent:
        copy.wait_send()
    for copy in keep:
        copy.wait()


def gather_pieces(pieces, sources, tiles, weights, identity):
    chips = lax.axis_size("fsdp") // 2
    splits = sum(piece.split for piece in pieces)
    hops = chips // 2
    peers = 2 * chips - 1
    lines = weights.shape[1] // 128

    def sems(number):
        return [pltpu.SemaphoreType.DMA((number, 2, hops))] * 2

    return pl.pallas_call(
        partial(gather_body, pieces, chips, len(sources)),
        out_shape=[
            jax.ShapeDtypeStruct((chips * source.shape[0], source.shape[1]), source.dtype)
            for source in sources
        ]
        + [jax.ShapeDtypeStruct((lines, 128), jnp.float32)],
        in_specs=[pl.BlockSpec(memory_space=pl.ANY)] * len(sources)
        + [pl.BlockSpec(memory_space=pltpu.VMEM)] * 2,
        out_specs=[pl.BlockSpec(memory_space=pl.ANY)] * len(sources)
        + [pl.BlockSpec(memory_space=pltpu.VMEM)],
        scratch_shapes=sems(len(pieces))
        + sems(len(pieces) + splits)
        + sems(splits)
        + [pltpu.SemaphoreType.DMA((len(sources),))]
        + [
            pltpu.VMEM((peers, 8, 128), jnp.float32),
            pltpu.VMEM((2 * chips, lines, 128), jnp.float32),
            pltpu.VMEM((peers, lines, 128), jnp.float32),
        ]
        + [pltpu.SemaphoreType.DMA((peers,))] * 4,
        compiler_params=pltpu.CompilerParams(
            collective_id=identity, has_side_effects=True, vmem_limit_bytes=32 * 1024 * 1024
        ),
    )(*sources, tiles, weights)


def chip_rows(shard):
    other = swap_cores(shard)
    core = lax.axis_index("fsdp") % 2
    return jnp.where(
        core == 0, jnp.concatenate([shard, other]), jnp.concatenate([other, shard])
    )


def by_chip(turned):
    chips = lax.axis_size("fsdp") // 2
    return turned.reshape(chips, -1, turned.shape[1])


def by_device(turned):
    chips = lax.axis_size("fsdp") // 2
    return turned.reshape(chips, 2, -1, turned.shape[1])


def join_cores(both, columns):
    joined, at = [], 0
    for width in columns:
        end = at + core_columns(width)
        twice = 2 * core_columns(width) - width
        joined += [both[0, :, at:end], both[1, :, at + twice : end]]
        at = end
    return joined


def plain_sum(left, right):
    total = lax.psum_scatter(
        outer_rows(left, right).astype(jnp.bfloat16), "fsdp", scatter_dimension=0, tiled=True
    )
    return lax.psum(total.astype(jnp.float32), "rep")


def kernels_fit(rows):
    return 2 * rows % 16 == 0 and lax.axis_size("rep") == 2


def sum_grads(factors, first=None, second=None, third=None, identity=0):
    (normed, attended, mixed, active), (triple_grad, branch_grad, pre_grad, feed_grad) = factors
    count = lax.axis_size("fsdp")
    rows = MODEL_WIDTH // count
    extra = [pair for pair in (first, second, third) if pair is not None]
    if not kernels_fit(rows):
        wide = [
            plain_sum(left.reshape(-1, left.shape[-1]).T, right)
            for left, right in zip((normed, attended, mixed, active), factors[1])
        ]
        return (wide[:3], wide[3], [plain_sum(left.T, right) for left, right in extra])
    triple_half = core_columns(triple_grad.shape[1])
    branch_half = core_columns(branch_grad.shape[1])
    pre_half = core_columns(pre_grad.shape[1])
    plain_part = 8 * 128
    pre_part = (pre_half - plain_part) // 2
    deep_rows = active.shape[2] // 2
    pre_at = triple_half + branch_half
    terms = [
        Term(3, 3, deep_rows, 0, MODEL_WIDTH, 0, False, 0, 0, 1, 0, 0),
        Term(3, 3, deep_rows, deep_rows, MODEL_WIDTH, 0, False, 1, 0, 1, deep_rows, 0),
        Term(2, 2, 2 * rows, 0, pre_part, plain_part, True, 1, 2, 0, 0, pre_at + plain_part),
        Term(0, 0, 2 * rows, 0, triple_half // 2, 0, True, 0, 3, 0, 0, 0),
        Term(2, 2, 2 * rows, 0, plain_part, 0, False, 1, 4, 0, 0, pre_at),
        Term(1, 1, 2 * rows, 0, branch_half, 0, False, 0, 5, 0, 0, triple_half),
    ]
    lefts = [normed, attended, mixed, active]
    rights = [triple_grad, branch_grad, pre_grad, feed_grad]
    columns = []
    for pair, ways in ((first, "s"), (second, "ps"), (third, "p")):
        if pair is None:
            continue
        at, out = len(lefts), 2 + len(columns)
        lefts.append(by_chip(pair[0]))
        rights.append(pair[1])
        height, half = lefts[-1].shape[1], core_columns(pair[1].shape[1])
        if ways == "s":
            terms.append(Term(at, at, height, 0, half // 2, 0, True, 0, 1, out, 0, 0))
        elif ways == "p":
            terms.append(Term(at, at, height, 0, 128, 0, False, 0, 1, out, 0, 0))
            terms.append(Term(at, at, height, 0, half - 128, 128, False, 1, 1, out, 0, 128))
        else:
            alike, split = half // 4, 3 * half // 8
            terms.append(Term(at, at, height, 0, alike, 0, False, 1, 1, out, 0, 0))
            terms.append(Term(at, at, height, 0, split, alike, True, 0, 2, out, 0, alike))
        columns.append(pair[1].shape[1])
    outs = reduce_terms(tuple(terms), lefts, rights, identity)
    wide = join_cores(outs[0], [triple_grad.shape[1], branch_grad.shape[1], pre_grad.shape[1]])
    rest = [
        jnp.concatenate(join_cores(out, [width]), axis=1)
        for out, width in zip(outs[2:], columns)
    ]
    return (wide, outs[1][0], rest)


def pack_body(*refs):
    out, at = refs[-1], 0
    for ref in refs[:-1]:
        width = ref.shape[1]
        out[:, at : at + width] = ref[...].astype(jnp.bfloat16).astype(out.dtype)
        at += width


def pack_rows(pieces, dtype):
    rows = pieces[0].shape[0]
    width = sum(piece.shape[1] for piece in pieces)
    return pl.pallas_call(
        pack_body, out_shape=jax.ShapeDtypeStruct((rows, width), dtype)
    )(*pieces)


def gathered_terms(row):
    return lax.all_gather(row, ("fsdp", "rep"), axis=0, tiled=True)


def fetch_first(wide_weight, deep_shard, silu_low, block_bias, identity):
    rest = wide_weight[0, :, 6 * MODEL_WIDTH :].astype(jnp.bfloat16)
    low = deep_shard.astype(jnp.bfloat16)
    rows = rest.shape[0]
    count = lax.axis_size("fsdp")
    if kernels_fit(rows) and silu_low.shape[0] == 1 and rows <= 128:
        unit = MODEL_WIDTH
        deep_rows = low.shape[0] // 2
        pieces = (
            Piece(0, 2 * rows, unit, 0, 0, 0, 4 * unit, unit, True, 0),
            Piece(1, deep_rows, unit, 2 * deep_rows, deep_rows, 0, 0, 0, True, 1),
            Piece(0, 2 * rows, unit, 0, 0, 2 * unit, 4 * unit, unit, True, 1),
        )
        tiles = jnp.pad(
            silu_low.astype(jnp.float32).reshape(count, 1, rows),
            ((0, 0), (0, 7), (0, 128 - rows)),
        )
        weights = jnp.concatenate(
            [wide_weight[block, :, : 6 * unit].astype(jnp.bfloat16) for block in range(2)], axis=1
        )
        weights = jnp.pad(weights, ((0, 128 - rows), (0, 0)))
        whole, deep, products = gather_pieces(
            pieces, [chip_rows(rest), chip_rows(low)], tiles, weights, identity
        )
        products = products.reshape(2, 1, 6 * unit)
        modulations = [products[block] + block_bias[block, : 6 * unit] for block in range(2)]
    else:
        whole = lax.all_gather(rest, "fsdp", axis=0, tiled=True)
        deep = lax.all_gather(low, "fsdp", axis=0, tiled=True)
        modulations = plane_modulation(silu_low, wide_weight, block_bias)
    split = (
        whole[:, : 3 * MODEL_WIDTH],
        whole[:, 3 * MODEL_WIDTH : 4 * MODEL_WIDTH],
        whole[:, 4 * MODEL_WIDTH :],
        whole,
    )
    return (split, deep, modulations)


def fetch_block_and(wide_shard, deep_shard, other_shard):
    rest = jnp.concatenate(
        [wide_shard[:, 6 * MODEL_WIDTH :].astype(jnp.bfloat16), other_shard.astype(jnp.bfloat16)],
        axis=1,
    )
    whole = lax.all_gather(rest, "fsdp", axis=0, tiled=True)
    deep = lax.all_gather(deep_shard.astype(jnp.bfloat16), "fsdp", axis=0, tiled=True)
    end = whole.shape[1] - other_shard.shape[1]
    split = (
        whole[:, : 3 * MODEL_WIDTH],
        whole[:, 3 * MODEL_WIDTH : 4 * MODEL_WIDTH],
        whole[:, 4 * MODEL_WIDTH : end],
        whole,
    )
    return (split, deep, whole, end)


def plane_modulation(silu_low, wide_weight, block_bias):
    count = lax.axis_size("fsdp")
    sequences = silu_low.shape[0]
    rows = wide_weight.shape[1]
    device = lax.axis_index("fsdp")
    spread = jnp.broadcast_to(
        silu_low.reshape(1, sequences, count, rows).transpose(2, 0, 1, 3)[:, 0],
        (count, sequences, rows),
    )
    met = lax.all_to_all(spread, "fsdp", 0, 0, tiled=True)
    met = met.reshape(count * sequences, rows)
    partial = [
        jnp.dot(
            met,
            wide_weight[block, :, : 6 * MODEL_WIDTH].astype(jnp.bfloat16),
            preferred_element_type=jnp.float32,
        )
        for block in range(2)
    ]
    partial = jnp.stack(partial, axis=1).reshape(count, sequences, 2, 6 * MODEL_WIDTH)
    back = lax.all_to_all(partial, "fsdp", 0, 0, tiled=True)
    total = jnp.sum(back, axis=0)
    return [total[:, block] + block_bias[block, : 6 * MODEL_WIDTH] for block in range(2)]


HEAD_WINDOW = 256


def head_window(head, width):
    first = head * HEAD_DIM
    at = min(first // 128 * 128, width - HEAD_WINDOW)
    lane = lax.broadcasted_iota(jnp.int32, (1, HEAD_WINDOW), 1)
    return at, (lane >= first - at) & (lane < first - at + HEAD_DIM)


def only(mine, values):
    return jnp.where(mine, values, jnp.zeros_like(values))


def against(left, right):
    return lax.dot_general(
        left, right, (((1,), (1,)), ((), ())), preferred_element_type=jnp.float32
    )


def attend_body(lengths_ref, triple_ref, attended_ref, log_ref, total_ref):
    tokens, width = attended_ref.shape
    length = lengths_ref[pl.program_id(0)]
    seen = lax.broadcasted_iota(jnp.int32, (tokens, 1), 0) < length
    total_ref[...] = jnp.zeros_like(total_ref)
    for head in range(HEADS):
        at, mine = head_window(head, width)
        window = pl.ds(at, HEAD_WINDOW)
        keys = only(mine, triple_ref[:, pl.ds(width + at, HEAD_WINDOW)])
        values = only(mine, triple_ref[:, pl.ds(2 * width + at, HEAD_WINDOW)])
        scores = against(keys, triple_ref[:, window]) * HEAD_DIM ** (-0.5)
        scores = jnp.where(seen, scores, masked_score)
        largest = jnp.max(scores, axis=0, keepdims=True)
        expanded = jnp.exp(scores - largest)
        sums = jnp.sum(expanded, axis=0, keepdims=True)
        weights = (expanded * (1.0 / sums)).astype(jnp.bfloat16)
        total_ref[:, window] += lax.dot_general(
            weights, values, (((0,), (0,)), ((), ())), preferred_element_type=jnp.float32
        )
        log_ref[head : head + 1, :] = largest + jnp.log(sums)
    attended_ref[...] = total_ref[...].astype(jnp.bfloat16)


def attention_forward(triple, lengths):
    sequences, tokens, columns = triple.shape
    width = columns // 3
    return pl.pallas_call(
        attend_body,
        grid=(sequences,),
        out_shape=[
            jax.ShapeDtypeStruct((sequences, tokens, width), jnp.bfloat16),
            jax.ShapeDtypeStruct((sequences, HEADS, tokens), jnp.float32),
        ],
        in_specs=[
            pl.BlockSpec(memory_space=pltpu.SMEM),
            pl.BlockSpec((None, tokens, columns), lambda number: (number, 0, 0)),
        ],
        out_specs=[
            pl.BlockSpec((None, tokens, width), lambda number: (number, 0, 0)),
            pl.BlockSpec((None, HEADS, tokens), lambda number: (number, 0, 0)),
        ],
        scratch_shapes=[pltpu.VMEM((tokens, width), jnp.float32)],
        compiler_params=pltpu.CompilerParams(vmem_limit_bytes=48 * 1024 * 1024),
    )(lengths, triple)


def attend_back_body(lengths_ref, triple_ref, log_ref, upstream_ref, grad_ref, total_ref):
    tokens, width = upstream_ref.shape
    length = lengths_ref[pl.program_id(0)]
    factor = HEAD_DIM ** (-0.5)
    seen = lax.broadcasted_iota(jnp.int32, (tokens, 1), 0) < length
    total_ref[...] = jnp.zeros_like(total_ref)
    for head in range(HEADS):
        at, mine = head_window(head, width)
        query_at, key_at, value_at = (
            pl.ds(group * width + at, HEAD_WINDOW) for group in range(3)
        )
        queries = only(mine, triple_ref[:, query_at])
        keys = only(mine, triple_ref[:, key_at])
        values = only(mine, triple_ref[:, value_at])
        upstream = only(mine, upstream_ref[:, pl.ds(at, HEAD_WINDOW)])
        scores = against(keys, queries) * factor
        chances = jnp.where(seen, jnp.exp(scores - log_ref[head : head + 1, :]), 0.0)
        chance_grad = against(values, upstream)
        centre = jnp.sum(chance_grad * chances, axis=0, keepdims=True)
        score_grad = (chances * (chance_grad - centre)).astype(jnp.bfloat16)
        total_ref[:, value_at] += jnp.dot(
            chances.astype(jnp.bfloat16), upstream, preferred_element_type=jnp.float32
        )
        total_ref[:, key_at] += factor * jnp.dot(
            score_grad, queries, preferred_element_type=jnp.float32
        )
        total_ref[:, query_at] += factor * lax.dot_general(
            score_grad, keys, (((0,), (0,)), ((), ())), preferred_element_type=jnp.float32
        )
    grad_ref[...] = total_ref[...].astype(jnp.bfloat16)


def attention_backward(triple, logs, upstream, lengths):
    sequences, tokens, columns = triple.shape

    def spec(width):
        return pl.BlockSpec((None, tokens, width), lambda number: (number, 0, 0))

    return pl.pallas_call(
        attend_back_body,
        grid=(sequences,),
        out_shape=jax.ShapeDtypeStruct((sequences, tokens, columns), jnp.bfloat16),
        in_specs=[
            pl.BlockSpec(memory_space=pltpu.SMEM),
            spec(columns),
            pl.BlockSpec((None, HEADS, tokens), lambda number: (number, 0, 0)),
            spec(columns // 3),
        ],
        out_specs=spec(columns),
        scratch_shapes=[pltpu.VMEM((tokens, columns), jnp.float32)],
        compiler_params=pltpu.CompilerParams(vmem_limit_bytes=48 * 1024 * 1024),
    )(lengths, triple, logs, upstream)


def rise_body(activation, low_ref, weight_ref, bias_ref, pre_ref, active_ref, turned_ref):
    pre = (
        jnp.dot(low_ref[...], weight_ref[...], preferred_element_type=jnp.float32)
        + bias_ref[...]
    )
    active = activation(pre).astype(jnp.bfloat16)
    pre_ref[...] = pre
    active_ref[...] = active
    turned_ref[...] = active.T


def rise(activation, low, weight, bias, tile, first):
    tokens, depth = low.shape
    columns = bias.shape[1]
    return pl.pallas_call(
        partial(rise_body, activation),
        grid=(columns // tile,),
        in_specs=[
            pl.BlockSpec((tokens, depth), lambda at: (0, 0)),
            pl.BlockSpec((depth, tile), lambda at: (0, first + at)),
            pl.BlockSpec((1, tile), lambda at: (0, at)),
        ],
        out_specs=[
            pl.BlockSpec((tokens, tile), lambda at: (0, at)),
            pl.BlockSpec((tokens, tile), lambda at: (0, at)),
            pl.BlockSpec((tile, tokens), lambda at: (at, 0)),
        ],
        out_shape=[
            jax.ShapeDtypeStruct((tokens, columns), jnp.float32),
            jax.ShapeDtypeStruct((tokens, columns), jnp.bfloat16),
            jax.ShapeDtypeStruct((columns, tokens), jnp.bfloat16),
        ],
        compiler_params=pltpu.CompilerParams(vmem_limit_bytes=40 * 1024 * 1024),
    )(low, weight, bias)


def sink_body(gradient_ref, weight_ref, pre_ref, out_ref, sum_ref):
    active_grad = against(gradient_ref[...], weight_ref[...])
    pre = pre_ref[...]
    scale, cubic = 0.7978845608028654, 0.044715
    bent = jnp.tanh(scale * (pre + cubic * pre * pre * pre))
    slope = 0.5 * (1.0 + bent) + 0.5 * pre * (1.0 - bent * bent) * scale * (
        1.0 + 3.0 * cubic * pre * pre
    )
    low = (active_grad * slope).astype(jnp.bfloat16)
    out_ref[...] = low
    sum_ref[...] = jnp.sum(low.astype(jnp.float32), axis=0, keepdims=True)


def sink(gradient, weight, pre):
    tokens, width = gradient.shape
    depth = pre.shape[1]
    tile = depth // 6
    return pl.pallas_call(
        sink_body,
        grid=(depth // tile,),
        in_specs=[
            pl.BlockSpec((tokens, width), lambda at: (0, 0)),
            pl.BlockSpec((tile, width), lambda at: (at, 0)),
            pl.BlockSpec((tokens, tile), lambda at: (0, at)),
        ],
        out_specs=[
            pl.BlockSpec((tokens, tile), lambda at: (0, at)),
            pl.BlockSpec((1, tile), lambda at: (0, at)),
        ],
        out_shape=[
            jax.ShapeDtypeStruct((tokens, depth), jnp.bfloat16),
            jax.ShapeDtypeStruct((1, depth), jnp.float32),
        ],
        compiler_params=pltpu.CompilerParams(vmem_limit_bytes=40 * 1024 * 1024),
    )(gradient, weight, pre)


def project_body(normed_ref, weight_ref, bias_ref, triple_ref):
    triple_ref[...] = (
        jnp.dot(normed_ref[...], weight_ref[...], preferred_element_type=jnp.float32)
        + bias_ref[...]
    ).astype(jnp.bfloat16)


def project(normed, wide, bias):
    tokens, width = normed.shape
    columns = bias.shape[1]
    tile = width
    return pl.pallas_call(
        project_body,
        grid=(columns // tile,),
        in_specs=[
            pl.BlockSpec((tokens, width), lambda at: (0, 0)),
            pl.BlockSpec((width, tile), lambda at: (0, at)),
            pl.BlockSpec((1, tile), lambda at: (0, at)),
        ],
        out_specs=pl.BlockSpec((tokens, tile), lambda at: (0, at)),
        out_shape=jax.ShapeDtypeStruct((tokens, columns), jnp.bfloat16),
        compiler_params=pltpu.CompilerParams(vmem_limit_bytes=32 * 1024 * 1024),
    )(normed, wide, bias)


def fall_body(active_ref, weight_ref, bias_ref, middle_ref, gate_ref, feed_ref, result_ref):
    @pl.when(pl.program_id(0) == 0)
    def _():
        feed_ref[...] = jnp.broadcast_to(bias_ref[...], feed_ref.shape)

    feed_ref[...] += jnp.dot(
        active_ref[...], weight_ref[...], preferred_element_type=jnp.float32
    )

    @pl.when(pl.program_id(0) == pl.num_programs(0) - 1)
    def _():
        result_ref[...] = middle_ref[...] + gate_ref[...] * feed_ref[...]


def fall(active, weight, bias, middle, gate):
    tokens, depth = active.shape
    width = weight.shape[1]
    tile = depth // 3
    whole = pl.BlockSpec((tokens, width), lambda at: (0, 0))
    row = pl.BlockSpec((1, width), lambda at: (0, 0))
    return pl.pallas_call(
        fall_body,
        grid=(depth // tile,),
        in_specs=[
            pl.BlockSpec((tokens, tile), lambda at: (0, at)),
            pl.BlockSpec((tile, width), lambda at: (at, 0)),
            row,
            whole,
            row,
        ],
        out_specs=[whole, whole],
        out_shape=[jax.ShapeDtypeStruct((tokens, width), jnp.float32)] * 2,
        compiler_params=pltpu.CompilerParams(vmem_limit_bytes=40 * 1024 * 1024),
    )(active, weight, bias, middle, gate)


def block_forward(hidden, modulation, wide_matrix, deep_matrix, bias, lengths):
    sequences = hidden.shape[0]
    offset_first, factor_first, gate_first, offset_second, factor_second, gate_second = (
        split_modulation(modulation)
    )
    normed_low = modulate(hidden, offset_first, factor_first).astype(jnp.bfloat16)
    triple_bias = jnp.concatenate(
        [
            bias[6 * MODEL_WIDTH : 7 * MODEL_WIDTH],
            jnp.zeros((MODEL_WIDTH,), jnp.float32),
            bias[7 * MODEL_WIDTH : 8 * MODEL_WIDTH],
        ]
    )
    if sequences == 1:
        triple = project(normed_low[0], wide_matrix[3], triple_bias[None])[None]
    else:
        triple = (
            jnp.dot(normed_low, wide_matrix[0], preferred_element_type=jnp.float32) + triple_bias
        ).astype(jnp.bfloat16)
    attended_low, log_total = attention_forward(triple, lengths)
    branch = (
        jnp.dot(
            attended_low,
            wide_matrix[1],
            preferred_element_type=jnp.float32,
        )
        + bias[8 * MODEL_WIDTH : 9 * MODEL_WIDTH]
    )
    middle = hidden + gate_first * branch
    mixed_low = modulate(middle, offset_second, factor_second).astype(jnp.bfloat16)
    pre_bias = bias[None, 9 * MODEL_WIDTH : 9 * MODEL_WIDTH + FF]
    feed_bias = bias[None, 9 * MODEL_WIDTH + FF :]
    if sequences == 1:
        pre_active, active_low, active_turned = rise(
            gelu_tanh, mixed_low[0], wide_matrix[3], pre_bias, MODEL_WIDTH, 4
        )
        feed_out, result = fall(
            active_low, deep_matrix, feed_bias, middle[0], gate_second[0]
        )
        pre_active, active_low, feed_out, result = (
            pre_active[None],
            active_low[None],
            feed_out[None],
            result[None],
        )
    else:
        pre_active = (
            jnp.dot(mixed_low, wide_matrix[2], preferred_element_type=jnp.float32) + pre_bias
        )
        active_low = gelu_tanh(pre_active).astype(jnp.bfloat16)
        active_turned = active_low.reshape(-1, FF).T
        feed_out = (
            jnp.dot(active_low, deep_matrix, preferred_element_type=jnp.float32) + feed_bias
        )
        result = middle + gate_second * feed_out
    saved = (
        hidden,
        modulation,
        normed_low,
        triple,
        log_total,
        attended_low,
        branch,
        middle,
        mixed_low,
        pre_active,
        active_turned,
        feed_out,
    )
    return (result, saved)


def block_backward(upstream, saved, wide_matrix, deep_matrix, lengths):
    (
        hidden,
        modulation,
        normed_low,
        triple,
        log_total,
        attended_low,
        branch,
        middle,
        mixed_low,
        pre_active,
        active_turned,
        feed_out,
    ) = saved
    sequences = hidden.shape[0]
    offset_first, factor_first, gate_first, offset_second, factor_second, gate_second = (
        split_modulation(modulation)
    )
    feedforward_gradient = (upstream * gate_second).astype(jnp.bfloat16)
    gate_second_grad = jnp.sum(upstream * feed_out, axis=1, keepdims=True)
    if sequences == 1:
        preactivation_gradient, pre_sum = sink(
            feedforward_gradient[0], deep_matrix, pre_active[0]
        )
        preactivation_gradient = preactivation_gradient[None]
    else:
        activation_gradient = jnp.einsum(
            "xjn,mn->xjm", feedforward_gradient, deep_matrix, preferred_element_type=jnp.float32
        )
        preactivation_gradient = jax.vjp(gelu_tanh, pre_active)[1](activation_gradient)[
            0
        ].astype(jnp.bfloat16)
        pre_sum = jnp.sum(
            preactivation_gradient, axis=(0, 1), dtype=jnp.float32, keepdims=True
        )[0]
    mixed_grad = jnp.einsum(
        "qvm,am->qva",
        preactivation_gradient,
        wide_matrix[2],
        preferred_element_type=jnp.float32,
    )
    second_back = jax.vjp(modulate, middle, offset_second, factor_second)[1]
    middle_part, offset_second_grad, factor_second_grad = second_back(mixed_grad)
    middle_grad = upstream + middle_part
    gate_first_grad = jnp.sum(middle_grad * branch, axis=1, keepdims=True)
    branch_gradient = (middle_grad * gate_first).astype(jnp.bfloat16)
    attended_grad = jnp.einsum(
        "tbr,ar->tba",
        branch_gradient,
        wide_matrix[1],
        preferred_element_type=jnp.float32,
    ).astype(jnp.bfloat16)
    triple_gradient = attention_backward(triple, log_total, attended_grad, lengths)
    normed_grad = jnp.einsum(
        "tbr,ar->tba",
        triple_gradient,
        wide_matrix[0],
        preferred_element_type=jnp.float32,
    )
    first_back = jax.vjp(modulate, hidden, offset_first, factor_first)[1]
    hidden_part, offset_first_grad, factor_first_grad = first_back(normed_grad)
    hidden_grad = middle_grad + hidden_part
    def column_sum(values):
        return jnp.sum(values, axis=(0, 1), dtype=jnp.float32, keepdims=True)[0]

    triple_sum = column_sum(triple_gradient)
    row_pieces = [
        piece.reshape(1, -1)
        for piece in (
            offset_first_grad,
            factor_first_grad,
            gate_first_grad,
            offset_second_grad,
            factor_second_grad,
            gate_second_grad,
        )
    ] + [
        triple_sum[:, :MODEL_WIDTH],
        triple_sum[:, 2 * MODEL_WIDTH :],
        column_sum(branch_gradient),
        pre_sum,
        column_sum(feedforward_gradient),
    ]

    def flat(values):
        return values.reshape(-1, values.shape[-1])

    entering = [by_chip(flat(values).T) for values in (normed_low, attended_low, mixed_low)]
    entering.append(by_device(active_turned))
    returning = [
        flat(values)
        for values in (
            triple_gradient,
            branch_gradient,
            preactivation_gradient,
            feedforward_gradient,
        )
    ]
    factors = (entering, returning)
    return (hidden_grad, row_pieces, factors)


def adam_update(weight, grad, first, second, rate, decay):
    first_new = 0.9 * first + 0.1 * grad
    second_new = 0.999 * second + 0.001 * grad * grad
    first_hat = first_new / (1.0 - 0.9**STEP)
    second_hat = second_new / (1.0 - 0.999**STEP)
    updated = weight - rate * (first_hat / (jnp.sqrt(second_hat) + adam_epsilon) + decay * weight)
    return (first_new, second_new, updated)


def per_device(
    tokens,
    condition,
    lengths,
    targets,
    cotangent,
    wide_weight,
    deep_weight,
    head_first,
    head_second,
    block_bias,
    head_bias,
    wide_mean,
    deep_mean,
    head_first_mean,
    head_second_mean,
    block_bias_mean,
    head_bias_mean,
    wide_square,
    deep_square,
    head_first_square,
    head_second_square,
    block_bias_square,
    head_bias_square,
):
    sequences = condition.shape[0]
    hidden = tokens.astype(jnp.float32).reshape(sequences, SEQ_LEN, MODEL_WIDTH)
    silu_low = jax.nn.silu(condition.astype(jnp.float32)).astype(jnp.bfloat16)
    visible = jnp.arange(SEQ_LEN, dtype=jnp.int32)[None, :] < lengths[:, None]
    wide_early, deep_early, (modulation_early, modulation_late) = fetch_first(
        wide_weight, deep_weight[0], silu_low, block_bias, 3
    )
    tapped, saved_early = block_forward(
        hidden, modulation_early, wide_early, deep_early, block_bias[0], lengths
    )
    wide_late, deep_late, joint, first_at = fetch_block_and(
        wide_weight[1], deep_weight[1], head_first
    )
    first_matrix = joint[:, first_at:]
    second_w = lax.all_gather(head_second.astype(jnp.bfloat16), "fsdp", axis=0, tiled=True)
    final, saved_late = block_forward(
        tapped, modulation_late, wide_late, deep_late, block_bias[1], lengths
    )
    raw_targets = targets.astype(jnp.float32).reshape(sequences, SEQ_LEN, PZ)
    target_unit = raw_targets * lax.rsqrt(
        jnp.sum(raw_targets * raw_targets, axis=-1, keepdims=True) + norm_epsilon
    )

    def alignment(values):
        unit = values * lax.rsqrt(jnp.sum(values * values, axis=-1, keepdims=True) + norm_epsilon)
        return jnp.sum(unit * target_unit, axis=-1)

    upstream = cotangent.astype(jnp.float32).reshape(sequences, SEQ_LEN, MODEL_WIDTH)
    late_input_grad, late_row, late_factors = block_backward(
        upstream, saved_late, wide_late, deep_late, lengths
    )
    tapped_low, late_input_grad, late_factors = lax.optimization_barrier(
        (tapped.astype(jnp.bfloat16), late_input_grad, late_factors)
    )
    first_bias, second_bias = head_bias[None, :PH], head_bias[None, PH : 2 * PH]
    if sequences == 1:
        tile = PH // 2
        first_pre, first_low, first_turned = rise(
            jax.nn.silu, tapped_low[0], joint, first_bias, tile, first_at // tile
        )
        second_pre, second_low, second_turned = rise(
            jax.nn.silu, first_low, second_w, second_bias, tile, 0
        )
        first_pre, first_low, second_pre, second_low = (
            first_pre[None],
            first_low[None],
            second_pre[None],
            second_low[None],
        )
    else:
        first_pre = (
            jnp.dot(tapped_low, first_matrix, preferred_element_type=jnp.float32) + first_bias
        )
        first_low = jax.nn.silu(first_pre).astype(jnp.bfloat16)
        second_pre = (
            jnp.dot(first_low, second_w[:, :PH], preferred_element_type=jnp.float32)
            + second_bias
        )
        second_low = jax.nn.silu(second_pre).astype(jnp.bfloat16)
        first_turned = first_low.reshape(-1, PH).T
        second_turned = second_low.reshape(-1, PH).T
    projected = (
        jnp.dot(second_low, second_w[:, PH:], preferred_element_type=jnp.float32)
        + head_bias[2 * PH :]
    )
    projected_grad = jax.vjp(alignment, projected)[1](-repa_weight * visible.astype(jnp.float32))[
        0
    ].astype(jnp.bfloat16)
    second_act_grad = jnp.einsum(
        "slz,hz->slh", projected_grad, second_w[:, PH:], preferred_element_type=jnp.float32
    )
    second_grad = jax.vjp(jax.nn.silu, second_pre)[1](second_act_grad)[0].astype(jnp.bfloat16)
    first_act_grad = jnp.einsum(
        "slh,gh->slg", second_grad, second_w[:, :PH], preferred_element_type=jnp.float32
    )
    first_gradient = jax.vjp(jax.nn.silu, first_pre)[1](first_act_grad)[0].astype(jnp.bfloat16)
    tapped_gradient = jnp.einsum(
        "ejk,rk->ejr", first_gradient, first_matrix, preferred_element_type=jnp.float32
    )

    def column_sum(values):
        return jnp.sum(values, axis=(0, 1), dtype=jnp.float32, keepdims=True)[0]

    def flat(values):
        return values.reshape(-1, values.shape[-1])

    late_packed = pack_rows(
        [silu_low]
        + late_row
        + [column_sum(first_gradient), column_sum(second_grad), column_sum(projected_grad)],
        jnp.float32,
    )
    late_packed, late_input_grad = lax.optimization_barrier((late_packed, late_input_grad))
    late_rows = gathered_terms(late_packed)
    input_grad, early_row, early_factors = block_backward(
        late_input_grad + tapped_gradient, saved_early, wide_early, deep_early, lengths
    )
    early_packed = pack_rows(early_row, jnp.float32)
    first_pair = [flat(tapped_low).T, flat(first_gradient)]
    second_pair = [first_turned, flat(second_grad)]
    third_pair = [second_turned, flat(projected_grad)]
    early_packed, early_factors, late_factors, second_pair = lax.optimization_barrier(
        (early_packed, early_factors, late_factors, second_pair)
    )
    early_rows = gathered_terms(early_packed)
    late_wide_grad, late_deep_grad, (first_weight_grad, third_weight_grad) = sum_grads(
        late_factors, first=first_pair, third=third_pair, identity=0
    )
    early_rows, early_factors, late_deep_grad = lax.optimization_barrier(
        (early_rows, early_factors, late_deep_grad)
    )
    early_wide_grad, early_deep_grad, (second_weight_grad,) = sum_grads(
        early_factors, second=second_pair, identity=1
    )
    second_weight_grad = jnp.concatenate([second_weight_grad, third_weight_grad], axis=1)
    own_silu = lax.dynamic_slice_in_dim(
        late_rows,
        lax.axis_index("fsdp") * wide_weight.shape[1],
        wide_weight.shape[1],
        axis=1,
    ).astype(jnp.bfloat16)
    late_rows = late_rows[:, MODEL_WIDTH:]
    bias_width = block_bias.shape[1]

    def modulation_weight_grad(rows):
        return lax.dot_general(
            own_silu,
            rows[:, : 6 * MODEL_WIDTH].astype(jnp.bfloat16),
            (((0,), (0,)), ((), ())),
            preferred_element_type=jnp.float32,
        )

    wide_grad = jnp.stack(
        [
            jnp.concatenate(
                [modulation_weight_grad(early_rows)] + early_wide_grad,
                axis=1,
            ),
            jnp.concatenate(
                [modulation_weight_grad(late_rows)] + late_wide_grad,
                axis=1,
            ),
        ]
    )
    deep_grad = jnp.stack([early_deep_grad, late_deep_grad])
    late_sum = jnp.sum(late_rows, axis=0, dtype=jnp.float32)
    early_sum = jnp.sum(early_rows, axis=0, dtype=jnp.float32)
    block_bias_grad = jnp.stack([early_sum, late_sum[:bias_width]])
    head_bias_total = late_sum[bias_width:]
    wide_m, wide_v, wide_new = adam_update(
        wide_weight, wide_grad, wide_mean, wide_square, matrix_rate, matrix_decay
    )
    deep_m, deep_v, deep_new = adam_update(
        deep_weight, deep_grad, deep_mean, deep_square, matrix_rate, matrix_decay
    )
    first_m, first_v, first_new = adam_update(
        head_first, first_weight_grad, head_first_mean, head_first_square, matrix_rate, matrix_decay
    )
    second_m, second_v, second_new = adam_update(
        head_second,
        second_weight_grad,
        head_second_mean,
        head_second_square,
        matrix_rate,
        matrix_decay,
    )
    bias_m, bias_v, bias_new = adam_update(
        block_bias, block_bias_grad, block_bias_mean, block_bias_square, bias_rate, 0.0
    )
    hbias_m, hbias_v, hbias_new = adam_update(
        head_bias, head_bias_total, head_bias_mean, head_bias_square, bias_rate, 0.0
    )
    output = final.reshape(sequences * SEQ_LEN, MODEL_WIDTH).astype(jnp.bfloat16)
    input_flat = input_grad.reshape(sequences * SEQ_LEN, MODEL_WIDTH)
    return (
        output,
        input_flat,
        wide_grad,
        deep_grad,
        first_weight_grad,
        second_weight_grad,
        block_bias_grad,
        head_bias_total,
        wide_m,
        deep_m,
        first_m,
        second_m,
        bias_m,
        hbias_m,
        wide_v,
        deep_v,
        first_v,
        second_v,
        bias_v,
        hbias_v,
        wide_new,
        deep_new,
        first_new,
        second_new,
        bias_new,
        hbias_new,
    )


def solution(mesh):
    in_specs = (
        P(("fsdp", "rep"), None),
        P(("fsdp", "rep"), None),
        P(("fsdp", "rep")),
        P(("fsdp", "rep"), None),
        P(("fsdp", "rep"), None),
        P(None, "fsdp", None),
        P(None, "fsdp", None),
        P("fsdp", None),
        P("fsdp", None),
        P(),
        P(),
        P(None, "fsdp", None),
        P(None, "fsdp", None),
        P("fsdp", None),
        P("fsdp", None),
        P(),
        P(),
        P(None, "fsdp", None),
        P(None, "fsdp", None),
        P("fsdp", None),
        P("fsdp", None),
        P(),
        P(),
    )
    out_specs = (
        P(("fsdp", "rep"), None),
        P(("fsdp", "rep"), None),
        P(None, "fsdp", None),
        P(None, "fsdp", None),
        P("fsdp", None),
        P("fsdp", None),
        P(),
        P(),
        P(None, "fsdp", None),
        P(None, "fsdp", None),
        P("fsdp", None),
        P("fsdp", None),
        P(),
        P(),
        P(None, "fsdp", None),
        P(None, "fsdp", None),
        P("fsdp", None),
        P("fsdp", None),
        P(),
        P(),
        P(None, "fsdp", None),
        P(None, "fsdp", None),
        P("fsdp", None),
        P("fsdp", None),
        P(),
        P(),
    )
    return jax.shard_map(
        per_device, mesh=mesh, in_specs=in_specs, out_specs=out_specs, check_vma=False
    )
```
